32 devices in a mesh: dp: 8 (over z, y), tensor: 4 (over x, core).
Axes of the slice: x: 2, y: 2, z: 4, core: 2. Of those that a mesh axis runs over, the one named last changes fastest.
Arguments:
- tokens: bfloat16 [8192, 2048], P(('dp', 'tensor')), may hold values from -6 to 6
- segment_ids: int32 [8192], P('dp'), may hold values from -1 to 2, as said below
- cotangent: bfloat16 [8192, 2048], P(('dp', 'tensor')), may hold values from -6 to 6
- w_qkv: bfloat16 [2048, 3, 2048], P(None, None, 'tensor'), may hold values from -0.125 to 0.125
- qkv_bias: float32 [3, 2048], P(None, 'tensor'), may hold values from -1.5 to 1.5
- w_out: bfloat16 [2048, 2048], P('tensor'), may hold values from -2 to 2
- w_gate_up: bfloat16 [2048, 2, 5632], P(None, None, 'tensor'), may hold values from -0.125 to 0.125
- w_down: bfloat16 [5632, 2048], P('tensor'), may hold values from -0.078125 to 0.078125
- norm_gains: float32 [2, 2048], replicated, may hold values from 0.5 to 1.5
- norm_biases: float32 [2, 2048], replicated, may hold values from -1.5 to 1.5
Outputs:
- output: bfloat16 [8192, 2048], P(('dp', 'tensor'))
- input_grad: float32 [8192, 2048], P(('dp', 'tensor'))
- qkv_grad: float32 [2048, 3, 2048], P('dp', None, 'tensor')
- qkv_bias_grad: float32 [3, 2048], P(None, 'tensor')
- out_grad: float32 [2048, 2048], P('tensor', 'dp')
- gate_up_grad: float32 [2048, 2, 5632], P('dp', None, 'tensor')
- down_grad: float32 [5632, 2048], P('tensor', 'dp')
- gains_grad: float32 [2, 2048], replicated
- biases_grad: float32 [2, 2048], replicated
The draws below stay inside these ranges and needn't reach their ends.
Inputs may be any that keep to these rules, and one draw needn't show every extreme that they name: `segment_ids`: within each block of 1024 slots every sequence is one run of consecutive slots; sequences are numbered from 0 in their order within the block, at most three of them; padding slots carry -1 and may stand before and after the sequences.
All inputs are finite; a program needn't handle non-finite values.
Results may differ from the reference program's by a relative error of at most 0.024.
Values may be sent and summed in bfloat16 or wider, within the bound.
No kernel may reach another device: no remote copies, remote signals or barrier semaphores. Data moves between devices by JAX's collectives and lax.ppermute only.
A program may use at most 256 MiB of HBM per device.

```python
import jax
import jax.numpy as jnp
from jax import lax

D = 2048
HEADS = 32
HD = 64
FF = 5632
ROT = 16
TOK_DP = 1024
TOKENS = 8192
N_DP = 8
N_TENSOR = 4


def draw_segment_ids(key, part):
    key = jax.random.fold_in(key, 7)
    key_start, key_long, key_split = jax.random.split(key, 3)
    shard_rows = TOK_DP // N_TENSOR
    group_index = jnp.arange(N_DP, dtype=jnp.int32)[:, None]
    row_index = jnp.arange(TOK_DP, dtype=jnp.int32)[None, :]
    long_start = shard_rows // 2 + jax.random.randint(key_start, (N_DP, 1), 0, shard_rows - shard_rows // 2)
    least_end = 3 * shard_rows + 1
    live_end = least_end + (TOK_DP - least_end) * group_index // max(N_DP - 1, 1)
    long_end = least_end + jax.random.randint(key_long, (N_DP, 1), 0, 1 << 20) % jnp.maximum(live_end - least_end - 1, 1)
    long_end = jnp.minimum(long_end, live_end)
    mean_length = max(shard_rows // 2, 2)
    breaks = jax.random.randint(key_split, (N_DP, TOK_DP), 0, mean_length) == 0
    forced = (row_index == live_end - 1) & (live_end - 1 > long_end)
    seg_opens = (row_index == long_start) | (row_index == long_end) & (long_end < live_end) | (breaks | forced) & (row_index > long_end) & (row_index < live_end)
    numbers = jnp.minimum(jnp.cumsum(seg_opens.astype(jnp.int32), axis=1) - 1, 2)
    live_rows = (row_index >= long_start) & (row_index < live_end)
    return jnp.where(live_rows, numbers, -1).reshape(N_DP * TOK_DP).astype(jnp.int32)


def spiked(drawn, key, source, target, shards_of, factor):
    def block_of(dim):
        return (jnp.arange(drawn.shape[dim]) // (drawn.shape[dim] // shards_of)).reshape((-1,) + (1,) * (drawn.ndim - 1 - dim))

    near = jax.random.permutation(key, shards_of)[block_of(target)]
    second = (block_of(target) + shards_of // 2) % shards_of
    return jnp.where((block_of(source) == near) | (block_of(source) == second), factor * drawn, drawn)


def block_levels(stream_key, dims, pieces, low, high):
    loudness, own = 1.0, jax.random.fold_in(stream_key, 6)
    for position, blocks in pieces:
        steps = jnp.exp(jax.random.uniform(jax.random.fold_in(own, position), (blocks,), jnp.float32, low / len(pieces), high / len(pieces)))
        loudness = loudness * jnp.repeat(steps, dims[position] // blocks).reshape([-1 if axis == position else 1 for axis in range(len(dims))])
    return loudness


def bell_draw(key, dims, spread, bound, pieces=(), kind=jnp.bfloat16):
    drawn = jax.random.normal(key, dims, jnp.float32) * spread
    if len(pieces) > 0:
        drawn = block_levels(key, dims, pieces, -0.22, 0.18) * drawn
    return jnp.clip(drawn, min=-bound, max=bound).astype(kind)


def noise_with(rng, extent, width, limit, cuts, heavy, kind=jnp.bfloat16):
    drawn = width * jax.random.normal(rng, extent, jnp.float32)
    if cuts:
        drawn = drawn * block_levels(rng, extent, cuts, -0.22, 0.18)
    return jnp.clip(spiked(drawn, jax.random.fold_in(rng, 3), *heavy), -limit, limit).astype(kind)


def setup_inputs(seed: int = 0) -> dict:
    arg_keys = jax.random.split(jax.random.key(seed), 11)
    return {
        "tokens": noise_with(arg_keys[0], (TOKENS, D), 1.0, 6.0, ((0, 32),), (0, 1, 32, 2.75)),
        "segment_ids": draw_segment_ids(jax.random.fold_in(arg_keys[10], 71), 0),
        "cotangent": noise_with(arg_keys[2], (TOKENS, D), 1.0, 6.0, ((0, 32),), (0, 1, 32, 2.75)),
        "w_qkv": bell_draw(arg_keys[3], (D, 3, D), D ** -0.5, 0.125, ((2, 4),)),
        "qkv_bias": bell_draw(arg_keys[4], (3, D), 0.3, 1.5, ((1, 4),), jnp.float32),
        "w_out": bell_draw(arg_keys[5], (D, D), (max(D * 4 // TOK_DP, 1)) ** -0.5, 2.0, ((0, 4),)),
        "w_gate_up": bell_draw(arg_keys[6], (D, 2, FF), D ** -0.5, 0.125, ((2, 4),)),
        "w_down": bell_draw(arg_keys[7], (FF, D), FF ** -0.5, 0.078125, ((0, 4),)),
        "norm_gains": jnp.clip(1.0 + 0.1 * jax.random.normal(arg_keys[8], (2, D), jnp.float32), 0.5, 1.5),
        "norm_biases": bell_draw(arg_keys[9], (2, D), 0.3, 1.5, (), jnp.float32),
    }


epsilon = 1e-05
rope_base = 10000.0

@jax.custom_vjp
def low(v):
    return lax.optimization_barrier(v.astype(jnp.bfloat16)).astype(jnp.float32)

@jax.custom_vjp
def low_back(v):
    return v

def low_keep(v):
    return (low(v), None)

def low_pass(kept, grad):
    return (grad,)

def back_keep(v):
    return (v, None)

def back_low(kept, grad):
    return (low(grad),)
low.defvjp(low_keep, low_pass)
low_back.defvjp(back_keep, back_low)

def layer_norm(values, gain_row, shift_row):
    average = lax.optimization_barrier(jnp.mean(values, axis=-1, keepdims=True))
    centered = values - average
    variance = lax.optimization_barrier(jnp.mean(centered * centered, axis=-1, keepdims=True))
    return centered * lax.rsqrt(variance + epsilon) * gain_row + shift_row

def positions_of(segments):
    row_index = jnp.arange(segments.shape[0], dtype=jnp.int32)
    previous = jnp.concatenate([jnp.full((1,), -2, jnp.int32), segments[:-1].astype(jnp.int32)])
    starts = jnp.where(segments != previous, row_index, 0).astype(jnp.int32)
    return row_index - lax.cummax(starts, axis=0)

def rotate(vectors, positions):
    half_rot = ROT // 2
    frequency = rope_base ** (-jnp.arange(half_rot).astype(jnp.float32) * 2.0 / ROT)
    angles = positions.astype(jnp.float32)[:, None] * frequency[None, :]
    cosine = jnp.cos(angles)[:, None, :]
    sine_part = jnp.sin(angles)[:, None, :]
    first_half = vectors[..., :half_rot]
    second = vectors[..., half_rot:ROT]
    return jnp.concatenate([first_half * cosine - second * sine_part, second * cosine + first_half * sine_part, vectors[..., ROT:]], axis=-1)

def group_forward(weights, inputs, segments):
    w_qkv, qkv_bias, w_out, w_gate_up, w_down, norm_gains, norm_biases = weights
    highest = lax.Precision.HIGHEST
    row_count = inputs.shape[0]
    positions = positions_of(segments)
    normed1 = low(layer_norm(inputs, norm_gains[0], norm_biases[0]))
    raw = low_back(jnp.einsum('td,dce->tce', normed1, w_qkv, precision=highest) + qkv_bias[None])
    raw = raw.reshape(row_count, 3, HEADS, HD)
    queries = low(rotate(raw[:, 0], positions))
    key_rows = low(rotate(raw[:, 1], positions))
    values = low(raw[:, 2])
    scores = low_back(jnp.einsum('qhd,khd->hqk', queries, key_rows, precision=highest) * HD ** (-0.5))
    row_index = jnp.arange(row_count, dtype=jnp.int32)
    allowed = (segments[:, None] == segments[None, :]) & (row_index[None, :] <= row_index[:, None])
    scores = jnp.where(allowed[None], scores, -1e+30)
    probs = low(jax.nn.softmax(scores, axis=-1))
    attended = low(low_back(jnp.einsum('hqk,khd->qhd', probs, values, precision=highest)))
    attended = attended.reshape(row_count, D)
    branch = low_back(jnp.dot(attended, w_out, precision=highest))
    hidden = inputs + branch
    normed2 = low(layer_norm(hidden, norm_gains[1], norm_biases[1]))
    gate_up = low_back(jnp.einsum('td,dcf->tcf', normed2, w_gate_up, precision=highest))
    activated = low(jax.nn.silu(gate_up[:, 0]) * gate_up[:, 1])
    return hidden + low_back(jnp.dot(activated, w_down, precision=highest))

def reference(tokens, segment_ids, cotangent, w_qkv, qkv_bias, w_out, w_gate_up, w_down, norm_gains, norm_biases):
    weights = tuple((member.astype(jnp.float32) for member in (w_qkv, qkv_bias, w_out, w_gate_up, w_down, norm_gains, norm_biases)))
    inputs = tokens.astype(jnp.float32).reshape(N_DP, TOK_DP, D)
    segments = segment_ids.astype(jnp.int32).reshape(N_DP, TOK_DP)
    live_mask = (segments >= 0).astype(jnp.float32)
    checked = jax.checkpoint(group_forward)

    def forward(weights, inputs):
        return lax.map(lambda member: checked(weights, member[0], member[1]), (inputs, segments))
    output, pullback = jax.vjp(forward, weights, inputs)
    incoming = cotangent.astype(jnp.float32).reshape(N_DP, TOK_DP, D) * live_mask[..., None]
    weight_grads, input_grad = pullback(incoming)
    live_total = jnp.sum(live_mask)
    scaled = [grad / live_total for grad in weight_grads]
    return (output.reshape(TOKENS, D).astype(jnp.bfloat16), input_grad.reshape(TOKENS, D), scaled[0], scaled[1], scaled[2], scaled[3], scaled[4], scaled[5], scaled[6])
```

```python
import functools

import jax
import jax.numpy as jnp
from jax import lax
from jax.experimental import pallas as pl
from jax.experimental.pallas import tpu as pltpu
from jax.sharding import PartitionSpec as P

HD = 64
ROT = 16
LANES = 128
epsilon = 1e-05
rope_base = 10000.0
BF = jnp.bfloat16
F32 = jnp.float32
VMEM_BYTES = 48 << 20
NT = (((1,), (1,)), ((), ()))
TN = (((0,), (0,)), ((), ()))


def layer_norm(values, gain_row, shift_row):
    average = jnp.mean(values, axis=-1, keepdims=True)
    centered = values - average
    variance = jnp.mean(centered * centered, axis=-1, keepdims=True)
    return centered * lax.rsqrt(variance + epsilon) * gain_row + shift_row


def positions_of(segments):
    row_index = jnp.arange(segments.shape[0], dtype=jnp.int32)
    previous = jnp.concatenate([jnp.full((1,), -2, jnp.int32), segments[:-1]])
    starts = jnp.where(segments != previous, row_index, 0)
    return row_index - lax.cummax(starts, axis=0)


def rope_tables(positions):
    half = ROT // 2
    dim = jnp.arange(LANES) % HD
    exponent = (dim % half).astype(F32) * 2.0 / ROT
    frequency = jnp.where(dim < ROT, rope_base ** (-exponent), 0.0)
    angles = positions.astype(F32)[:, None] * frequency[None, :]
    cosine, sine = jnp.cos(angles), jnp.sin(angles)
    lower = jnp.where(dim < half, -sine, 0.0)
    upper = jnp.where((dim >= half) & (dim < ROT), sine, 0.0)
    return jnp.stack([cosine, lower, upper])


def turn(block, table_ref, rows, sign):
    half = ROT // 2
    back = pltpu.roll(block, LANES - half, 1)
    ahead = pltpu.roll(block, half, 1)
    return (
        block * table_ref[0, rows, :]
        + sign * (back * table_ref[1, rows, :] + ahead * table_ref[2, rows, :])
    )


def project_kernel(first_ref, second_ref, w_ref, bias_ref, table_ref, out_ref, rows_ref):
    shard = first_ref.shape[0]

    @pl.when(pl.program_id(0) == 0)
    def _():
        rows_ref[:shard, :] = first_ref[...]
        rows_ref[shard:, :] = second_ref[...]

    raw = jnp.dot(rows_ref[...], w_ref[0], preferred_element_type=F32) + bias_ref[0]

    @pl.when(pl.program_id(0) < 2)
    def _():
        for start in range(0, raw.shape[1], LANES):
            piece = turn(raw[:, start : start + LANES], table_ref, slice(None), 1.0)
            out_ref[0, :, start : start + LANES] = piece.astype(BF)

    @pl.when(pl.program_id(0) == 2)
    def _():
        out_ref[0] = raw.astype(BF)


def project(first, second, w, bias, table):
    shard, width = first.shape
    local_width = w.shape[2]
    return pl.pallas_call(
        project_kernel,
        grid=(3,),
        in_specs=[
            pl.BlockSpec((shard, width), lambda c: (0, 0)),
            pl.BlockSpec((shard, width), lambda c: (0, 0)),
            pl.BlockSpec((1, width, local_width), lambda c: (c, 0, 0)),
            pl.BlockSpec((1, 1, local_width), lambda c: (c, 0, 0)),
            pl.BlockSpec((3, 2 * shard, LANES), lambda c: (0, 0, 0)),
        ],
        out_specs=pl.BlockSpec((1, 2 * shard, local_width), lambda c: (c, 0, 0)),
        out_shape=jax.ShapeDtypeStruct((3, 2 * shard, local_width), BF),
        scratch_shapes=[pltpu.VMEM((2 * shard, width), BF)],
        compiler_params=pltpu.CompilerParams(vmem_limit_bytes=VMEM_BYTES),
        cost_estimate=pl.CostEstimate(
            flops=12 * shard * width * local_width,
            bytes_accessed=6 * width * local_width,
            transcendentals=0,
        ),
    )(first, second, w, bias, table)


def head_lanes(shape, head):
    lane = lax.broadcasted_iota(jnp.int32, shape, 1)
    return (lane < HD) if head == 0 else (lane >= HD)


def attend_kernel(count, me_ref, column_ref, row_ref, low_ref, out_ref, lse_ref, bias_ref):
    me = me_ref[0]
    shard = column_ref.shape[0] // count

    def place(index):
        return pl.multiple_of((index ^ me) * shard, shard)

    @pl.when(pl.program_id(0) == 0)
    def _():
        for index in range(count):
            span = (index + 1) * shard
            rows = slice(index * shard, span)
            own = lax.broadcasted_iota(jnp.int32, (shard, span), 0) + index * shard
            other = lax.broadcasted_iota(jnp.int32, (shard, span), 1)
            allowed = (column_ref[rows, :] == row_ref[:, :span]) & (other <= own)
            bias_ref[rows, :span] = jnp.where(allowed, 0.0, -1e30)

    lane = lax.broadcasted_iota(jnp.int32, (shard, LANES), 1)
    for index in range(count):
        rows = slice(index * shard, (index + 1) * shard)
        query = low_ref[0, pl.ds(place(index), shard), :]
        parts, sums = [], []
        for head in range(2):
            mine = jnp.where(head_lanes(query.shape, head), query, 0) * jnp.asarray(HD**-0.5, BF)
            scores = []
            for other in range(index + 1):
                keys = low_ref[1, pl.ds(place(other), shard), :]
                scores.append(
                    lax.dot_general(mine, keys, NT, preferred_element_type=F32)
                    + bias_ref[rows, other * shard : (other + 1) * shard]
                )
            largest = functools.reduce(
                jnp.maximum, [jnp.max(s, axis=1, keepdims=True) for s in scores]
            )
            total, acc = 0.0, 0.0
            for other in range(index + 1):
                lifted = jnp.exp(scores[other] - largest)
                total = total + jnp.sum(lifted, axis=1, keepdims=True)
                acc = acc + jnp.dot(
                    lifted.astype(BF),
                    low_ref[2, pl.ds(place(other), shard), :],
                    preferred_element_type=F32,
                )
            parts.append(acc / total)
            sums.append(largest + jnp.log(total))
        out_ref[pl.ds(place(index), shard), :] = jnp.where(lane < HD, parts[0], parts[1]).astype(BF)
        wide = jnp.where(lane == 0, sums[0], jnp.where(lane == 1, sums[1], 0.0))
        lse_ref[0, :, rows] = wide.T[:8, :]


def attend(me, segments, qkv):
    _, group, local_width = qkv.shape
    count = 4
    pairs = local_width // LANES

    def kernel(me_ref, column_ref, row_ref, qkv_ref, out_ref, lse_ref, bias_ref):
        attend_kernel(count, me_ref, column_ref, row_ref, qkv_ref, out_ref, lse_ref, bias_ref)

    return pl.pallas_call(
        kernel,
        grid_spec=pltpu.PrefetchScalarGridSpec(
            num_scalar_prefetch=1,
            grid=(pairs,),
            in_specs=[
                pl.BlockSpec((group, 1), lambda p, me: (0, 0)),
                pl.BlockSpec((1, group), lambda p, me: (0, 0)),
                pl.BlockSpec((3, group, LANES), lambda p, me: (0, 0, p)),
            ],
            out_specs=[
                pl.BlockSpec((group, LANES), lambda p, me: (0, p)),
                pl.BlockSpec((1, 8, group), lambda p, me: (p, 0, 0)),
            ],
            scratch_shapes=[pltpu.VMEM((group, group), F32)],
        ),
        out_shape=[
            jax.ShapeDtypeStruct((group, local_width), BF),
            jax.ShapeDtypeStruct((pairs, 8, group), F32),
        ],
        compiler_params=pltpu.CompilerParams(vmem_limit_bytes=VMEM_BYTES),
        cost_estimate=pl.CostEstimate(
            flops=16 * group * group * local_width, bytes_accessed=8 * group * local_width,
            transcendentals=group * group * local_width // HD,
        ),
    )(me, segments[:, None], segments[None, :], qkv)


def attend_back_kernel(
    count, me_ref, column_ref, row_ref, qkv_ref, out_ref, grad_ref, lse_ref, table_ref,
    raw_ref, bias_ref, key_grad_ref, value_grad_ref, key_turned_ref,
):
    me = me_ref[0]
    pair = pl.program_id(0)
    group = column_ref.shape[0]
    shard = group // count
    local_width = raw_ref.shape[1] // 3
    scale = jnp.asarray(HD**-0.5, BF)

    def place(index):
        return pl.multiple_of((index ^ me) * shard, shard)

    def target(part):
        return pl.ds(pl.multiple_of(part * local_width + pair * LANES, LANES), LANES)

    @pl.when(pair == 0)
    def _():
        for index in range(count):
            rows = slice(index * shard, group)
            keys = lax.broadcasted_iota(jnp.int32, (shard, group - index * shard), 0)
            queries = lax.broadcasted_iota(jnp.int32, (shard, group - index * shard), 1)
            own = slice(index * shard, (index + 1) * shard)
            allowed = (column_ref[own, :] == row_ref[:, rows]) & (keys <= queries)
            bias_ref[own, rows] = jnp.where(allowed, 0.0, -1e30)

    for index in range(count):
        rows = slice(index * shard, (index + 1) * shard)
        keys = qkv_ref[1, pl.ds(place(index), shard), :]
        key_turned_ref[:, rows] = keys.astype(F32).T.astype(BF)

    sub = lax.broadcasted_iota(jnp.int32, (8, LANES), 0)
    lane = lax.broadcasted_iota(jnp.int32, (8, LANES), 1)
    chooser = jnp.where((lane // HD) == sub, 1.0, 0.0)
    for index in range(count):
        rows = slice(index * shard, (index + 1) * shard)
        here = pl.ds(place(index), shard)
        query = qkv_ref[0, here, :]
        grad = grad_ref[here, :]
        product = grad.astype(F32) * out_ref[here, :].astype(F32)
        centres = lax.dot_general(
            chooser, product, NT, precision=lax.Precision.HIGHEST, preferred_element_type=F32
        )
        turned = []
        for head in range(2):
            chosen = head_lanes(query.shape, head)
            mine = jnp.where(chosen, query, 0) * scale
            grad_mine = jnp.where(chosen, grad, 0)
            lse = lse_ref[0, head : head + 1, rows]
            centre = centres[head : head + 1, :]
            query_turned = 0.0
            for other in range(index + 1):
                there = pl.ds(place(other), shard)
                span = slice(other * shard, (other + 1) * shard)
                scores = lax.dot_general(
                    qkv_ref[1, there, :], mine, NT, preferred_element_type=F32
                )
                probs = jnp.exp(scores + bias_ref[span, rows] - lse)
                prob_grad = lax.dot_general(
                    qkv_ref[2, there, :], grad_mine, NT, preferred_element_type=F32
                )
                cot = (probs * (prob_grad - centre)).astype(BF)
                value_add = jnp.dot(probs.astype(BF), grad_mine, preferred_element_type=F32)
                key_add = jnp.dot(cot, mine, preferred_element_type=F32)
                if other == index and head == 0:
                    value_grad_ref[span, :] = value_add
                    key_grad_ref[span, :] = key_add
                else:
                    value_grad_ref[span, :] += value_add
                    key_grad_ref[span, :] += key_add
                query_turned = query_turned + jnp.dot(
                    key_turned_ref[head * HD : (head + 1) * HD, span],
                    cot,
                    preferred_element_type=F32,
                )
            turned.append(query_turned)
        query_grad = jnp.concatenate(turned, axis=0).T * HD**-0.5
        raw_ref[here, target(0)] = turn(query_grad, table_ref, here, -1.0).astype(BF)
    for index in range(count):
        rows = slice(index * shard, (index + 1) * shard)
        here = pl.ds(place(index), shard)
        raw_ref[here, target(1)] = turn(key_grad_ref[rows, :], table_ref, here, -1.0).astype(BF)
        raw_ref[here, target(2)] = value_grad_ref[rows, :].astype(BF)


def attend_back(me, segments, qkv, attended, grad, lse, table):
    _, group, local_width = qkv.shape
    count = 4
    pairs = local_width // LANES
    return pl.pallas_call(
        functools.partial(attend_back_kernel, count),
        grid_spec=pltpu.PrefetchScalarGridSpec(
            num_scalar_prefetch=1,
            grid=(pairs,),
            in_specs=[
                pl.BlockSpec((group, 1), lambda p, me: (0, 0)),
                pl.BlockSpec((1, group), lambda p, me: (0, 0)),
                pl.BlockSpec((3, group, LANES), lambda p, me: (0, 0, p)),
                pl.BlockSpec((group, LANES), lambda p, me: (0, p)),
                pl.BlockSpec((group, LANES), lambda p, me: (0, p)),
                pl.BlockSpec((1, 8, group), lambda p, me: (p, 0, 0)),
                pl.BlockSpec((3, group, LANES), lambda p, me: (0, 0, 0)),
            ],
            out_specs=pl.BlockSpec((group, 3 * local_width), lambda p, me: (0, 0)),
            scratch_shapes=[
                pltpu.VMEM((group, group), F32),
                pltpu.VMEM((group, LANES), F32),
                pltpu.VMEM((group, LANES), F32),
                pltpu.VMEM((LANES, group), BF),
            ],
        ),
        out_shape=jax.ShapeDtypeStruct((group, 3 * local_width), BF),
        compiler_params=pltpu.CompilerParams(vmem_limit_bytes=VMEM_BYTES),
        cost_estimate=pl.CostEstimate(
            flops=32 * group * group * local_width, bytes_accessed=20 * group * local_width,
            transcendentals=group * group * local_width // HD,
        ),
    )(me, segments[:, None], segments[None, :], qkv, attended, grad, lse, table)


def weight_grad(blocks, rows, cots):
    many = blocks.shape[0]
    tokens, width = rows.shape
    units = cots.shape[1]
    depth = width // (2 * many)
    if depth % LANES:
        return [
            lax.dot_general(
                lax.dynamic_slice_in_dim(rows, blocks[index] * depth, depth, 1),
                cots,
                TN,
                preferred_element_type=F32,
            ).astype(BF)
            for index in range(many)
        ]

    def kernel(blocks_ref, rows_ref, cots_ref, *out_refs):
        product = lax.dot_general(rows_ref[...], cots_ref[...], TN, preferred_element_type=F32)
        for index, out_ref in enumerate(out_refs):

            @pl.when(pl.program_id(0) == index)
            def _():
                out_ref[...] = product.astype(BF)

    return pl.pallas_call(
        kernel,
        grid_spec=pltpu.PrefetchScalarGridSpec(
            num_scalar_prefetch=1,
            grid=(many,),
            in_specs=[
                pl.BlockSpec((tokens, depth), lambda i, blocks: (0, blocks[i])),
                pl.BlockSpec((tokens, units), lambda i, blocks: (0, 0)),
            ],
            out_specs=[pl.BlockSpec((depth, units), lambda i, blocks: (0, 0))] * many,
        ),
        out_shape=[jax.ShapeDtypeStruct((depth, units), BF)] * many,
        compiler_params=pltpu.CompilerParams(vmem_limit_bytes=VMEM_BYTES),
        cost_estimate=pl.CostEstimate(
            flops=2 * many * depth * tokens * units,
            bytes_accessed=2 * (tokens * units + many * depth * (tokens + units)),
            transcendentals=0,
        ),
    )(blocks, rows, cots)


def local(
    n_dp,
    tokens,
    segment_ids,
    cotangent,
    w_qkv,
    qkv_bias,
    w_out,
    w_gate_up,
    w_down,
    norm_gains,
    norm_biases,
):
    shard, width = tokens.shape
    group = segment_ids.shape[0]
    local_width = w_out.shape[0]
    units = w_down.shape[0]
    n_tensor = group // shard
    n_ring = n_dp // 2
    me = lax.axis_index("tensor")
    data_index = lax.axis_index("dp")
    to_core = [(t, t ^ 1) for t in range(n_tensor)]
    to_x = [(t, t ^ 2) for t in range(n_tensor)]
    to_y = [(d, d ^ 1) for d in range(n_dp)]
    up_z = [(d, (d + 2) % n_dp) for d in range(n_dp)]

    def core(value):
        return lax.ppermute(value, "tensor", to_core)

    def across(value):
        return lax.ppermute(value, "tensor", to_x)

    def after(value, *earlier):
        return lax.optimization_barrier((value, *earlier))[0]

    def gather(own):
        far = across(own)
        return own, core(own), far, core(far)

    def scatter_far(far_pair):
        mixed = far_pair[:shard].astype(F32) + core(far_pair[shard:]).astype(F32)
        return across(mixed.astype(BF))

    def scatter_near(near_pair, far):
        near = core(near_pair[shard:].astype(BF)).astype(F32)
        return near_pair[:shard].astype(F32) + near + far.astype(F32)

    def everywhere(value):
        for step in range((n_dp - 1).bit_length()):
            value = value + lax.ppermute(value, "dp", [(d, d ^ (1 << step)) for d in range(n_dp)])
        return value

    def in_pieces(values):
        blocks = values.reshape((n_tensor, shard) + values.shape[1:])
        return jnp.concatenate(
            [lax.dynamic_index_in_dim(blocks, me ^ k, 0, False) for k in range(n_tensor)], 0
        )

    ring_index = data_index // 2
    ring_order = jnp.stack([(ring_index - 1 - s + 2 * n_ring) % n_ring for s in range(n_ring)])
    keep_blocks = 2 * ring_order + data_index % 2
    send_blocks = 2 * ring_order + 1 - data_index % 2

    def ring_sum(kept, received):
        carried = None
        for step in range(n_ring):
            total = kept[step].astype(F32) + received[step].astype(F32)
            if carried is not None:
                total = total + carried.astype(F32)
            if step < n_ring - 1:
                carried = lax.ppermute(total.astype(BF), "dp", up_z)
        return total

    def reduce_weight(rows, cots):
        sent = weight_grad(send_blocks, rows, cots)
        received = [lax.ppermute(part, "dp", to_y) for part in sent]
        kept = weight_grad(keep_blocks, after(rows, sent[-1]), cots)
        return ring_sum(kept, received)

    me_one = me[None].astype(jnp.int32)
    live = (segment_ids >= 0).astype(F32)
    live_total = everywhere(jnp.sum(live)[None])[0]
    live_rows = lax.dynamic_slice_in_dim(live, me * shard, shard, 0)
    inputs = tokens.astype(F32)
    normed_one, norm_one_back = jax.vjp(layer_norm, inputs, norm_gains[0], norm_biases[0])
    one = gather(normed_one.astype(BF))
    out_cot = cotangent.astype(F32) * live_rows[:, None]
    incoming = gather(after(out_cot.astype(BF), one[2]))
    incoming_full = jnp.concatenate(incoming, 0)
    table = rope_tables(in_pieces(positions_of(segment_ids)))
    w_qkv_split = jnp.transpose(w_qkv, (1, 0, 2))
    w_qkv_flat = w_qkv.reshape(width, 3 * local_width)
    w_gate_up_flat = w_gate_up.reshape(width, 2 * units)
    bias_rows = qkv_bias[:, None, :]
    near = project(one[0], one[1], w_qkv_split, bias_rows, table[:, : 2 * shard])
    far = project(one[2], one[3], w_qkv_split, bias_rows, table[:, 2 * shard :])
    qkv = jnp.concatenate([near, far], axis=1)
    attended, lse = attend(me_one, segment_ids, qkv)
    branch_far = jnp.dot(attended[2 * shard :], w_out, preferred_element_type=F32).astype(BF)
    branch_sent = scatter_far(branch_far)
    branch_near = jnp.dot(
        after(attended[: 2 * shard], branch_far), w_out, preferred_element_type=F32
    )
    hidden = inputs + scatter_near(branch_near, branch_sent)
    normed_two, norm_two_back = jax.vjp(layer_norm, hidden, norm_gains[1], norm_biases[1])
    two = gather(normed_two.astype(BF))
    act_grad = lax.dot_general(incoming_full, w_down, NT, preferred_element_type=F32)

    def feed(first, second, act_grad_rows):
        rows = jnp.concatenate([first, second], 0)
        gate_up = jnp.dot(rows, w_gate_up_flat, preferred_element_type=F32)
        gate, up = gate_up[:, :units], gate_up[:, units:]
        s = jax.nn.sigmoid(gate)
        silu = gate * s
        activated = (silu * up).astype(BF)
        gate_grad = act_grad_rows * up * (s + silu * (1.0 - s))
        up_grad = act_grad_rows * silu
        return rows, activated, jnp.concatenate([gate_grad, up_grad], 1).astype(BF)

    near_rows, near_act, near_cot = feed(two[0], two[1], act_grad[: 2 * shard])
    far_rows, far_act, far_cot = feed(two[2], two[3], act_grad[2 * shard :])
    second_full = jnp.concatenate([near_rows, far_rows], 0)
    activated = jnp.concatenate([near_act, far_act], 0)
    gate_up_cot = jnp.concatenate([near_cot, far_cot], 0)

    down_sum = reduce_weight(incoming_full, activated)

    second_far = lax.dot_general(
        far_cot, w_gate_up_flat, NT, preferred_element_type=F32
    ).astype(BF)
    second_sent = scatter_far(second_far)
    second_near = lax.dot_general(
        after(near_cot, second_far), w_gate_up_flat, NT, preferred_element_type=F32
    )
    gate_up_sum = reduce_weight(after(second_full, second_far), gate_up_cot)
    second_grad = scatter_near(second_near, second_sent)
    hidden_part, gain_two, bias_two = norm_two_back(second_grad)
    hidden_grad = out_cot + hidden_part
    branch = gather(hidden_grad.astype(BF))
    branch_full = jnp.concatenate(branch, 0)

    down_far = jnp.dot(far_act, w_down, preferred_element_type=F32).astype(BF)
    down_sent = scatter_far(after(down_far, branch[2]))
    down_near = jnp.dot(near_act, w_down, preferred_element_type=F32)
    output = (hidden + scatter_near(down_near, down_sent)).astype(BF)

    attended_grad = lax.dot_general(
        branch_full, w_out, NT, preferred_element_type=F32
    ).astype(BF)
    raw_cot = attend_back(me_one, segment_ids, qkv, attended, attended_grad, lse, table)
    out_sum = reduce_weight(branch_full, attended)
    qkv_sum = reduce_weight(jnp.concatenate(one, 0), raw_cot)
    first_far = lax.dot_general(
        raw_cot[2 * shard :], w_qkv_flat, NT, preferred_element_type=F32
    ).astype(BF)
    first_sent = scatter_far(first_far)
    first_near = lax.dot_general(
        raw_cot[: 2 * shard], w_qkv_flat, NT, preferred_element_type=F32
    )
    first_grad = scatter_near(first_near, first_sent)
    input_part, gain_one, bias_one = norm_one_back(first_grad)
    input_grad = hidden_grad + input_part

    bias_sum = everywhere(jnp.sum(raw_cot.astype(F32), axis=0).reshape(3, local_width))
    rows_sum = jnp.stack([gain_one, gain_two, bias_one, bias_two])
    rows_sum = rows_sum + core(rows_sum)
    rows_sum = everywhere(rows_sum + across(rows_sum)) / live_total
    return (
        output,
        input_grad,
        qkv_sum.reshape(-1, 3, local_width) / live_total,
        bias_sum / live_total,
        out_sum.T / live_total,
        gate_up_sum.reshape(-1, 2, units) / live_total,
        down_sum.T / live_total,
        rows_sum[:2],
        rows_sum[2:],
    )


def solution(mesh):
    in_specs = (
        P(("dp", "tensor"), None),
        P("dp"),
        P(("dp", "tensor"), None),
        P(None, None, "tensor"),
        P(None, "tensor"),
        P("tensor", None),
        P(None, None, "tensor"),
        P("tensor", None),
        P(),
        P(),
    )
    out_specs = (
        P(("dp", "tensor"), None),
        P(("dp", "tensor"), None),
        P("dp", None, "tensor"),
        P(None, "tensor"),
        P("tensor", "dp"),
        P("dp", None, "tensor"),
        P("tensor", "dp"),
        P(),
        P(),
    )
    return jax.shard_map(
        functools.partial(local, mesh.shape["dp"]),
        mesh=mesh,
        in_specs=in_specs,
        out_specs=out_specs,
        check_vma=False,
    )
```

```python
import functools

import jax
import jax.numpy as jnp
from jax import lax
from jax.experimental import pallas as pl
from jax.experimental.pallas import tpu as pltpu
from jax.sharding import PartitionSpec as P

HD = 64
ROT = 16
LANES = 128
epsilon = 1e-05
rope_base = 10000.0
BF = jnp.bfloat16
F32 = jnp.float32
VMEM_BYTES = 48 << 20
MOST_VMEM_BYTES = 60 << 20
LIGHT = pl.CostEstimate(flops=1, bytes_accessed=1, transcendentals=0)
NT = (((1,), (1,)), ((), ()))
TN = (((0,), (0,)), ((), ()))
NN = (((1,), (0,)), ((), ()))


def positions_of(segments):
    row_index = jnp.arange(segments.shape[0], dtype=jnp.int32)
    previous = jnp.concatenate([jnp.full((1,), -2, jnp.int32), segments[:-1]])
    starts = jnp.where(segments != previous, row_index, 0)
    return row_index - lax.cummax(starts, axis=0)


def rope_tables(positions):
    half = ROT // 2
    dim = jnp.arange(LANES) % HD
    exponent = (dim % half).astype(F32) * 2.0 / ROT
    frequency = jnp.where(dim < ROT, rope_base ** (-exponent), 0.0)
    angles = positions.astype(F32)[:, None] * frequency[None, :]
    cosine, sine = jnp.cos(angles), jnp.sin(angles)
    lower = jnp.where(dim < half, -sine, 0.0)
    upper = jnp.where((dim >= half) & (dim < ROT), sine, 0.0)
    return jnp.stack([cosine, lower, upper])


def turn(block, table_ref, rows, sign):
    half = ROT // 2
    back = pltpu.roll(block, LANES - half, 1)
    ahead = pltpu.roll(block, half, 1)
    return (
        block * table_ref[0, rows, :]
        + sign * (back * table_ref[1, rows, :] + ahead * table_ref[2, rows, :])
    )


def project_kernel(
    first_ref, second_ref, w_ref, bias_ref, table_ref, old_ref, out_ref, rows_ref
):
    shard = first_ref.shape[0]

    @pl.when(pl.program_id(0) == 0)
    def _():
        rows_ref[:shard, :] = first_ref[...]
        rows_ref[shard:, :] = second_ref[...]

    raw = jnp.dot(rows_ref[...], w_ref[0], preferred_element_type=F32) + bias_ref[0]

    @pl.when(pl.program_id(0) < 2)
    def _():
        for start in range(0, raw.shape[1], LANES):
            piece = turn(raw[:, start : start + LANES], table_ref, slice(None), 1.0)
            out_ref[0, :, start : start + LANES] = piece.astype(BF)

    @pl.when(pl.program_id(0) == 2)
    def _():
        out_ref[0] = raw.astype(BF)


def project(half, first, second, w, bias, table, old):
    shard, width = first.shape
    local_width = w.shape[2]
    whole = jax.ShapeDtypeStruct((3, 4 * shard, local_width), BF)
    kernel = project_kernel
    operands = [first, second, w, bias, table]
    specs = [
        pl.BlockSpec((shard, width), lambda c: (0, 0)),
        pl.BlockSpec((shard, width), lambda c: (0, 0)),
        pl.BlockSpec((1, width, local_width), lambda c: (c, 0, 0)),
        pl.BlockSpec((1, 1, local_width), lambda c: (c, 0, 0)),
        pl.BlockSpec((3, 2 * shard, LANES), lambda c: (0, half, 0)),
    ]
    aliases = {}
    if old is None:

        def kernel(a, b, c, d, e, out_ref, rows_ref):
            project_kernel(a, b, c, d, e, None, out_ref, rows_ref)

    else:
        operands.append(old)
        specs.append(pl.BlockSpec(memory_space=pl.ANY))
        aliases = {5: 0}
    return pl.pallas_call(
        kernel,
        grid=(3,),
        in_specs=specs,
        out_specs=pl.BlockSpec((1, 2 * shard, local_width), lambda c: (c, half, 0)),
        out_shape=whole,
        input_output_aliases=aliases,
        scratch_shapes=[pltpu.VMEM((2 * shard, width), BF)],
        compiler_params=pltpu.CompilerParams(vmem_limit_bytes=MOST_VMEM_BYTES),
        cost_estimate=LIGHT,
    )(*operands)


def feed_kernel(
    first_ref, second_ref, w0_ref, w1_ref, w2_ref, w3_ref, act_grad_ref,
    act_ref, gate_ref, up_ref, rows_ref, w_ref,
):
    shard = first_ref.shape[0]

    @pl.when(pl.program_id(0) == 0)
    def _():
        rows_ref[:shard, :] = first_ref[...]
        rows_ref[shard:, :] = second_ref[...]

    for index, part_ref in enumerate((w0_ref, w1_ref, w2_ref, w3_ref)):
        w_ref[:, index * LANES : (index + 1) * LANES] = part_ref[...]
    products = [
        jnp.dot(
            rows_ref[...],
            w_ref[:, 2 * index * LANES : 2 * (index + 1) * LANES],
            preferred_element_type=F32,
        )
        for index in range(2)
    ]
    for index, product in enumerate(products):
        lanes = slice(index * LANES, (index + 1) * LANES)
        gate, up = product[:, :LANES], product[:, LANES:]
        s = jax.nn.sigmoid(gate)
        silu = gate * s
        act_grad = act_grad_ref[:, lanes].astype(F32)
        act_ref[:, lanes] = (silu * up).astype(BF)
        gate_ref[:, lanes] = (act_grad * up * (s + silu * (1.0 - s))).astype(BF)
        up_ref[:, lanes] = (act_grad * silu).astype(BF)


def feed(half, first, second, w, act_grad, old):
    shard, width = first.shape
    units = w.shape[1] // 2
    tiles = units // LANES

    def tile(base, index):
        return pl.BlockSpec(
            (width, LANES), lambda j: (0, base + jnp.minimum(2 * j + index, tiles - 1))
        )

    operands = [first, second, w, w, w, w, act_grad]
    specs = [
        pl.BlockSpec((shard, width), lambda j: (0, 0)),
        pl.BlockSpec((shard, width), lambda j: (0, 0)),
        tile(0, 0),
        tile(tiles, 0),
        tile(0, 1),
        tile(tiles, 1),
        pl.BlockSpec((2 * shard, 2 * LANES), lambda j: (half, j)),
    ]
    kernel = feed_kernel
    aliases = {}
    if old is not None:

        def kernel(*refs):
            feed_kernel(*refs[:7], *refs[10:])

        operands += list(old)
        specs += [pl.BlockSpec(memory_space=pl.ANY)] * 3
        aliases = {7: 0, 8: 1, 9: 2}
    return pl.pallas_call(
        kernel,
        grid=(pl.cdiv(tiles, 2),),
        in_specs=specs,
        out_specs=[pl.BlockSpec((2 * shard, 2 * LANES), lambda j: (half, j))] * 3,
        out_shape=[jax.ShapeDtypeStruct((4 * shard, units), BF)] * 3,
        input_output_aliases=aliases,
        scratch_shapes=[pltpu.VMEM((2 * shard, width), BF), pltpu.VMEM((width, 4 * LANES), BF)],
        compiler_params=pltpu.CompilerParams(vmem_limit_bytes=MOST_VMEM_BYTES),
        cost_estimate=LIGHT,
    )(*operands)


def pair_product(half, rows, w, dims):
    group = rows[0].shape[0]
    shard = group // 4
    depth = sum(r.shape[1] for r in rows)
    turned = dims is NT
    width = w.shape[-2] if turned else w.shape[-1]
    tile = min(512, width)
    if w.ndim == 3:
        w_spec = pl.BlockSpec((w.shape[0], tile, w.shape[2]), lambda j: (0, j, 0))
    elif turned:
        w_spec = pl.BlockSpec((tile, depth), lambda j: (j, 0))
    else:
        w_spec = pl.BlockSpec((depth, tile), lambda j: (0, j))

    def kernel(*refs):
        *rows_refs, w_ref, first_ref, second_ref = refs
        if w.ndim == 3:
            part = w.shape[2]
            product = sum(
                lax.dot_general(
                    rows_refs[0][:, c * part : (c + 1) * part],
                    w_ref[c],
                    dims,
                    preferred_element_type=F32,
                )
                for c in range(w.shape[0])
            )
        elif turned:
            product, start = 0.0, 0
            for rows_ref in rows_refs:
                end = start + rows_ref.shape[1]
                product = product + lax.dot_general(
                    rows_ref[...], w_ref[:, start:end], dims, preferred_element_type=F32
                )
                start = end
        else:
            product = lax.dot_general(
                rows_refs[0][...], w_ref[...], dims, preferred_element_type=F32
            )
        product = product.astype(BF)
        first_ref[...] = product[:shard]
        second_ref[...] = product[shard:]

    return pl.pallas_call(
        kernel,
        grid=(width // tile,),
        in_specs=[pl.BlockSpec((2 * shard, r.shape[1]), lambda j: (half, 0)) for r in rows]
        + [w_spec],
        out_specs=[pl.BlockSpec((shard, tile), lambda j: (0, j))] * 2,
        out_shape=[jax.ShapeDtypeStruct((shard, width), BF)] * 2,
        compiler_params=pltpu.CompilerParams(vmem_limit_bytes=VMEM_BYTES),
        cost_estimate=LIGHT,
    )(*rows, w)


def centre_rows(values):
    average = jnp.mean(values, axis=-1, keepdims=True)
    centered = values - average
    variance = jnp.mean(centered * centered, axis=-1, keepdims=True)
    spread = lax.rsqrt(variance + epsilon)
    return centered * spread, spread


ROW_STEP = 64


def row_call(kernel, shard, width, inputs, per_row, outs):
    step = min(ROW_STEP, shard)
    specs = [
        pl.BlockSpec((step, a.shape[1]), lambda i: (i, 0))
        if rowwise
        else pl.BlockSpec(a.shape, lambda i: (0, 0))
        for a, rowwise in zip(inputs, per_row)
    ]
    out_specs = [
        pl.BlockSpec((step, width), lambda i: (i, 0))
        if o.shape[0] == shard
        else pl.BlockSpec(o.shape, lambda i: (0, 0))
        for o in outs
    ]
    return pl.pallas_call(
        kernel,
        grid=(shard // step,),
        in_specs=specs,
        out_specs=out_specs,
        out_shape=outs,
        compiler_params=pltpu.CompilerParams(vmem_limit_bytes=VMEM_BYTES),
        cost_estimate=LIGHT,
    )(*inputs)


def norm_rows(tokens, gain, shift):
    def kernel(tokens_ref, gain_ref, shift_ref, out_ref):
        hat, _ = centre_rows(tokens_ref[...].astype(F32))
        out_ref[...] = (hat * gain_ref[...] + shift_ref[...]).astype(BF)

    shard, width = tokens.shape
    return row_call(
        kernel, shard, width, (tokens, gain, shift), (1, 0, 0),
        [jax.ShapeDtypeStruct((shard, width), BF)],
    )[0]


def add_norm_rows(tokens, own, near, far, gain, shift):
    def kernel(tokens_ref, own_ref, near_ref, far_ref, gain_ref, shift_ref, hidden_ref, out_ref):
        hidden = tokens_ref[...].astype(F32) + (
            own_ref[...].astype(F32) + near_ref[...].astype(F32) + far_ref[...].astype(F32)
        )
        hidden_ref[...] = hidden
        hat, _ = centre_rows(hidden)
        out_ref[...] = (hat * gain_ref[...] + shift_ref[...]).astype(BF)

    shard, width = tokens.shape
    return row_call(
        kernel, shard, width, (tokens, own, near, far, gain, shift), (1, 1, 1, 1, 0, 0),
        [jax.ShapeDtypeStruct((shard, width), F32), jax.ShapeDtypeStruct((shard, width), BF)],
    )


def norm_rows_back(values, own, near, far, base, gain, dtypes):
    def kernel(values_ref, own_ref, near_ref, far_ref, base_ref, gain_ref, *out_refs):
        *grad_refs, sums_ref = out_refs
        hat, spread = centre_rows(values_ref[...].astype(F32))
        grad = own_ref[...].astype(F32) + near_ref[...].astype(F32) + far_ref[...].astype(F32)
        scaled = grad * gain_ref[...]
        mean_scaled = jnp.mean(scaled, axis=-1, keepdims=True)
        mean_hat = jnp.mean(scaled * hat, axis=-1, keepdims=True)
        result = base_ref[...].astype(F32) + spread * (scaled - mean_scaled - hat * mean_hat)
        for ref in grad_refs:
            ref[...] = result.astype(ref.dtype)
        sums = jnp.concatenate(
            [
                jnp.sum(grad * hat, axis=0, keepdims=True),
                jnp.sum(grad, axis=0, keepdims=True),
            ],
            0,
        )

        @pl.when(pl.program_id(0) == 0)
        def _():
            sums_ref[...] = sums

        @pl.when(pl.program_id(0) > 0)
        def _():
            sums_ref[...] += sums

    shard, width = values.shape
    return row_call(
        kernel, shard, width, (values, own, near, far, base, gain), (1, 1, 1, 1, 1, 0),
        [jax.ShapeDtypeStruct((shard, width), d) for d in dtypes]
        + [jax.ShapeDtypeStruct((2, width), F32)],
    )


def head_lanes(shape, head):
    lane = lax.broadcasted_iota(jnp.int32, shape, 1)
    return (lane < HD) if head == 0 else (lane >= HD)


def attend_kernel(count, me_ref, column_ref, row_ref, low_ref, out_ref, lse_ref, bias_ref):
    me = me_ref[0]
    shard = column_ref.shape[0] // count

    def place(index):
        return pl.multiple_of((index ^ me) * shard, shard)

    @pl.when(pl.program_id(0) == 0)
    def _():
        for index in range(count):
            span = (index + 1) * shard
            rows = slice(index * shard, span)
            own = lax.broadcasted_iota(jnp.int32, (shard, span), 0) + index * shard
            other = lax.broadcasted_iota(jnp.int32, (shard, span), 1)
            allowed = (column_ref[rows, :] == row_ref[:, :span]) & (other <= own)
            bias_ref[rows, :span] = jnp.where(allowed, 0.0, -1e30)

    lane = lax.broadcasted_iota(jnp.int32, (shard, LANES), 1)
    for index in range(count):
        rows = slice(index * shard, (index + 1) * shard)
        query = low_ref[0, pl.ds(place(index), shard), :]
        parts, sums = [], []
        for head in range(2):
            mine = jnp.where(head_lanes(query.shape, head), query, 0) * jnp.asarray(HD**-0.5, BF)
            scores = []
            for other in range(index + 1):
                keys = low_ref[1, pl.ds(place(other), shard), :]
                scores.append(
                    lax.dot_general(mine, keys, NT, preferred_element_type=F32)
                    + bias_ref[rows, other * shard : (other + 1) * shard]
                )
            largest = functools.reduce(
                jnp.maximum, [jnp.max(s, axis=1, keepdims=True) for s in scores]
            )
            total, acc = 0.0, 0.0
            for other in range(index + 1):
                lifted = jnp.exp(scores[other] - largest)
                total = total + jnp.sum(lifted, axis=1, keepdims=True)
                acc = acc + jnp.dot(
                    lifted.astype(BF),
                    low_ref[2, pl.ds(place(other), shard), :],
                    preferred_element_type=F32,
                )
            parts.append(acc / total)
            sums.append(largest + jnp.log(total))
        out_ref[pl.ds(place(index), shard), :] = jnp.where(lane < HD, parts[0], parts[1]).astype(BF)
        wide = jnp.where(lane == 0, sums[0], jnp.where(lane == 1, sums[1], 0.0))
        lse_ref[0, :, rows] = wide.T[:8, :]


def attend(me, segments, qkv):
    _, group, local_width = qkv.shape
    count = 4
    pairs = local_width // LANES

    def kernel(me_ref, column_ref, row_ref, qkv_ref, out_ref, lse_ref, bias_ref):
        attend_kernel(count, me_ref, column_ref, row_ref, qkv_ref, out_ref, lse_ref, bias_ref)

    return pl.pallas_call(
        kernel,
        grid_spec=pltpu.PrefetchScalarGridSpec(
            num_scalar_prefetch=1,
            grid=(pairs,),
            in_specs=[
                pl.BlockSpec((group, 1), lambda p, me: (0, 0)),
                pl.BlockSpec((1, group), lambda p, me: (0, 0)),
                pl.BlockSpec((3, group, LANES), lambda p, me: (0, 0, p)),
            ],
            out_specs=[
                pl.BlockSpec((group, LANES), lambda p, me: (0, p)),
                pl.BlockSpec((1, 8, group), lambda p, me: (p, 0, 0)),
            ],
            scratch_shapes=[pltpu.VMEM((group, group), F32)],
        ),
        out_shape=[
            jax.ShapeDtypeStruct((group, local_width), BF),
            jax.ShapeDtypeStruct((pairs, 8, group), F32),
        ],
        compiler_params=pltpu.CompilerParams(vmem_limit_bytes=MOST_VMEM_BYTES),
        cost_estimate=LIGHT,
    )(me, segments[:, None], segments[None, :], qkv)


def attend_back_kernel(
    count, me_ref, column_ref, row_ref, qkv_ref, out_ref, grad_ref, lse_ref, table_ref,
    raw_ref, bias_ref, key_grad_ref, value_grad_ref, key_turned_ref,
):
    me = me_ref[0]
    pair = pl.program_id(0)
    group = column_ref.shape[0]
    shard = group // count
    local_width = raw_ref.shape[1] // 3
    scale = jnp.asarray(HD**-0.5, BF)

    def place(index):
        return pl.multiple_of((index ^ me) * shard, shard)

    def target(part):
        return pl.ds(pl.multiple_of(part * local_width + pair * LANES, LANES), LANES)

    @pl.when(pair == 0)
    def _():
        for index in range(count):
            rows = slice(index * shard, group)
            keys = lax.broadcasted_iota(jnp.int32, (shard, group - index * shard), 0)
            queries = lax.broadcasted_iota(jnp.int32, (shard, group - index * shard), 1)
            own = slice(index * shard, (index + 1) * shard)
            allowed = (column_ref[own, :] == row_ref[:, rows]) & (keys <= queries)
            bias_ref[own, rows] = jnp.where(allowed, 0.0, -1e30)

    for index in range(count):
        rows = slice(index * shard, (index + 1) * shard)
        keys = qkv_ref[1, pl.ds(place(index), shard), :]
        key_turned_ref[:, rows] = keys.astype(F32).T.astype(BF)

    sub = lax.broadcasted_iota(jnp.int32, (8, LANES), 0)
    lane = lax.broadcasted_iota(jnp.int32, (8, LANES), 1)
    chooser = jnp.where((lane // HD) == sub, 1.0, 0.0)
    for index in range(count):
        rows = slice(index * shard, (index + 1) * shard)
        here = pl.ds(place(index), shard)
        query = qkv_ref[0, here, :]
        grad = grad_ref[here, :]
        product = grad.astype(F32) * out_ref[here, :].astype(F32)
        centres = lax.dot_general(
            chooser, product, NT, precision=lax.Precision.HIGHEST, preferred_element_type=F32
        )
        turned = []
        for head in range(2):
            chosen = head_lanes(query.shape, head)
            mine = jnp.where(chosen, query, 0) * scale
            grad_mine = jnp.where(chosen, grad, 0)
            lse = lse_ref[0, head : head + 1, rows]
            centre = centres[head : head + 1, :]
            query_turned = 0.0
            for other in range(index + 1):
                there = pl.ds(place(other), shard)
                span = slice(other * shard, (other + 1) * shard)
                scores = lax.dot_general(
                    qkv_ref[1, there, :], mine, NT, preferred_element_type=F32
                )
                probs = jnp.exp(scores + bias_ref[span, rows] - lse)
                prob_grad = lax.dot_general(
                    qkv_ref[2, there, :], grad_mine, NT, preferred_element_type=F32
                )
                cot = (probs * (prob_grad - centre)).astype(BF)
                value_add = jnp.dot(probs.astype(BF), grad_mine, preferred_element_type=F32)
                key_add = jnp.dot(cot, mine, preferred_element_type=F32)
                if other == index and head == 0:
                    value_grad_ref[span, :] = value_add
                    key_grad_ref[span, :] = key_add
                else:
                    value_grad_ref[span, :] += value_add
                    key_grad_ref[span, :] += key_add
                query_turned = query_turned + jnp.dot(
                    key_turned_ref[head * HD : (head + 1) * HD, span],
                    cot,
                    preferred_element_type=F32,
                )
            turned.append(query_turned)
        query_grad = jnp.concatenate(turned, axis=0).T * HD**-0.5
        raw_ref[here, target(0)] = turn(query_grad, table_ref, here, -1.0).astype(BF)
    for index in range(count):
        rows = slice(index * shard, (index + 1) * shard)
        here = pl.ds(place(index), shard)
        raw_ref[here, target(1)] = turn(key_grad_ref[rows, :], table_ref, here, -1.0).astype(BF)
        raw_ref[here, target(2)] = value_grad_ref[rows, :].astype(BF)


def attend_back(me, segments, qkv, attended, grad, lse, table):
    _, group, local_width = qkv.shape
    count = 4
    pairs = local_width // LANES
    return pl.pallas_call(
        functools.partial(attend_back_kernel, count),
        grid_spec=pltpu.PrefetchScalarGridSpec(
            num_scalar_prefetch=1,
            grid=(pairs,),
            in_specs=[
                pl.BlockSpec((group, 1), lambda p, me: (0, 0)),
                pl.BlockSpec((1, group), lambda p, me: (0, 0)),
                pl.BlockSpec((3, group, LANES), lambda p, me: (0, 0, p)),
                pl.BlockSpec((group, LANES), lambda p, me: (0, p)),
                pl.BlockSpec((group, LANES), lambda p, me: (0, p)),
                pl.BlockSpec((1, 8, group), lambda p, me: (p, 0, 0)),
                pl.BlockSpec((3, group, LANES), lambda p, me: (0, 0, 0)),
            ],
            out_specs=pl.BlockSpec((group, 3 * local_width), lambda p, me: (0, 0)),
            scratch_shapes=[
                pltpu.VMEM((group, group), F32),
                pltpu.VMEM((group, LANES), F32),
                pltpu.VMEM((group, LANES), F32),
                pltpu.VMEM((LANES, group), BF),
            ],
        ),
        out_shape=jax.ShapeDtypeStruct((group, 3 * local_width), BF),
        compiler_params=pltpu.CompilerParams(vmem_limit_bytes=VMEM_BYTES),
        cost_estimate=LIGHT,
    )(me, segments[:, None], segments[None, :], qkv, attended, grad, lse, table)


def weight_grad(blocks, pieces, cots, part, parts, splits):
    many = blocks.shape[0]
    shard, width = pieces[0].shape
    tokens = cots.shape[0]
    units = cots.shape[1] // parts
    depth = width // (2 * many)
    share = depth // splits
    if depth % LANES:
        rows = jnp.concatenate(pieces, 0)
        columns = [
            lax.dynamic_slice_in_dim(rows, blocks[index] * depth, depth, 1) for index in range(many)
        ]
        products = lax.dot_general(
            jnp.concatenate(columns, 1),
            cots[:, part * units : (part + 1) * units],
            TN,
            preferred_element_type=F32,
        ).astype(BF)
        products = products.reshape(many, splits, share, units)
        return [products[:, index].reshape(many * share, units) for index in range(splits)]

    def kernel(blocks_ref, *refs):
        piece_refs, cots_ref, out_refs, rows_ref = refs[:4], refs[4], refs[5:-1], refs[-1]
        for index, piece_ref in enumerate(piece_refs):
            rows_ref[index * shard : (index + 1) * shard, :] = piece_ref[...]
        product = lax.dot_general(
            rows_ref[...], cots_ref[...], TN, preferred_element_type=F32
        ).astype(BF)
        for index, out_ref in enumerate(out_refs):
            out_ref[...] = product[index * share : (index + 1) * share]

    return pl.pallas_call(
        kernel,
        grid_spec=pltpu.PrefetchScalarGridSpec(
            num_scalar_prefetch=1,
            grid=(many,),
            in_specs=[pl.BlockSpec((shard, depth), lambda i, blocks: (0, blocks[i]))] * 4
            + [pl.BlockSpec((tokens, units), lambda i, blocks: (0, part))],
            out_specs=[pl.BlockSpec((share, units), lambda i, blocks: (i, 0))] * splits,
            scratch_shapes=[pltpu.VMEM((tokens, depth), BF)],
        ),
        out_shape=[jax.ShapeDtypeStruct((many * share, units), BF)] * splits,
        compiler_params=pltpu.CompilerParams(vmem_limit_bytes=VMEM_BYTES),
        cost_estimate=pl.CostEstimate(
            flops=2 * many * depth * tokens * units,
            bytes_accessed=2 * (tokens * units + many * depth * (tokens + units)),
            transcendentals=0,
        ),
    )(blocks, *pieces, cots)


def ring_add(entries, finals):
    shape = entries[0][0][2]
    counts = [len(entry) for entry in entries]
    sends = sum(final is None for final in finals)

    def kernel(*refs):
        out_refs = list(refs[sum(counts) :])
        start, sent = 0, 0
        for count, final in zip(counts, finals):
            total = functools.reduce(
                jnp.add, [ref[...].astype(F32) for ref in refs[start : start + count]]
            )
            start += count
            if final is None:
                out_refs[0][sent * shape[0] : (sent + 1) * shape[0], :] = total.astype(BF)
                sent += 1
            else:
                out_refs.pop(1 if sends else 0)[...] = total.astype(final)

    def spec(block):
        return pl.BlockSpec(shape, lambda i: (block, 0))

    outs = [jax.ShapeDtypeStruct((sends * shape[0], shape[1]), BF)] if sends else []
    outs += [jax.ShapeDtypeStruct(shape, final) for final in finals if final is not None]
    return pl.pallas_call(
        kernel,
        grid=(1,),
        in_specs=[spec(block) for entry in entries for _, block, _ in entry],
        out_specs=[pl.BlockSpec(o.shape, lambda i: (0, 0)) for o in outs],
        out_shape=outs,
        compiler_params=pltpu.CompilerParams(vmem_limit_bytes=VMEM_BYTES),
        cost_estimate=LIGHT,
    )(*[array for entry in entries for array, _, _ in entry])


def barrier(value, *others):
    return lax.optimization_barrier((value, *others))[0]


class Order:
    def __init__(self):
        self.last = None

    def __call__(self, step, operand, *others, wait=()):
        if self.last is not None:
            operand = barrier(operand, self.last, *wait)
        result = step(operand, *others)
        self.last = jax.tree.leaves(result)[0]
        return result


class Reducer:
    def __init__(self, order, rounds, partner, along):
        self.order, self.rounds, self.partner, self.along = order, rounds, partner, along
        self.flying, self.rings = [], []
        self.popped = None
        self.kept, self.done, self.late = {}, {}, []

    def send(self, name, sent, kept=None):
        if self.popped is not None:
            sent = barrier(sent, self.popped)
        if kept is not None:
            self.kept[name] = kept
        self.flying.append((name, self.partner(sent)))

    def ring(self, name, kept, other):
        self._enter(name, [kept], F32)
        self._enter(name + "/other", [other], BF)

    def _enter(self, name, arrays, final):
        shape = (arrays[0].shape[0] // self.rounds, arrays[0].shape[1])
        self.rings.append(
            dict(name=name, arrays=arrays, shape=shape, step=0, carry=[], final=final)
        )

    def turn(self, pop=True):
        if pop and self.flying:
            name, got = self.flying.pop(0)
            self.popped = got
            self._enter(name, [self.kept.pop(name), got], F32)
        late, self.late = self.late, []
        for name, got in late:
            self.done[name] = self.order(lambda a, n=name: self.done[n] + a.astype(F32), got)
        rings, self.rings = self.rings, []
        for shape in dict.fromkeys(ring["shape"] for ring in rings):
            self._move([ring for ring in rings if ring["shape"] == shape], shape)

    def _move(self, rings, shape):
        entries = [
            [(array, r["step"], shape) for array in r["arrays"]] + r["carry"] for r in rings
        ]
        ends = [r["step"] == self.rounds - 1 for r in rings]
        finals = [r["final"] if end else None for r, end in zip(rings, ends)]

        def step(first):
            entries[0][0] = (first,) + entries[0][0][1:]
            return ring_add(entries, finals)

        outs = list(self.order(step, entries[0][0][0]))
        if not all(ends):
            message = self.along(outs.pop(0))
        sent = 0
        for ring, end in zip(rings, ends):
            if end:
                self._finish(ring["name"], outs.pop(0))
            else:
                ring["carry"] = [(message, sent, shape)]
                ring["step"] += 1
                sent += 1
                self.rings.append(ring)

    def _finish(self, name, result):
        if name.endswith("/other"):
            self.late.append((name.split("/")[0], self.partner(result)))
        else:
            self.done[name] = result

    def busy(self):
        return bool(self.flying or self.rings or self.late)


def local(
    n_dp,
    tokens,
    segment_ids,
    cotangent,
    w_qkv,
    qkv_bias,
    w_out,
    w_gate_up,
    w_down,
    norm_gains,
    norm_biases,
):
    shard, width = tokens.shape
    group = segment_ids.shape[0]
    local_width = w_out.shape[0]
    units = w_down.shape[0]
    n_tensor = group // shard
    n_ring = n_dp // 2
    me = lax.axis_index("tensor")
    data_index = lax.axis_index("dp")
    to_core = [(t, t ^ 1) for t in range(n_tensor)]
    to_x = [(t, t ^ 2) for t in range(n_tensor)]
    to_y = [(d, d ^ 1) for d in range(n_dp)]
    up_z = [(d, (d + 2) % n_dp) for d in range(n_dp)]
    order = Order()

    def core(value):
        return lax.ppermute(value, "tensor", to_core)

    def across(value):
        return lax.ppermute(value, "tensor", to_x)

    def over_dp(value, step):
        return lax.ppermute(value, "dp", [(d, d ^ (1 << step)) for d in range(n_dp)])

    dp_steps = (n_dp - 1).bit_length()

    def in_pieces(values):
        blocks = values.reshape((n_tensor, shard) + values.shape[1:])
        return jnp.concatenate(
            [lax.dynamic_index_in_dim(blocks, me ^ k, 0, False) for k in range(n_tensor)], 0
        )

    def add(first, second):
        return (first.astype(F32) + second.astype(F32)).astype(BF)

    def stack(*pieces):
        return jnp.concatenate(pieces, 0)

    def rows_of(half, rows, w, dims):
        return order(lambda r, *more: pair_product(half, (r, *more), w, dims), *rows)

    def send_far(mine, other):
        return across(order(add, core(other), mine))

    ring_index = data_index // 2
    rings = jnp.stack([(ring_index - 1 - s + 2 * n_ring) % n_ring for s in range(n_ring)])
    keep_blocks = (2 * rings + data_index % 2).astype(jnp.int32)
    send_blocks = (2 * rings + 1 - data_index % 2).astype(jnp.int32)

    def grad_of(blocks, cots, pieces, part=0, parts=1, splits=1):
        return order(lambda c: weight_grad(blocks, pieces, c, part, parts, splits), cots)

    reducer = Reducer(
        order,
        n_ring,
        lambda value: lax.ppermute(value, "dp", to_y),
        lambda value: lax.ppermute(value, "dp", up_z),
    )

    me_one = me[None].astype(jnp.int32)
    gains = [norm_gains[index : index + 1] for index in range(2)]
    shifts = [norm_biases[index : index + 1] for index in range(2)]
    live = (segment_ids >= 0).astype(F32)
    live_rows = lax.dynamic_slice_in_dim(live, me * shard, shard, 0)

    one_own = order(norm_rows, tokens, gains[0], shifts[0])
    one_far = across(one_own)
    one_near = core(one_own)
    out_cot = (cotangent.astype(F32) * live_rows[:, None]).astype(BF)
    in_near = core(out_cot)
    live_total = jnp.sum(live)[None]
    table = rope_tables(in_pieces(positions_of(segment_ids)))
    w_flat = w_gate_up.reshape(width, 2 * units)
    w_split = jnp.transpose(w_qkv, (1, 0, 2))
    bias_rows = qkv_bias[:, None, :]
    qkv = order(
        lambda a: project(0, a, one_near, w_split, bias_rows, table, None),
        one_own, wait=(w_flat, table),
    )
    one_far = barrier(one_far, qkv)
    one_last = core(one_far)
    in_far = across(barrier(out_cot, one_far))
    qkv = order(
        lambda a: project(1, a, one_last, w_split, bias_rows, table, qkv), one_far
    )
    attended, lse = order(lambda q: attend(me_one, segment_ids, q), qkv)
    branch_far = send_far(*rows_of(1, (attended,), w_out, NN))
    near0, near1 = rows_of(0, (attended,), w_out, NN)
    in_last = core(in_far)
    incoming = (out_cot, in_near, in_far, in_last)
    incoming_full = order(stack, *incoming)
    act_grad = order(
        lambda r: lax.dot_general(r, w_down, NT, preferred_element_type=F32), incoming_full
    )
    hidden, two_own = order(
        lambda t, *a: add_norm_rows(t, *a, gains[1], shifts[1]),
        tokens, near0, core(near1), branch_far,
    )
    two_far = across(two_own)
    two_near = core(two_own)
    fed = order(lambda a: feed(0, a, two_near, w_flat, act_grad, None), two_own)
    two_far = barrier(two_far, fed[0])
    two_last = core(two_far)
    activated, gate_cot, up_cot = order(
        lambda a: feed(1, a, two_last, w_flat, act_grad, fed), two_far
    )
    two = (two_own, two_near, two_far, two_last)
    one = (one_own, one_near, one_far, one_last)
    wide = dict(splits=2)

    down_sent = grad_of(send_blocks, activated, incoming, **wide)
    reducer.send("down1", down_sent[1])
    down_kept = grad_of(keep_blocks, activated, incoming, **wide)
    reducer.kept["down1"] = down_kept[1]
    reducer.ring("down0", down_kept[0], down_sent[0])
    reducer.turn(pop=False)
    second_pair = rows_of(1, (gate_cot, up_cot), w_flat, NT)
    gate_sent = grad_of(send_blocks, gate_cot, two, **wide)

    reducer.turn()
    second_far = send_far(*second_pair)
    reducer.send("gate0", gate_sent[0])
    near0, near1 = rows_of(0, (gate_cot, up_cot), w_flat, NT)
    gate_kept = grad_of(keep_blocks, gate_cot, two, **wide)
    reducer.kept["gate0"] = gate_kept[0]

    reducer.turn()
    reducer.send("gate1", gate_sent[1], gate_kept[1])
    hidden_grad, branch_own, sums_two = order(
        lambda h, *a: norm_rows_back(h, *a, gains[1], (F32, BF)),
        hidden, near0, core(near1), second_far, out_cot,
    )
    branch_far = across(branch_own)
    branch_near = core(branch_own)
    up_sent = grad_of(send_blocks, up_cot, two, **wide)
    up_kept = grad_of(keep_blocks, up_cot, two, **wide)

    branch_far = barrier(branch_far, order.last)
    branch_last = core(branch_far)
    reducer.turn()
    reducer.send("up0", up_sent[0], up_kept[0])
    branch = (branch_own, branch_near, branch_far, branch_last)
    branch_full = order(stack, *branch)
    attended_grad = order(
        lambda r: lax.dot_general(r, w_out, NT, preferred_element_type=F32).astype(BF),
        branch_full,
    )
    raw_cot = order(
        lambda g: attend_back(me_one, segment_ids, qkv, attended, g, lse, table), attended_grad
    )

    reducer.turn()
    reducer.send("up1", up_sent[1], up_kept[1])
    first_pair = rows_of(1, (raw_cot,), w_split, NT)
    near0, near1 = rows_of(0, (raw_cot,), w_split, NT)
    (out_sent,) = grad_of(send_blocks, attended, branch)
    (reducer.kept["out"],) = grad_of(keep_blocks, attended, branch)

    reducer.turn()
    first_far = send_far(*first_pair)
    reducer.send("out", out_sent)
    value_sent, value_kept = [
        grad_of(blocks, raw_cot, one, 2, 3)[0] for blocks in (send_blocks, keep_blocks)
    ]
    (query_sent,) = grad_of(send_blocks, raw_cot, one, 0, 3)

    reducer.ring("value", value_kept, value_sent)
    reducer.turn()
    reducer.send("query", query_sent)
    input_grad, sums_one = order(
        lambda t, *a: norm_rows_back(t, *a, gains[0], (F32,)),
        tokens, near0, core(near1), first_far, hidden_grad,
    )
    (reducer.kept["query"],) = grad_of(keep_blocks, raw_cot, one, 0, 3)
    (key_sent,) = grad_of(send_blocks, raw_cot, one, 1, 3)
    down_pair = rows_of(1, (activated,), w_down, NN)

    reducer.turn()
    rows_sum = jnp.concatenate([sums_one[:1], sums_two[:1], sums_one[1:], sums_two[1:]], 0)
    rows_sum = order(jnp.add, core(rows_sum), rows_sum)
    rows_far = across(rows_sum)
    down_far = send_far(*down_pair)
    reducer.send("key", key_sent)
    (reducer.kept["key"],) = grad_of(keep_blocks, raw_cot, one, 1, 3)
    near0, near1 = rows_of(0, (activated,), w_down, NN)
    bias_sum = order(lambda r: jnp.sum(r.astype(F32), axis=0).reshape(3, local_width), raw_cot)

    rows_sum = order(jnp.add, rows_far, rows_sum)
    small = jnp.concatenate([rows_sum.reshape(-1), bias_sum.reshape(-1), live_total])
    for step in range(dp_steps):
        reducer.turn()
        if step == 0:
            output = order(
                lambda h, a, b, c: (
                    h + (a.astype(F32) + b.astype(F32) + c.astype(F32))
                ).astype(BF),
                hidden, near0, core(near1), down_far,
            )
        small = order(jnp.add, over_dp(small, step), small)
    live_total = small[-1]
    small = small[:-1] / live_total
    rows_sum = small[: 4 * width].reshape(4, width)
    bias_sum = small[4 * width :].reshape(3, local_width)

    def whole(name):
        return jnp.concatenate([reducer.done[name + "0"], reducer.done[name + "1"]], 0) / live_total

    while reducer.busy():
        reducer.turn()
    down_sum = whole("down").T
    gate_up_sum = jnp.stack([whole("gate"), whole("up")], 1)
    qkv_sum = jnp.stack([reducer.done[name] for name in ("query", "key", "value")], 1)
    return (
        output,
        input_grad,
        qkv_sum / live_total,
        bias_sum,
        reducer.done["out"].T / live_total,
        gate_up_sum,
        down_sum,
        rows_sum[:2],
        rows_sum[2:],
    )


def solution(mesh):
    in_specs = (
        P(("dp", "tensor"), None),
        P("dp"),
        P(("dp", "tensor"), None),
        P(None, None, "tensor"),
        P(None, "tensor"),
        P("tensor", None),
        P(None, None, "tensor"),
        P("tensor", None),
        P(),
        P(),
    )
    out_specs = (
        P(("dp", "tensor"), None),
        P(("dp", "tensor"), None),
        P("dp", None, "tensor"),
        P(None, "tensor"),
        P("tensor", "dp"),
        P("dp", None, "tensor"),
        P("tensor", "dp"),
        P(),
        P(),
    )
    return jax.shard_map(
        functools.partial(local, mesh.shape["dp"]),
        mesh=mesh,
        in_specs=in_specs,
        out_specs=out_specs,
        check_vma=False,
    )
```

```python
import functools

import jax
import jax.numpy as jnp
from jax import lax
from jax.experimental import pallas as pl
from jax.experimental.pallas import tpu as pltpu
from jax.sharding import PartitionSpec as P

HD = 64
ROT = 16
LANES = 128
epsilon = 1e-05
rope_base = 10000.0
BF = jnp.bfloat16
F32 = jnp.float32
MIB = 1 << 20
GROUP_BYTES = 2_200_000
LIGHT = pl.CostEstimate(flops=1, bytes_accessed=1, transcendentals=0)
NT = (((1,), (1,)), ((), ()))
TN = (((0,), (0,)), ((), ()))
NN = (((1,), (0,)), ((), ()))


def positions_of(segments):
    row_index = jnp.arange(segments.shape[0], dtype=jnp.int32)
    previous = jnp.concatenate([jnp.full((1,), -2, jnp.int32), segments[:-1]])
    starts = jnp.where(segments != previous, row_index, 0)
    return row_index - lax.cummax(starts, axis=0)


def rope_tables(positions):
    half = ROT // 2
    dim = jnp.arange(LANES) % HD
    exponent = (dim % half).astype(F32) * 2.0 / ROT
    frequency = jnp.where(dim < ROT, rope_base ** (-exponent), 0.0)
    angles = positions.astype(F32)[:, None] * frequency[None, :]
    cosine, sine = jnp.cos(angles), jnp.sin(angles)
    lower = jnp.where(dim < half, -sine, 0.0)
    upper = jnp.where((dim >= half) & (dim < ROT), sine, 0.0)
    return jnp.stack([cosine, lower, upper])


def turn(block, table_ref, rows, sign):
    half = ROT // 2
    back = pltpu.roll(block, LANES - half, 1)
    ahead = pltpu.roll(block, half, 1)
    return (
        block * table_ref[0, rows, :]
        + sign * (back * table_ref[1, rows, :] + ahead * table_ref[2, rows, :])
    )


def project_kernel(
    first_ref, second_ref, w_ref, bias_ref, table_ref, old_ref, out_ref, rows_ref
):
    shard = first_ref.shape[0]

    @pl.when(pl.program_id(0) == 0)
    def _():
        rows_ref[:shard, :] = first_ref[...]
        rows_ref[shard:, :] = second_ref[...]

    raw = jnp.dot(rows_ref[...], w_ref[0], preferred_element_type=F32) + bias_ref[0]

    @pl.when(pl.program_id(0) < 2)
    def _():
        for start in range(0, raw.shape[1], LANES):
            piece = turn(raw[:, start : start + LANES], table_ref, slice(None), 1.0)
            out_ref[0, :, start : start + LANES] = piece.astype(BF)

    @pl.when(pl.program_id(0) == 2)
    def _():
        out_ref[0] = raw.astype(BF)


def project(half, first, second, w, bias, table, old):
    shard, width = first.shape
    local_width = w.shape[2]
    whole = jax.ShapeDtypeStruct((3, 4 * shard, local_width), BF)
    kernel = project_kernel
    operands = [first, second, w, bias, table]
    specs = [
        pl.BlockSpec((shard, width), lambda c: (0, 0)),
        pl.BlockSpec((shard, width), lambda c: (0, 0)),
        pl.BlockSpec((1, width, local_width), lambda c: (c, 0, 0)),
        pl.BlockSpec((1, 1, local_width), lambda c: (c, 0, 0)),
        pl.BlockSpec((3, 2 * shard, LANES), lambda c: (0, half, 0)),
    ]
    aliases = {}
    if old is None:

        def kernel(a, b, c, d, e, out_ref, rows_ref):
            project_kernel(a, b, c, d, e, None, out_ref, rows_ref)

    else:
        operands.append(old)
        specs.append(pl.BlockSpec(memory_space=pl.ANY))
        aliases = {5: 0}
    return pl.pallas_call(
        kernel,
        name="project",
        grid=(3,),
        in_specs=specs,
        out_specs=pl.BlockSpec((1, 2 * shard, local_width), lambda c: (c, half, 0)),
        out_shape=whole,
        input_output_aliases=aliases,
        scratch_shapes=[pltpu.VMEM((2 * shard, width), BF)],
        compiler_params=pltpu.CompilerParams(vmem_limit_bytes=48 * MIB),
        cost_estimate=LIGHT,
    )(*operands)


def feed_kernel(
    first_ref, second_ref, w0_ref, w1_ref, w2_ref, w3_ref, act_grad_ref,
    act_ref, gate_ref, up_ref, rows_ref, w_ref,
):
    shard = first_ref.shape[0]

    @pl.when(pl.program_id(0) == 0)
    def _():
        rows_ref[:shard, :] = first_ref[...]
        rows_ref[shard:, :] = second_ref[...]

    for index, part_ref in enumerate((w0_ref, w1_ref, w2_ref, w3_ref)):
        w_ref[:, index * LANES : (index + 1) * LANES] = part_ref[...]
    products = [
        jnp.dot(
            rows_ref[...],
            w_ref[:, 2 * index * LANES : 2 * (index + 1) * LANES],
            preferred_element_type=F32,
        )
        for index in range(2)
    ]
    for index, product in enumerate(products):
        lanes = slice(index * LANES, (index + 1) * LANES)
        gate, up = product[:, :LANES], product[:, LANES:]
        s = jax.nn.sigmoid(gate)
        silu = gate * s
        act_grad = act_grad_ref[:, lanes].astype(F32)
        act_ref[:, lanes] = (silu * up).astype(BF)
        gate_ref[:, lanes] = (act_grad * up * (s + silu * (1.0 - s))).astype(BF)
        up_ref[:, lanes] = (act_grad * silu).astype(BF)


def feed(half, first, second, w, act_grad, old):
    shard, width = first.shape
    units = w.shape[1] // 2
    tiles = units // LANES

    def tile(base, index):
        return pl.BlockSpec(
            (width, LANES), lambda j: (0, base + jnp.minimum(2 * j + index, tiles - 1))
        )

    operands = [first, second, w, w, w, w, act_grad]
    specs = [
        pl.BlockSpec((shard, width), lambda j: (0, 0)),
        pl.BlockSpec((shard, width), lambda j: (0, 0)),
        tile(0, 0),
        tile(tiles, 0),
        tile(0, 1),
        tile(tiles, 1),
        pl.BlockSpec((2 * shard, 2 * LANES), lambda j: (half, j)),
    ]
    kernel = feed_kernel
    aliases = {}
    if old is not None:

        def kernel(*refs):
            feed_kernel(*refs[:7], *refs[10:])

        operands += list(old)
        specs += [pl.BlockSpec(memory_space=pl.ANY)] * 3
        aliases = {7: 0, 8: 1, 9: 2}
    return pl.pallas_call(
        kernel,
        name="feed",
        grid=(pl.cdiv(tiles, 2),),
        in_specs=specs,
        out_specs=[pl.BlockSpec((2 * shard, 2 * LANES), lambda j: (half, j))] * 3,
        out_shape=[jax.ShapeDtypeStruct((4 * shard, units), BF)] * 3,
        input_output_aliases=aliases,
        scratch_shapes=[pltpu.VMEM((2 * shard, width), BF), pltpu.VMEM((width, 4 * LANES), BF)],
        compiler_params=pltpu.CompilerParams(vmem_limit_bytes=60 * MIB),
        cost_estimate=LIGHT,
    )(*operands)


def pair_product(half, rows, w, dims):
    group = rows[0].shape[0]
    shard = group // 4
    depth = sum(r.shape[1] for r in rows)
    turned = dims is NT
    width = w.shape[-2] if turned else w.shape[-1]
    tile = min(512, width)
    if w.ndim == 3:
        w_spec = pl.BlockSpec((w.shape[0], tile, w.shape[2]), lambda j: (0, j, 0))
    elif turned:
        w_spec = pl.BlockSpec((tile, depth), lambda j: (j, 0))
    else:
        w_spec = pl.BlockSpec((depth, tile), lambda j: (0, j))

    def kernel(*refs):
        rows_refs, w_ref = refs[: len(rows)], refs[len(rows)]
        first_ref, second_ref = refs[len(rows) + 1 :]
        if w.ndim == 3:
            part = w.shape[2]
            product = sum(
                lax.dot_general(
                    rows_refs[0][:, c * part : (c + 1) * part],
                    w_ref[c],
                    dims,
                    preferred_element_type=F32,
                )
                for c in range(w.shape[0])
            )
        elif turned:
            product, start = 0.0, 0
            for rows_ref in rows_refs:
                end = start + rows_ref.shape[1]
                product = product + lax.dot_general(
                    rows_ref[...], w_ref[:, start:end], dims, preferred_element_type=F32
                )
                start = end
        else:
            product = lax.dot_general(
                rows_refs[0][...], w_ref[...], dims, preferred_element_type=F32
            )
        product = product.astype(BF)
        first_ref[...] = product[:shard]
        second_ref[...] = product[shard:]

    return pl.pallas_call(
        kernel,
        name="pair_product",
        grid=(width // tile,),
        in_specs=[pl.BlockSpec((2 * shard, r.shape[1]), lambda j: (half, 0)) for r in rows]
        + [w_spec],
        out_specs=[pl.BlockSpec((shard, tile), lambda j: (0, j))] * 2,
        out_shape=[jax.ShapeDtypeStruct((shard, width), BF)] * 2,
        compiler_params=pltpu.CompilerParams(vmem_limit_bytes=48 * MIB),
        cost_estimate=LIGHT,
    )(*rows, w)


def centre_rows(values):
    average = jnp.mean(values, axis=-1, keepdims=True)
    centered = values - average
    variance = jnp.mean(centered * centered, axis=-1, keepdims=True)
    spread = lax.rsqrt(variance + epsilon)
    return centered * spread, spread


ROW_STEP = 64


def row_call(kernel, shard, width, inputs, per_row, outs):
    step = min(ROW_STEP, shard)
    specs = [
        pl.BlockSpec((step, a.shape[1]), lambda i: (i, 0))
        if rowwise
        else pl.BlockSpec(a.shape, lambda i: (0, 0))
        for a, rowwise in zip(inputs, per_row)
    ]
    out_specs = [
        pl.BlockSpec((step, width), lambda i: (i, 0))
        if o.shape[0] == shard
        else pl.BlockSpec(o.shape, lambda i: (0, 0))
        for o in outs
    ]
    return pl.pallas_call(
        kernel,
        name="row_call",
        grid=(shard // step,),
        in_specs=specs,
        out_specs=out_specs,
        out_shape=outs,
        compiler_params=pltpu.CompilerParams(vmem_limit_bytes=48 * MIB),
        cost_estimate=LIGHT,
    )(*inputs)


def norm_rows(tokens, gain, shift):
    def kernel(tokens_ref, gain_ref, shift_ref, out_ref):
        hat, _ = centre_rows(tokens_ref[...].astype(F32))
        out_ref[...] = (hat * gain_ref[...] + shift_ref[...]).astype(BF)

    shard, width = tokens.shape
    return row_call(
        kernel, shard, width, (tokens, gain, shift), (1, 0, 0),
        [jax.ShapeDtypeStruct((shard, width), BF)],
    )[0]


def total_of(own_ref, far_ref, tile_refs):
    tiles = jnp.concatenate([ref[...].astype(F32) for ref in tile_refs], axis=1)
    return own_ref[...].astype(F32) + tiles + far_ref[...].astype(F32)


def add_tiles(own, tiles):
    def kernel(own_ref, *refs):
        *tile_refs, out_ref = refs
        tiles = jnp.concatenate([ref[...].astype(F32) for ref in tile_refs], axis=1)
        out_ref[...] = (own_ref[...].astype(F32) + tiles).astype(BF)

    return row_call(
        kernel, *own.shape, (own, *tiles), (1,) * (1 + len(tiles)),
        [jax.ShapeDtypeStruct(own.shape, BF)],
    )[0]


def add_rows(values, own, far, tiles):
    def kernel(values_ref, own_ref, far_ref, *refs):
        *tile_refs, out_ref = refs
        total = values_ref[...] + total_of(own_ref, far_ref, tile_refs)
        out_ref[...] = total.astype(BF)

    return row_call(
        kernel, *own.shape, (values, own, far, *tiles), (1,) * (3 + len(tiles)),
        [jax.ShapeDtypeStruct(own.shape, BF)],
    )[0]


def add_norm_rows(tokens, own, far, tiles, gain, shift):
    def kernel(tokens_ref, own_ref, far_ref, gain_ref, shift_ref, *refs):
        *tile_refs, hidden_ref, out_ref = refs
        hidden = tokens_ref[...].astype(F32) + total_of(own_ref, far_ref, tile_refs)
        hidden_ref[...] = hidden
        hat, _ = centre_rows(hidden)
        out_ref[...] = (hat * gain_ref[...] + shift_ref[...]).astype(BF)

    shard, width = tokens.shape
    return row_call(
        kernel, shard, width, (tokens, own, far, gain, shift, *tiles),
        (1, 1, 1, 0, 0) + (1,) * len(tiles),
        [jax.ShapeDtypeStruct((shard, width), F32), jax.ShapeDtypeStruct((shard, width), BF)],
    )


def norm_rows_back(values, own, far, tiles, base, gain, dtypes):
    def kernel(values_ref, own_ref, far_ref, base_ref, gain_ref, *refs):
        tile_refs, grad_refs, sums_ref = refs[: len(tiles)], refs[len(tiles) : -1], refs[-1]
        hat, spread = centre_rows(values_ref[...].astype(F32))
        grad = total_of(own_ref, far_ref, tile_refs)
        scaled = grad * gain_ref[...]
        mean_scaled = jnp.mean(scaled, axis=-1, keepdims=True)
        mean_hat = jnp.mean(scaled * hat, axis=-1, keepdims=True)
        result = base_ref[...].astype(F32) + spread * (scaled - mean_scaled - hat * mean_hat)
        for ref in grad_refs:
            ref[...] = result.astype(ref.dtype)
        sums = jnp.concatenate(
            [
                jnp.sum(grad * hat, axis=0, keepdims=True),
                jnp.sum(grad, axis=0, keepdims=True),
            ],
            0,
        )

        @pl.when(pl.program_id(0) == 0)
        def _():
            sums_ref[...] = sums

        @pl.when(pl.program_id(0) > 0)
        def _():
            sums_ref[...] += sums

    shard, width = values.shape
    return row_call(
        kernel, shard, width, (values, own, far, base, gain, *tiles),
        (1, 1, 1, 1, 0) + (1,) * len(tiles),
        [jax.ShapeDtypeStruct((shard, width), d) for d in dtypes]
        + [jax.ShapeDtypeStruct((2, width), F32)],
    )


def head_lanes(shape, head):
    lane = lax.broadcasted_iota(jnp.int32, shape, 1)
    return (lane < HD) if head == 0 else (lane >= HD)


def attend_kernel(count, me_ref, column_ref, row_ref, low_ref, out_ref, lse_ref, bias_ref):
    me = me_ref[0]
    shard = column_ref.shape[0] // count

    def place(index):
        return pl.multiple_of((index ^ me) * shard, shard)

    @pl.when(pl.program_id(0) == 0)
    def _():
        for index in range(count):
            span = (index + 1) * shard
            rows = slice(index * shard, span)
            own = lax.broadcasted_iota(jnp.int32, (shard, span), 0) + index * shard
            other = lax.broadcasted_iota(jnp.int32, (shard, span), 1)
            allowed = (column_ref[rows, :] == row_ref[:, :span]) & (other <= own)
            bias_ref[rows, :span] = jnp.where(allowed, 0.0, -1e30)

    lane = lax.broadcasted_iota(jnp.int32, (shard, LANES), 1)
    for index in range(count):
        rows = slice(index * shard, (index + 1) * shard)
        query = low_ref[0, pl.ds(place(index), shard), :]
        parts, sums = [], []
        for head in range(2):
            mine = jnp.where(head_lanes(query.shape, head), query, 0) * jnp.asarray(HD**-0.5, BF)
            scores = []
            for other in range(index + 1):
                keys = low_ref[1, pl.ds(place(other), shard), :]
                scores.append(
                    lax.dot_general(mine, keys, NT, preferred_element_type=F32)
                    + bias_ref[rows, other * shard : (other + 1) * shard]
                )
            largest = functools.reduce(
                jnp.maximum, [jnp.max(s, axis=1, keepdims=True) for s in scores]
            )
            total, acc = 0.0, 0.0
            for other in range(index + 1):
                lifted = jnp.exp(scores[other] - largest)
                total = total + jnp.sum(lifted, axis=1, keepdims=True)
                acc = acc + jnp.dot(
                    lifted.astype(BF),
                    low_ref[2, pl.ds(place(other), shard), :],
                    preferred_element_type=F32,
                )
            parts.append(acc / total)
            sums.append(largest + jnp.log(total))
        out_ref[pl.ds(place(index), shard), :] = jnp.where(lane < HD, parts[0], parts[1]).astype(BF)
        wide = jnp.where(lane == 0, sums[0], jnp.where(lane == 1, sums[1], 0.0))
        lse_ref[0, :, rows] = wide.T[:8, :]


def attend(me, segments, qkv):
    _, group, local_width = qkv.shape
    count = 4
    pairs = local_width // LANES

    def kernel(me_ref, column_ref, row_ref, qkv_ref, out_ref, lse_ref, bias_ref):
        attend_kernel(count, me_ref, column_ref, row_ref, qkv_ref, out_ref, lse_ref, bias_ref)

    return pl.pallas_call(
        kernel,
        name="attend",
        grid_spec=pltpu.PrefetchScalarGridSpec(
            num_scalar_prefetch=1,
            grid=(pairs,),
            in_specs=[
                pl.BlockSpec((group, 1), lambda p, me: (0, 0)),
                pl.BlockSpec((1, group), lambda p, me: (0, 0)),
                pl.BlockSpec((3, group, LANES), lambda p, me: (0, 0, p)),
            ],
            out_specs=[
                pl.BlockSpec((group, LANES), lambda p, me: (0, p)),
                pl.BlockSpec((1, 8, group), lambda p, me: (p, 0, 0)),
            ],
            scratch_shapes=[pltpu.VMEM((group, group), F32)],
        ),
        out_shape=[
            jax.ShapeDtypeStruct((group, local_width), BF),
            jax.ShapeDtypeStruct((pairs, 8, group), F32),
        ],
        compiler_params=pltpu.CompilerParams(vmem_limit_bytes=48 * MIB),
        cost_estimate=LIGHT,
    )(me, segments[:, None], segments[None, :], qkv)


def attend_back_kernel(
    count, me_ref, column_ref, row_ref, qkv_ref, out_ref, grad_ref, lse_ref, table_ref,
    raw_ref, bias_ref, key_grad_ref, value_grad_ref, key_turned_ref,
):
    me = me_ref[0]
    pair = pl.program_id(0)
    group = column_ref.shape[0]
    shard = group // count
    local_width = raw_ref.shape[1] // 3
    scale = jnp.asarray(HD**-0.5, BF)

    def place(index):
        return pl.multiple_of((index ^ me) * shard, shard)

    def target(part):
        return pl.ds(pl.multiple_of(part * local_width + pair * LANES, LANES), LANES)

    @pl.when(pair == 0)
    def _():
        for index in range(count):
            rows = slice(index * shard, group)
            keys = lax.broadcasted_iota(jnp.int32, (shard, group - index * shard), 0)
            queries = lax.broadcasted_iota(jnp.int32, (shard, group - index * shard), 1)
            own = slice(index * shard, (index + 1) * shard)
            allowed = (column_ref[own, :] == row_ref[:, rows]) & (keys <= queries)
            bias_ref[own, rows] = jnp.where(allowed, 0.0, -1e30)

    for index in range(count):
        rows = slice(index * shard, (index + 1) * shard)
        keys = qkv_ref[1, pl.ds(place(index), shard), :]
        key_turned_ref[:, rows] = keys.astype(F32).T.astype(BF)

    sub = lax.broadcasted_iota(jnp.int32, (8, LANES), 0)
    lane = lax.broadcasted_iota(jnp.int32, (8, LANES), 1)
    chooser = jnp.where((lane // HD) == sub, 1.0, 0.0)
    for index in range(count):
        rows = slice(index * shard, (index + 1) * shard)
        here = pl.ds(place(index), shard)
        query = qkv_ref[0, here, :]
        grad = grad_ref[here, :]
        product = grad.astype(F32) * out_ref[here, :].astype(F32)
        centres = lax.dot_general(
            chooser, product, NT, precision=lax.Precision.HIGHEST, preferred_element_type=F32
        )
        turned = []
        for head in range(2):
            chosen = head_lanes(query.shape, head)
            mine = jnp.where(chosen, query, 0) * scale
            grad_mine = jnp.where(chosen, grad, 0)
            lse = lse_ref[0, head : head + 1, rows]
            centre = centres[head : head + 1, :]
            query_turned = 0.0
            for other in range(index + 1):
                there = pl.ds(place(other), shard)
                span = slice(other * shard, (other + 1) * shard)
                scores = lax.dot_general(
                    qkv_ref[1, there, :], mine, NT, preferred_element_type=F32
                )
                probs = jnp.exp(scores + bias_ref[span, rows] - lse)
                prob_grad = lax.dot_general(
                    qkv_ref[2, there, :], grad_mine, NT, preferred_element_type=F32
                )
                cot = (probs * (prob_grad - centre)).astype(BF)
                value_add = jnp.dot(probs.astype(BF), grad_mine, preferred_element_type=F32)
                key_add = jnp.dot(cot, mine, preferred_element_type=F32)
                if other == index and head == 0:
                    value_grad_ref[span, :] = value_add
                    key_grad_ref[span, :] = key_add
                else:
                    value_grad_ref[span, :] += value_add
                    key_grad_ref[span, :] += key_add
                query_turned = query_turned + jnp.dot(
                    key_turned_ref[head * HD : (head + 1) * HD, span],
                    cot,
                    preferred_element_type=F32,
                )
            turned.append(query_turned)
        query_grad = jnp.concatenate(turned, axis=0).T * HD**-0.5
        raw_ref[here, target(0)] = turn(query_grad, table_ref, here, -1.0).astype(BF)
    for index in range(count):
        rows = slice(index * shard, (index + 1) * shard)
        here = pl.ds(place(index), shard)
        raw_ref[here, target(1)] = turn(key_grad_ref[rows, :], table_ref, here, -1.0).astype(BF)
        raw_ref[here, target(2)] = value_grad_ref[rows, :].astype(BF)


def attend_back(me, segments, qkv, attended, grad, lse, table):
    _, group, local_width = qkv.shape
    count = 4
    pairs = local_width // LANES
    return pl.pallas_call(
        functools.partial(attend_back_kernel, count),
        name="attend_back",
        grid_spec=pltpu.PrefetchScalarGridSpec(
            num_scalar_prefetch=1,
            grid=(pairs,),
            in_specs=[
                pl.BlockSpec((group, 1), lambda p, me: (0, 0)),
                pl.BlockSpec((1, group), lambda p, me: (0, 0)),
                pl.BlockSpec((3, group, LANES), lambda p, me: (0, 0, p)),
                pl.BlockSpec((group, LANES), lambda p, me: (0, p)),
                pl.BlockSpec((group, LANES), lambda p, me: (0, p)),
                pl.BlockSpec((1, 8, group), lambda p, me: (p, 0, 0)),
                pl.BlockSpec((3, group, LANES), lambda p, me: (0, 0, 0)),
            ],
            out_specs=pl.BlockSpec((group, 3 * local_width), lambda p, me: (0, 0)),
            scratch_shapes=[
                pltpu.VMEM((group, group), F32),
                pltpu.VMEM((group, LANES), F32),
                pltpu.VMEM((group, LANES), F32),
                pltpu.VMEM((LANES, group), BF),
            ],
        ),
        out_shape=jax.ShapeDtypeStruct((group, 3 * local_width), BF),
        compiler_params=pltpu.CompilerParams(vmem_limit_bytes=48 * MIB),
        cost_estimate=LIGHT,
    )(me, segments[:, None], segments[None, :], qkv, attended, grad, lse, table)


def weight_grad(sets, pieces, cots, splits, depth):
    many = sets[0].shape[0]
    shard = pieces[0].shape[0]
    tokens = cots[0][0].shape[0]
    widths = [units for _, _, units in cots]
    share = depth // splits
    grouped = len(cots) * splits
    if depth % LANES:
        rows = jnp.concatenate(pieces, 0)
        results = []
        for blocks in sets:
            columns = [
                lax.dynamic_slice_in_dim(rows, blocks[index] * depth, depth, 1)
                for index in range(many)
            ]
            columns = jnp.concatenate(columns, 1)
            for (array, part, _), units in zip(cots, widths):
                products = lax.dot_general(
                    columns,
                    array[:, part * units : (part + 1) * units],
                    TN,
                    preferred_element_type=F32,
                ).astype(BF)
                products = products.reshape(many, splits, share, units)
                results += [
                    products[:, index].reshape(many * share, units) for index in range(splits)
                ]
        return results

    def kernel(blocks_ref, *refs):
        cots_refs = refs[len(pieces) : len(pieces) + len(cots)]
        out_refs, rows_ref = refs[len(pieces) + len(cots) : -1], refs[-1]
        for index, piece_ref in enumerate(refs[: len(pieces)]):
            rows_ref[index * shard : (index + 1) * shard, :] = piece_ref[...]
        products = [
            lax.dot_general(
                rows_ref[...], cots_ref[...], TN, preferred_element_type=F32
            ).astype(BF)
            for cots_ref in cots_refs
        ]
        for turn_index in range(len(sets)):

            @pl.when(pl.program_id(0) // many == turn_index)
            def _():
                mine = iter(out_refs[turn_index * grouped : (turn_index + 1) * grouped])
                for product in products:
                    for index in range(splits):
                        next(mine)[...] = product[index * share : (index + 1) * share]

    def out_spec(turn_index, units):
        return pl.BlockSpec(
            (share, units),
            lambda i, blocks: (jnp.clip(i - turn_index * many, 0, many - 1), 0),
        )

    def cots_spec(part, units):
        return pl.BlockSpec((tokens, units), lambda i, blocks: (0, part))

    order = [(t, units) for t in range(len(sets)) for units in widths for _ in range(splits)]
    return pl.pallas_call(
        kernel,
        name="weight_grad",
        grid_spec=pltpu.PrefetchScalarGridSpec(
            num_scalar_prefetch=1,
            grid=(len(sets) * many,),
            in_specs=[pl.BlockSpec((shard, depth), lambda i, blocks: (0, blocks[i]))] * len(pieces)
            + [cots_spec(part, units) for (_, part, _), units in zip(cots, widths)],
            out_specs=[out_spec(t, units) for t, units in order],
            scratch_shapes=[pltpu.VMEM((tokens, depth), BF)],
        ),
        out_shape=[jax.ShapeDtypeStruct((many * share, units), BF) for _, units in order],
        compiler_params=pltpu.CompilerParams(vmem_limit_bytes=48 * MIB),
        cost_estimate=LIGHT,
    )(jnp.concatenate(sets), *pieces, *[array for array, _, _ in cots])


def ring_add(groups):
    operands, specs, outs, plans = [], [], [], []
    for shape, entries in groups:
        sends = sum(final is None for _, final in entries)
        if sends:
            outs.append(jax.ShapeDtypeStruct((sends * shape[0], shape[1]), BF))
        message = len(outs) - 1
        sent = 0
        for pairs, final in entries:
            place = (message, sent * shape[0])
            if final is None:
                sent += 1
            else:
                outs.append(jax.ShapeDtypeStruct(shape, final))
                place = (len(outs) - 1, 0)
            plans.append((len(operands), len(pairs), place, shape[0]))
            for array, block in pairs:
                operands.append(array)
                specs.append(pl.BlockSpec(shape, lambda i, block=block: (block, 0)))

    def kernel(*refs):
        for start, count, (out, row), rows in plans:
            total = functools.reduce(
                jnp.add, [ref[...].astype(F32) for ref in refs[start : start + count]]
            )
            out_ref = refs[len(operands) + out]
            out_ref[row : row + rows, :] = total.astype(out_ref.dtype)

    return pl.pallas_call(
        kernel,
        name="ring_add",
        grid=(1,),
        in_specs=specs,
        out_specs=[pl.BlockSpec(o.shape, lambda i: (0, 0)) for o in outs],
        out_shape=outs,
        compiler_params=pltpu.CompilerParams(vmem_limit_bytes=48 * MIB),
        cost_estimate=LIGHT,
    )(*operands)


def barrier(value, *others):
    return lax.optimization_barrier((value, *others))[0]


class Order:
    def __init__(self):
        self.last = None

    def __call__(self, step, operand, *others, wait=()):
        if self.last is not None:
            operand = barrier(operand, self.last, *wait)
        result = step(operand, *others)
        self.last = jax.tree.leaves(result)[0]
        return result


class Reducer:
    def __init__(self, order, rounds, partner, along):
        self.order, self.rounds, self.partner, self.along = order, rounds, partner, along
        self.flying, self.rings = [], []
        self.popped = None
        self.kept, self.done, self.late = {}, {}, []

    def send(self, name, sent, kept=None):
        if self.popped is not None:
            sent = barrier(sent, self.popped)
        if kept is not None:
            self.kept[name] = kept
        self.flying.append((name, self.partner(sent)))

    def ring(self, name, kept, other):
        self._enter(name, [kept], F32)
        self._enter(name + "/other", [other], BF)

    def _enter(self, name, arrays, final):
        shape = (arrays[0].shape[0] // self.rounds, arrays[0].shape[1])
        self.rings.append(
            dict(name=name, arrays=arrays, shape=shape, step=0, carry=[], final=final)
        )

    def turn(self, pop=True):
        if pop and self.flying:
            name, got = self.flying.pop(0)
            self.popped = got
            self._enter(name, [self.kept.pop(name), got], F32)
        rings, self.rings = self.rings, []
        groups, members = [], []
        for group in self._groups(rings):
            shape = group[0]["shape"]
            entries = []
            for ring in group:
                end = ring["step"] == self.rounds - 1
                pairs = [(array, ring["step"]) for array in ring["arrays"]] + ring["carry"]
                entries.append((pairs, ring["final"] if end else None))
            groups.append((shape, entries))
            members.append(group)
        if not groups:
            return

        def step(first):
            pairs = groups[0][1][0][0]
            pairs[0] = (first, pairs[0][1])
            return ring_add(groups)

        outs = list(self.order(step, groups[0][1][0][0][0][0]))
        for (shape, entries), group in zip(groups, members):
            message = None
            if any(final is None for _, final in entries):
                message = self.along(outs.pop(0))
            sent = 0
            for ring, (_, final) in zip(group, entries):
                if final is None:
                    ring["carry"] = [(message, sent)]
                    ring["step"] += 1
                    sent += 1
                    self.rings.append(ring)
                else:
                    self._finish(ring["name"], outs.pop(0))

    def _groups(self, rings):
        for shape in dict.fromkeys(ring["shape"] for ring in rings):
            members = [ring for ring in rings if ring["shape"] == shape]
            most = max(1, GROUP_BYTES // (2 * shape[0] * shape[1]))
            count = -(-len(members) // most)
            size = -(-len(members) // count)
            for start in range(0, len(members), size):
                yield members[start : start + size]

    def _finish(self, name, result):
        if name.endswith("/other"):
            self.late.append((name.split("/")[0], self.partner(result)))
        else:
            self.done[name] = result

    def close(self):
        late, self.late = self.late, []
        for name, got in late:
            self.done[name] = self.order(lambda a, n=name: self.done[n] + a.astype(F32), got)

    def busy(self):
        return bool(self.flying or self.rings)


def local(
    n_dp,
    tokens,
    segment_ids,
    cotangent,
    w_qkv,
    qkv_bias,
    w_out,
    w_gate_up,
    w_down,
    norm_gains,
    norm_biases,
):
    shard, width = tokens.shape
    group = segment_ids.shape[0]
    local_width = w_out.shape[0]
    units = w_down.shape[0]
    n_tensor = group // shard
    n_ring = n_dp // 2
    me = lax.axis_index("tensor")
    data_index = lax.axis_index("dp")
    to_core = [(t, t ^ 1) for t in range(n_tensor)]
    to_x = [(t, t ^ 2) for t in range(n_tensor)]
    to_y = [(d, d ^ 1) for d in range(n_dp)]
    up_z = [(d, (d + 2) % n_dp) for d in range(n_dp)]
    order = Order()

    def core(value):
        return lax.ppermute(value, "tensor", to_core)

    def across(value):
        return lax.ppermute(value, "tensor", to_x)

    def over_dp(value, step):
        return lax.ppermute(value, "dp", [(d, d ^ (1 << step)) for d in range(n_dp)])

    dp_steps = (n_dp - 1).bit_length()

    def in_pieces(values):
        blocks = values.reshape((n_tensor, shard) + values.shape[1:])
        return jnp.concatenate(
            [lax.dynamic_index_in_dim(blocks, me ^ k, 0, False) for k in range(n_tensor)], 0
        )

    def stack(*pieces):
        return jnp.concatenate(pieces, 0)

    def rows_of(half, rows, w, dims):
        return order(lambda r, *more: pair_product(half, (r, *more), w, dims), *rows)

    def hop(pair):
        return pair[0], [core(pair[1])]

    def send_far(pair):
        mine, tiles = hop(pair)
        return across(order(lambda t: add_tiles(mine, (t,)), *tiles))

    ring_index = data_index // 2
    rings = jnp.stack([(ring_index - 1 - s + 2 * n_ring) % n_ring for s in range(n_ring)])
    keep_blocks = (2 * rings + data_index % 2).astype(jnp.int32)
    send_blocks = (2 * rings + 1 - data_index % 2).astype(jnp.int32)

    depth = width // n_dp

    def grad_of(sets, pieces, *cots, splits=1):
        def step(first):
            arrays = [(first,) + cots[0][1:], *cots[1:]]
            return weight_grad(sets, pieces, arrays, splits, depth)

        return order(step, cots[0][0])

    reducer = Reducer(
        order,
        n_ring,
        lambda value: lax.ppermute(value, "dp", to_y),
        lambda value: lax.ppermute(value, "dp", up_z),
    )

    me_one = me[None].astype(jnp.int32)
    gains = [norm_gains[index : index + 1] for index in range(2)]
    shifts = [norm_biases[index : index + 1] for index in range(2)]
    live = (segment_ids >= 0).astype(F32)
    live_rows = lax.dynamic_slice_in_dim(live, me * shard, shard, 0)

    one_own = order(norm_rows, tokens, gains[0], shifts[0])
    one_far = across(one_own)
    one_near = core(one_own)
    out_cot = (cotangent.astype(F32) * live_rows[:, None]).astype(BF)
    in_near = core(out_cot)
    live_total = jnp.sum(live)[None]
    table = rope_tables(in_pieces(positions_of(segment_ids)))
    w_flat = w_gate_up.reshape(width, 2 * units)
    w_split = jnp.transpose(w_qkv, (1, 0, 2))
    bias_rows = qkv_bias[:, None, :]
    qkv = order(
        lambda a: project(0, a, one_near, w_split, bias_rows, table, None),
        one_own, wait=(w_flat, table),
    )
    one_far = barrier(one_far, qkv)
    one_last = core(one_far)
    in_far = across(barrier(out_cot, one_far))
    qkv = order(
        lambda a: project(1, a, one_last, w_split, bias_rows, table, qkv), one_far
    )
    attended, lse = order(lambda q: attend(me_one, segment_ids, q), qkv)
    attended = barrier(attended, in_far)
    branch_far = send_far(rows_of(1, (attended,), w_out, NN))
    near, tiles = hop(rows_of(0, (attended,), w_out, NN))
    in_far = barrier(in_far, attended)
    in_last = core(in_far)
    incoming = (out_cot, in_near, in_far, in_last)
    incoming_full = order(stack, *incoming)
    act_grad = order(
        lambda r: lax.dot_general(r, w_down, NT, preferred_element_type=F32), incoming_full
    )
    live_total = order(jnp.add, over_dp(live_total, 0), live_total)
    hidden, two_own = order(
        lambda t: add_norm_rows(t, near, branch_far, tiles, gains[1], shifts[1]), tokens
    )
    two_far = across(two_own)
    two_near = core(two_own)
    fed = order(lambda a: feed(0, a, two_near, w_flat, act_grad, None), two_own)
    for step in range(1, dp_steps):
        live_total = order(jnp.add, over_dp(live_total, step), live_total)
    live_total = live_total[0]
    two_far = barrier(two_far, order.last)
    two_last = core(two_far)
    activated, gate_cot, up_cot = order(
        lambda a: feed(1, a, two_last, w_flat, act_grad, fed), two_far
    )
    two = (two_own, two_near, two_far, two_last)
    one = (one_own, one_near, one_far, one_last)

    down_sent = grad_of([send_blocks], incoming, (activated, 0, units), splits=2)
    reducer.send("down1", down_sent[1])
    (gate_sent,) = grad_of([send_blocks], two, (gate_cot, 0, units))
    down_kept = grad_of([keep_blocks], incoming, (activated, 0, units), splits=2)
    reducer.kept["down1"] = down_kept[1]
    reducer.ring("down0", down_kept[0], down_sent[0])
    second_far_pair = rows_of(1, (gate_cot, up_cot), w_flat, NT)
    reducer.turn(pop=False)
    second_near_pair = rows_of(0, (gate_cot, up_cot), w_flat, NT)

    reducer.send("gate", gate_sent)
    reducer.turn()
    second_far = send_far(second_far_pair)
    second_near, second_tiles = hop(second_near_pair)
    (reducer.kept["gate"],) = grad_of([keep_blocks], two, (gate_cot, 0, units))
    up_grads = grad_of([send_blocks, keep_blocks], two, (up_cot, 0, units))
    reducer.send("up", *up_grads)
    reducer.turn(pop=False)
    hidden_grad, branch_own, sums_two = order(
        lambda h: norm_rows_back(
            h, second_near, second_far, second_tiles, out_cot, gains[1], (F32, BF)
        ),
        hidden,
    )
    branch_far = across(branch_own)
    branch_near = core(branch_own)
    down_pair = rows_of(1, (activated,), w_down, NN)
    down_near_pair = rows_of(0, (activated,), w_down, NN)

    reducer.turn()
    branch_last = core(barrier(branch_far, order.last))
    branch = (branch_own, branch_near, branch_far, branch_last)
    branch_full = order(stack, *branch)
    attended_grad = order(
        lambda r: lax.dot_general(r, w_out, NT, preferred_element_type=F32).astype(BF),
        branch_full,
    )
    raw_cot = order(
        lambda g: attend_back(me_one, segment_ids, qkv, attended, g, lse, table), attended_grad
    )
    reducer.turn(pop=False)
    qkv_grads = grad_of(
        [send_blocks, keep_blocks],
        one,
        (raw_cot, 0, 2 * local_width),
        (raw_cot, 2, local_width),
    )
    reducer.send("query_key", qkv_grads[0], qkv_grads[2])

    reducer.turn()
    out_grads = grad_of([send_blocks, keep_blocks], branch, (attended, 0, local_width))
    reducer.send("out", *out_grads)
    first_far_pair = rows_of(1, (raw_cot,), w_split, NT)
    first_near_pair = rows_of(0, (raw_cot,), w_split, NT)
    bias_sum = order(lambda r: jnp.sum(r.astype(F32), axis=0).reshape(3, local_width), raw_cot)

    reducer.turn(pop=False)
    reducer.turn()
    reducer.send("value", qkv_grads[1], qkv_grads[3])
    first_far = send_far(first_far_pair)
    first_near, first_tiles = hop(first_near_pair)

    reducer.turn()
    input_grad, sums_one = order(
        lambda t: norm_rows_back(
            t, first_near, first_far, first_tiles, hidden_grad, gains[0], (F32,)
        ),
        tokens,
    )
    down_far = send_far(down_pair)
    down_near, down_tiles = hop(down_near_pair)
    rows_sum = jnp.concatenate([sums_one[:1], sums_two[:1], sums_one[1:], sums_two[1:]], 0)
    rows_near = core(rows_sum)

    reducer.turn()
    reducer.close()
    rows_sum = order(jnp.add, rows_near, rows_sum)
    rows_far = across(rows_sum)
    output = order(lambda h: add_rows(h, down_near, down_far, down_tiles), hidden)
    rows_sum = order(jnp.add, rows_far, rows_sum)
    small = jnp.concatenate([rows_sum.reshape(-1), bias_sum.reshape(-1)])
    scaled = {}

    def finish():
        for name, parts, turned in (
            ("down", ("down0", "down1"), True),
            ("gate", ("gate",), False),
            ("up", ("up",), False),
            ("out", ("out",), True),
            ("query_key", ("query_key",), False),
            ("value", ("value",), False),
        ):
            if name not in scaled and all(part in reducer.done for part in parts):

                def step(first, parts=parts, turned=turned):
                    arrays = [first, *[reducer.done[part] for part in parts[1:]]]
                    whole = jnp.concatenate(arrays, 0) / live_total
                    return whole.T if turned else whole

                scaled[name] = order(step, reducer.done[parts[0]])

    for step in range(dp_steps):
        small_far = over_dp(small, step)
        reducer.turn()
        small = order(jnp.add, small_far, small)
        finish()
    small = small / live_total
    rows_sum = small[: 4 * width].reshape(4, width)
    bias_sum = small[4 * width :].reshape(3, local_width)
    while reducer.busy():
        reducer.turn()
        finish()
    return (
        output,
        input_grad,
        jnp.concatenate([scaled["query_key"], scaled["value"]], 1).reshape(-1, 3, local_width),
        bias_sum,
        scaled["out"],
        jnp.stack([scaled["gate"], scaled["up"]], 1),
        scaled["down"],
        rows_sum[:2],
        rows_sum[2:],
    )


def solution(mesh):
    in_specs = (
        P(("dp", "tensor"), None),
        P("dp"),
        P(("dp", "tensor"), None),
        P(None, None, "tensor"),
        P(None, "tensor"),
        P("tensor", None),
        P(None, None, "tensor"),
        P("tensor", None),
        P(),
        P(),
    )
    out_specs = (
        P(("dp", "tensor"), None),
        P(("dp", "tensor"), None),
        P("dp", None, "tensor"),
        P(None, "tensor"),
        P("tensor", "dp"),
        P("dp", None, "tensor"),
        P("tensor", "dp"),
        P(),
        P(),
    )
    return jax.shard_map(
        functools.partial(local, mesh.shape["dp"]),
        mesh=mesh,
        in_specs=in_specs,
        out_specs=out_specs,
        check_vma=False,
    )
```

```python
import functools

import jax
import jax.numpy as jnp
from jax import lax
from jax.experimental import pallas as pl
from jax.experimental.pallas import tpu as pltpu
from jax.sharding import PartitionSpec as P

HD = 64
ROT = 16
LANES = 128
epsilon = 1e-05
rope_base = 10000.0
BF = jnp.bfloat16
F32 = jnp.float32
MIB = 1 << 20
GROUP_BYTES = 1_200_000
LIGHT = pl.CostEstimate(flops=1, bytes_accessed=1, transcendentals=0)
NT = (((1,), (1,)), ((), ()))
TN = (((0,), (0,)), ((), ()))
NN = (((1,), (0,)), ((), ()))


def positions_of(segments):
    row_index = jnp.arange(segments.shape[0], dtype=jnp.int32)
    previous = jnp.concatenate([jnp.full((1,), -2, jnp.int32), segments[:-1]])
    starts = jnp.where(segments != previous, row_index, 0)
    return row_index - lax.cummax(starts, axis=0)


def rope_tables(positions):
    half = ROT // 2
    dim = jnp.arange(LANES) % HD
    exponent = (dim % half).astype(F32) * 2.0 / ROT
    frequency = jnp.where(dim < ROT, rope_base ** (-exponent), 0.0)
    angles = positions.astype(F32)[:, None] * frequency[None, :]
    cosine, sine = jnp.cos(angles), jnp.sin(angles)
    lower = jnp.where(dim < half, -sine, 0.0)
    upper = jnp.where((dim >= half) & (dim < ROT), sine, 0.0)
    return jnp.stack([cosine, lower, upper])


def turn(block, table_ref, rows, sign):
    half = ROT // 2
    back = pltpu.roll(block, LANES - half, 1)
    ahead = pltpu.roll(block, half, 1)
    return (
        block * table_ref[0, rows, :]
        + sign * (back * table_ref[1, rows, :] + ahead * table_ref[2, rows, :])
    )


def project_kernel(
    first_ref, second_ref, w_ref, bias_ref, table_ref, old_ref, out_ref, rows_ref
):
    shard = first_ref.shape[0]

    @pl.when(pl.program_id(0) == 0)
    def _():
        rows_ref[:shard, :] = first_ref[...]
        rows_ref[shard:, :] = second_ref[...]

    raw = jnp.dot(rows_ref[...], w_ref[0], preferred_element_type=F32) + bias_ref[0]

    @pl.when(pl.program_id(0) < 2)
    def _():
        for start in range(0, raw.shape[1], LANES):
            piece = turn(raw[:, start : start + LANES], table_ref, slice(None), 1.0)
            out_ref[0, :, start : start + LANES] = piece.astype(BF)

    @pl.when(pl.program_id(0) == 2)
    def _():
        out_ref[0] = raw.astype(BF)


def project(half, first, second, w, bias, table, old):
    shard, width = first.shape
    local_width = w.shape[2]
    whole = jax.ShapeDtypeStruct((3, 4 * shard, local_width), BF)
    kernel = project_kernel
    operands = [first, second, w, bias, table]
    specs = [
        pl.BlockSpec((shard, width), lambda c: (0, 0)),
        pl.BlockSpec((shard, width), lambda c: (0, 0)),
        pl.BlockSpec((1, width, local_width), lambda c: (c, 0, 0)),
        pl.BlockSpec((1, 1, local_width), lambda c: (c, 0, 0)),
        pl.BlockSpec((3, 2 * shard, LANES), lambda c: (0, half, 0)),
    ]
    aliases = {}
    if old is None:

        def kernel(a, b, c, d, e, out_ref, rows_ref):
            project_kernel(a, b, c, d, e, None, out_ref, rows_ref)

    else:
        operands.append(old)
        specs.append(pl.BlockSpec(memory_space=pl.ANY))
        aliases = {5: 0}
    return pl.pallas_call(
        kernel,
        name="project",
        grid=(3,),
        in_specs=specs,
        out_specs=pl.BlockSpec((1, 2 * shard, local_width), lambda c: (c, half, 0)),
        out_shape=whole,
        input_output_aliases=aliases,
        scratch_shapes=[pltpu.VMEM((2 * shard, width), BF)],
        compiler_params=pltpu.CompilerParams(vmem_limit_bytes=48 * MIB),
        cost_estimate=LIGHT,
    )(*operands)


def feed_kernel(
    first_ref, second_ref, w0_ref, w1_ref, w2_ref, w3_ref, act_grad_ref,
    act_ref, gate_ref, up_ref, rows_ref, w_ref,
):
    shard = first_ref.shape[0]

    @pl.when(pl.program_id(0) == 0)
    def _():
        rows_ref[:shard, :] = first_ref[...]
        rows_ref[shard:, :] = second_ref[...]

    for index, part_ref in enumerate((w0_ref, w1_ref, w2_ref, w3_ref)):
        w_ref[:, index * LANES : (index + 1) * LANES] = part_ref[...]
    products = [
        jnp.dot(
            rows_ref[...],
            w_ref[:, 2 * index * LANES : 2 * (index + 1) * LANES],
            preferred_element_type=F32,
        )
        for index in range(2)
    ]
    for index, product in enumerate(products):
        lanes = slice(index * LANES, (index + 1) * LANES)
        gate, up = product[:, :LANES], product[:, LANES:]
        s = jax.nn.sigmoid(gate)
        silu = gate * s
        act_grad = act_grad_ref[:, lanes].astype(F32)
        act_ref[:, lanes] = (silu * up).astype(BF)
        gate_ref[:, lanes] = (act_grad * up * (s + silu * (1.0 - s))).astype(BF)
        up_ref[:, lanes] = (act_grad * silu).astype(BF)


def feed(half, first, second, w, act_grad, old):
    shard, width = first.shape
    units = w.shape[1] // 2
    tiles = units // LANES

    def tile(base, index):
        return pl.BlockSpec(
            (width, LANES), lambda j: (0, base + jnp.minimum(2 * j + index, tiles - 1))
        )

    operands = [first, second, w, w, w, w, act_grad]
    specs = [
        pl.BlockSpec((shard, width), lambda j: (0, 0)),
        pl.BlockSpec((shard, width), lambda j: (0, 0)),
        tile(0, 0),
        tile(tiles, 0),
        tile(0, 1),
        tile(tiles, 1),
        pl.BlockSpec((2 * shard, 2 * LANES), lambda j: (half, j)),
    ]
    kernel = feed_kernel
    aliases = {}
    if old is not None:

        def kernel(*refs):
            feed_kernel(*refs[:7], *refs[10:])

        operands += list(old)
        specs += [pl.BlockSpec(memory_space=pl.ANY)] * 3
        aliases = {7: 0, 8: 1, 9: 2}
    return pl.pallas_call(
        kernel,
        name="feed",
        grid=(pl.cdiv(tiles, 2),),
        in_specs=specs,
        out_specs=[pl.BlockSpec((2 * shard, 2 * LANES), lambda j: (half, j))] * 3,
        out_shape=[jax.ShapeDtypeStruct((4 * shard, units), BF)] * 3,
        input_output_aliases=aliases,
        scratch_shapes=[pltpu.VMEM((2 * shard, width), BF), pltpu.VMEM((width, 4 * LANES), BF)],
        compiler_params=pltpu.CompilerParams(vmem_limit_bytes=60 * MIB),
        cost_estimate=LIGHT,
    )(*operands)


def pair_product(half, rows, w, dims):
    group = rows[0].shape[0]
    shard = group // 4
    depth = sum(r.shape[1] for r in rows)
    turned = dims is NT
    width = w.shape[-2] if turned else w.shape[-1]
    tile = min(512, width)
    if w.ndim == 3:
        w_spec = pl.BlockSpec((w.shape[0], tile, w.shape[2]), lambda j: (0, j, 0))
    elif turned:
        w_spec = pl.BlockSpec((tile, depth), lambda j: (j, 0))
    else:
        w_spec = pl.BlockSpec((depth, tile), lambda j: (0, j))

    def kernel(*refs):
        rows_refs, w_ref = refs[: len(rows)], refs[len(rows)]
        first_ref, second_ref = refs[len(rows) + 1 :]
        if w.ndim == 3:
            part = w.shape[2]
            product = sum(
                lax.dot_general(
                    rows_refs[0][:, c * part : (c + 1) * part],
                    w_ref[c],
                    dims,
                    preferred_element_type=F32,
                )
                for c in range(w.shape[0])
            )
        elif turned:
            product, start = 0.0, 0
            for rows_ref in rows_refs:
                end = start + rows_ref.shape[1]
                product = product + lax.dot_general(
                    rows_ref[...], w_ref[:, start:end], dims, preferred_element_type=F32
                )
                start = end
        else:
            product = lax.dot_general(
                rows_refs[0][...], w_ref[...], dims, preferred_element_type=F32
            )
        product = product.astype(BF)
        first_ref[...] = product[:shard]
        second_ref[...] = product[shard:]

    return pl.pallas_call(
        kernel,
        name="pair_product",
        grid=(width // tile,),
        in_specs=[pl.BlockSpec((2 * shard, r.shape[1]), lambda j: (half, 0)) for r in rows]
        + [w_spec],
        out_specs=[pl.BlockSpec((shard, tile), lambda j: (0, j))] * 2,
        out_shape=[jax.ShapeDtypeStruct((shard, width), BF)] * 2,
        compiler_params=pltpu.CompilerParams(vmem_limit_bytes=48 * MIB),
        cost_estimate=LIGHT,
    )(*rows, w)


def centre_rows(values):
    average = jnp.mean(values, axis=-1, keepdims=True)
    centered = values - average
    variance = jnp.mean(centered * centered, axis=-1, keepdims=True)
    spread = lax.rsqrt(variance + epsilon)
    return centered * spread, spread


ROW_STEP = 64


def row_call(kernel, shard, width, inputs, per_row, outs):
    step = min(ROW_STEP, shard)
    specs = [
        pl.BlockSpec((step, a.shape[1]), lambda i: (i, 0))
        if rowwise
        else pl.BlockSpec(a.shape, lambda i: (0, 0))
        for a, rowwise in zip(inputs, per_row)
    ]
    out_specs = [
        pl.BlockSpec((step, width), lambda i: (i, 0))
        if o.shape[0] == shard
        else pl.BlockSpec(o.shape, lambda i: (0, 0))
        for o in outs
    ]
    return pl.pallas_call(
        kernel,
        name="row_call",
        grid=(shard // step,),
        in_specs=specs,
        out_specs=out_specs,
        out_shape=outs,
        compiler_params=pltpu.CompilerParams(vmem_limit_bytes=48 * MIB),
        cost_estimate=LIGHT,
    )(*inputs)


def norm_rows(tokens, gain, shift):
    def kernel(tokens_ref, gain_ref, shift_ref, out_ref):
        hat, _ = centre_rows(tokens_ref[...].astype(F32))
        out_ref[...] = (hat * gain_ref[...] + shift_ref[...]).astype(BF)

    shard, width = tokens.shape
    return row_call(
        kernel, shard, width, (tokens, gain, shift), (1, 0, 0),
        [jax.ShapeDtypeStruct((shard, width), BF)],
    )[0]


def total_of(own_ref, far_ref, tile_refs):
    tiles = jnp.concatenate([ref[...].astype(F32) for ref in tile_refs], axis=1)
    return own_ref[...].astype(F32) + tiles + far_ref[...].astype(F32)


def add_tiles(own, tiles):
    def kernel(own_ref, *refs):
        *tile_refs, out_ref = refs
        tiles = jnp.concatenate([ref[...].astype(F32) for ref in tile_refs], axis=1)
        out_ref[...] = (own_ref[...].astype(F32) + tiles).astype(BF)

    return row_call(
        kernel, *own.shape, (own, *tiles), (1,) * (1 + len(tiles)),
        [jax.ShapeDtypeStruct(own.shape, BF)],
    )[0]


def add_rows(values, own, far, tiles):
    def kernel(values_ref, own_ref, far_ref, *refs):
        *tile_refs, out_ref = refs
        total = values_ref[...] + total_of(own_ref, far_ref, tile_refs)
        out_ref[...] = total.astype(BF)

    return row_call(
        kernel, *own.shape, (values, own, far, *tiles), (1,) * (3 + len(tiles)),
        [jax.ShapeDtypeStruct(own.shape, BF)],
    )[0]


def add_norm_rows(tokens, own, far, tiles, gain, shift):
    def kernel(tokens_ref, own_ref, far_ref, gain_ref, shift_ref, *refs):
        *tile_refs, hidden_ref, out_ref = refs
        hidden = tokens_ref[...].astype(F32) + total_of(own_ref, far_ref, tile_refs)
        hidden_ref[...] = hidden
        hat, _ = centre_rows(hidden)
        out_ref[...] = (hat * gain_ref[...] + shift_ref[...]).astype(BF)

    shard, width = tokens.shape
    return row_call(
        kernel, shard, width, (tokens, own, far, gain, shift, *tiles),
        (1, 1, 1, 0, 0) + (1,) * len(tiles),
        [jax.ShapeDtypeStruct((shard, width), F32), jax.ShapeDtypeStruct((shard, width), BF)],
    )


def norm_rows_back(values, own, far, tiles, base, gain, dtypes):
    def kernel(values_ref, own_ref, far_ref, base_ref, gain_ref, *refs):
        tile_refs, grad_refs, sums_ref = refs[: len(tiles)], refs[len(tiles) : -1], refs[-1]
        hat, spread = centre_rows(values_ref[...].astype(F32))
        grad = total_of(own_ref, far_ref, tile_refs)
        scaled = grad * gain_ref[...]
        mean_scaled = jnp.mean(scaled, axis=-1, keepdims=True)
        mean_hat = jnp.mean(scaled * hat, axis=-1, keepdims=True)
        result = base_ref[...].astype(F32) + spread * (scaled - mean_scaled - hat * mean_hat)
        for ref in grad_refs:
            ref[...] = result.astype(ref.dtype)
        sums = jnp.concatenate(
            [
                jnp.sum(grad * hat, axis=0, keepdims=True),
                jnp.sum(grad, axis=0, keepdims=True),
            ],
            0,
        )

        @pl.when(pl.program_id(0) == 0)
        def _():
            sums_ref[...] = sums

        @pl.when(pl.program_id(0) > 0)
        def _():
            sums_ref[...] += sums

    shard, width = values.shape
    return row_call(
        kernel, shard, width, (values, own, far, base, gain, *tiles),
        (1, 1, 1, 1, 0) + (1,) * len(tiles),
        [jax.ShapeDtypeStruct((shard, width), d) for d in dtypes]
        + [jax.ShapeDtypeStruct((2, width), F32)],
    )


def head_lanes(shape, head):
    lane = lax.broadcasted_iota(jnp.int32, shape, 1)
    return (lane < HD) if head == 0 else (lane >= HD)


def attend_kernel(count, me_ref, column_ref, row_ref, low_ref, out_ref, lse_ref, bias_ref):
    me = me_ref[0]
    shard = column_ref.shape[0] // count

    def place(index):
        return pl.multiple_of((index ^ me) * shard, shard)

    @pl.when(pl.program_id(0) == 0)
    def _():
        for index in range(count):
            span = (index + 1) * shard
            rows = slice(index * shard, span)
            own = lax.broadcasted_iota(jnp.int32, (shard, span), 0) + index * shard
            other = lax.broadcasted_iota(jnp.int32, (shard, span), 1)
            allowed = (column_ref[rows, :] == row_ref[:, :span]) & (other <= own)
            bias_ref[rows, :span] = jnp.where(allowed, 0.0, -1e30)

    lane = lax.broadcasted_iota(jnp.int32, (shard, LANES), 1)
    for index in range(count):
        rows = slice(index * shard, (index + 1) * shard)
        query = low_ref[0, pl.ds(place(index), shard), :]
        parts, sums = [], []
        for head in range(2):
            mine = jnp.where(head_lanes(query.shape, head), query, 0) * jnp.asarray(HD**-0.5, BF)
            scores = []
            for other in range(index + 1):
                keys = low_ref[1, pl.ds(place(other), shard), :]
                scores.append(
                    lax.dot_general(mine, keys, NT, preferred_element_type=F32)
                    + bias_ref[rows, other * shard : (other + 1) * shard]
                )
            largest = jnp.max(functools.reduce(jnp.maximum, scores), axis=1, keepdims=True)
            lifted = [jnp.exp(score - largest) for score in scores]
            total = jnp.sum(functools.reduce(jnp.add, lifted), axis=1, keepdims=True)
            acc = 0.0
            for other in range(index + 1):
                acc = acc + jnp.dot(
                    lifted[other].astype(BF),
                    low_ref[2, pl.ds(place(other), shard), :],
                    preferred_element_type=F32,
                )
            parts.append(acc / total)
            sums.append(largest + jnp.log(total))
        out_ref[pl.ds(place(index), shard), :] = jnp.where(lane < HD, parts[0], parts[1]).astype(BF)
        wide = jnp.where(lane == 0, sums[0], jnp.where(lane == 1, sums[1], 0.0))
        lse_ref[0, :, rows] = wide.T[:8, :]


def attend(me, segments, qkv):
    _, group, local_width = qkv.shape
    count = 4
    pairs = local_width // LANES

    def kernel(me_ref, column_ref, row_ref, qkv_ref, out_ref, lse_ref, bias_ref):
        attend_kernel(count, me_ref, column_ref, row_ref, qkv_ref, out_ref, lse_ref, bias_ref)

    return pl.pallas_call(
        kernel,
        name="attend",
        grid_spec=pltpu.PrefetchScalarGridSpec(
            num_scalar_prefetch=1,
            grid=(pairs,),
            in_specs=[
                pl.BlockSpec((group, 1), lambda p, me: (0, 0)),
                pl.BlockSpec((1, group), lambda p, me: (0, 0)),
                pl.BlockSpec((3, group, LANES), lambda p, me: (0, 0, p)),
            ],
            out_specs=[
                pl.BlockSpec((group, LANES), lambda p, me: (0, p)),
                pl.BlockSpec((1, 8, group), lambda p, me: (p, 0, 0)),
            ],
            scratch_shapes=[pltpu.VMEM((group, group), F32)],
        ),
        out_shape=[
            jax.ShapeDtypeStruct((group, local_width), BF),
            jax.ShapeDtypeStruct((pairs, 8, group), F32),
        ],
        compiler_params=pltpu.CompilerParams(vmem_limit_bytes=48 * MIB),
        cost_estimate=LIGHT,
    )(me, segments[:, None], segments[None, :], qkv)


def attend_back_kernel(
    count, me_ref, column_ref, row_ref, qkv_ref, out_ref, grad_ref, lse_ref, table_ref,
    raw_ref, bias_ref, key_grad_ref, value_grad_ref, key_turned_ref,
):
    me = me_ref[0]
    pair = pl.program_id(0)
    group = column_ref.shape[0]
    shard = group // count
    local_width = raw_ref.shape[1] // 3
    scale = jnp.asarray(HD**-0.5, BF)

    def place(index):
        return pl.multiple_of((index ^ me) * shard, shard)

    def target(part):
        return pl.ds(pl.multiple_of(part * local_width + pair * LANES, LANES), LANES)

    @pl.when(pair == 0)
    def _():
        for index in range(count):
            rows = slice(index * shard, group)
            keys = lax.broadcasted_iota(jnp.int32, (shard, group - index * shard), 0)
            queries = lax.broadcasted_iota(jnp.int32, (shard, group - index * shard), 1)
            own = slice(index * shard, (index + 1) * shard)
            allowed = (column_ref[own, :] == row_ref[:, rows]) & (keys <= queries)
            bias_ref[own, rows] = jnp.where(allowed, 0.0, -1e30)

    for index in range(count):
        rows = slice(index * shard, (index + 1) * shard)
        keys = qkv_ref[1, pl.ds(place(index), shard), :]
        key_turned_ref[:, rows] = keys.astype(F32).T.astype(BF)

    sub = lax.broadcasted_iota(jnp.int32, (8, LANES), 0)
    lane = lax.broadcasted_iota(jnp.int32, (8, LANES), 1)
    chooser = jnp.where((lane // HD) == sub, 1.0, 0.0)
    for index in range(count):
        rows = slice(index * shard, (index + 1) * shard)
        here = pl.ds(place(index), shard)
        query = qkv_ref[0, here, :]
        grad = grad_ref[here, :]
        product = grad.astype(F32) * out_ref[here, :].astype(F32)
        centres = lax.dot_general(
            chooser, product, NT, precision=lax.Precision.HIGHEST, preferred_element_type=F32
        )
        turned = []
        for head in range(2):
            chosen = head_lanes(query.shape, head)
            mine = jnp.where(chosen, query, 0) * scale
            grad_mine = jnp.where(chosen, grad, 0)
            lse = lse_ref[0, head : head + 1, rows]
            centre = centres[head : head + 1, :]
            query_turned = 0.0
            for other in range(index + 1):
                there = pl.ds(place(other), shard)
                span = slice(other * shard, (other + 1) * shard)
                scores = lax.dot_general(
                    qkv_ref[1, there, :], mine, NT, preferred_element_type=F32
                )
                probs = jnp.exp(scores + bias_ref[span, rows] - lse)
                prob_grad = lax.dot_general(
                    qkv_ref[2, there, :], grad_mine, NT, preferred_element_type=F32
                )
                cot = (probs * (prob_grad - centre)).astype(BF)
                value_add = jnp.dot(probs.astype(BF), grad_mine, preferred_element_type=F32)
                key_add = jnp.dot(cot, mine, preferred_element_type=F32)
                if other == index and head == 0:
                    value_grad_ref[span, :] = value_add
                    key_grad_ref[span, :] = key_add
                else:
                    value_grad_ref[span, :] += value_add
                    key_grad_ref[span, :] += key_add
                query_turned = query_turned + jnp.dot(
                    key_turned_ref[head * HD : (head + 1) * HD, span],
                    cot,
                    preferred_element_type=F32,
                )
            turned.append(query_turned)
        query_grad = jnp.concatenate(turned, axis=0).T * HD**-0.5
        raw_ref[here, target(0)] = turn(query_grad, table_ref, here, -1.0).astype(BF)
    for index in range(count):
        rows = slice(index * shard, (index + 1) * shard)
        here = pl.ds(place(index), shard)
        raw_ref[here, target(1)] = turn(key_grad_ref[rows, :], table_ref, here, -1.0).astype(BF)
        raw_ref[here, target(2)] = value_grad_ref[rows, :].astype(BF)


def attend_back(me, segments, qkv, attended, grad, lse, table):
    _, group, local_width = qkv.shape
    count = 4
    pairs = local_width // LANES
    return pl.pallas_call(
        functools.partial(attend_back_kernel, count),
        name="attend_back",
        grid_spec=pltpu.PrefetchScalarGridSpec(
            num_scalar_prefetch=1,
            grid=(pairs,),
            in_specs=[
                pl.BlockSpec((group, 1), lambda p, me: (0, 0)),
                pl.BlockSpec((1, group), lambda p, me: (0, 0)),
                pl.BlockSpec((3, group, LANES), lambda p, me: (0, 0, p)),
                pl.BlockSpec((group, LANES), lambda p, me: (0, p)),
                pl.BlockSpec((group, LANES), lambda p, me: (0, p)),
                pl.BlockSpec((1, 8, group), lambda p, me: (p, 0, 0)),
                pl.BlockSpec((3, group, LANES), lambda p, me: (0, 0, 0)),
            ],
            out_specs=pl.BlockSpec((group, 3 * local_width), lambda p, me: (0, 0)),
            scratch_shapes=[
                pltpu.VMEM((group, group), F32),
                pltpu.VMEM((group, LANES), F32),
                pltpu.VMEM((group, LANES), F32),
                pltpu.VMEM((LANES, group), BF),
            ],
        ),
        out_shape=jax.ShapeDtypeStruct((group, 3 * local_width), BF),
        compiler_params=pltpu.CompilerParams(vmem_limit_bytes=48 * MIB),
        cost_estimate=LIGHT,
    )(me, segments[:, None], segments[None, :], qkv, attended, grad, lse, table)


def weight_grad(sets, pieces, cots, splits, depth):
    many = sets[0].shape[0]
    shard = pieces[0].shape[0]
    tokens = cots[0][0].shape[0]
    widths = [units for _, _, units in cots]
    share = depth // splits
    grouped = len(cots) * splits
    if depth % LANES:
        rows = jnp.concatenate(pieces, 0)
        results = []
        for blocks in sets:
            columns = [
                lax.dynamic_slice_in_dim(rows, blocks[index] * depth, depth, 1)
                for index in range(many)
            ]
            columns = jnp.concatenate(columns, 1)
            for (array, part, _), units in zip(cots, widths):
                products = lax.dot_general(
                    columns,
                    array[:, part * units : (part + 1) * units],
                    TN,
                    preferred_element_type=F32,
                ).astype(BF)
                products = products.reshape(many, splits, share, units)
                results += [
                    products[:, index].reshape(many * share, units) for index in range(splits)
                ]
        return results

    def kernel(blocks_ref, *refs):
        cots_refs = refs[len(pieces) : len(pieces) + len(cots)]
        out_refs, rows_ref = refs[len(pieces) + len(cots) : -1], refs[-1]
        for index, piece_ref in enumerate(refs[: len(pieces)]):
            rows_ref[index * shard : (index + 1) * shard, :] = piece_ref[...]
        products = [
            lax.dot_general(
                rows_ref[...], cots_ref[...], TN, preferred_element_type=F32
            ).astype(BF)
            for cots_ref in cots_refs
        ]
        for turn_index in range(len(sets)):

            @pl.when(pl.program_id(0) // many == turn_index)
            def _():
                mine = iter(out_refs[turn_index * grouped : (turn_index + 1) * grouped])
                for product in products:
                    for index in range(splits):
                        next(mine)[...] = product[index * share : (index + 1) * share]

    def out_spec(turn_index, units):
        return pl.BlockSpec(
            (share, units),
            lambda i, blocks: (jnp.clip(i - turn_index * many, 0, many - 1), 0),
        )

    def cots_spec(part, units):
        return pl.BlockSpec((tokens, units), lambda i, blocks: (0, part))

    order = [(t, units) for t in range(len(sets)) for units in widths for _ in range(splits)]
    return pl.pallas_call(
        kernel,
        name="weight_grad",
        grid_spec=pltpu.PrefetchScalarGridSpec(
            num_scalar_prefetch=1,
            grid=(len(sets) * many,),
            in_specs=[pl.BlockSpec((shard, depth), lambda i, blocks: (0, blocks[i]))] * len(pieces)
            + [cots_spec(part, units) for (_, part, _), units in zip(cots, widths)],
            out_specs=[out_spec(t, units) for t, units in order],
            scratch_shapes=[pltpu.VMEM((tokens, depth), BF)],
        ),
        out_shape=[jax.ShapeDtypeStruct((many * share, units), BF) for _, units in order],
        compiler_params=pltpu.CompilerParams(vmem_limit_bytes=60 * MIB),
        cost_estimate=LIGHT,
    )(jnp.concatenate(sets), *pieces, *[array for array, _, _ in cots])


def ring_add(groups):
    operands, specs, outs, plans = [], [], [], []
    for shape, entries in groups:
        sends = sum(final is None for _, final in entries)
        if sends:
            outs.append(jax.ShapeDtypeStruct((sends * shape[0], shape[1]), BF))
        message = len(outs) - 1
        sent = 0
        for pairs, final in entries:
            place = (message, sent * shape[0])
            if final is None:
                sent += 1
            else:
                outs.append(jax.ShapeDtypeStruct(shape, final))
                place = (len(outs) - 1, 0)
            plans.append((len(operands), len(pairs), place, shape[0]))
            for array, block in pairs:
                operands.append(array)
                specs.append(pl.BlockSpec(shape, lambda i, block=block: (block, 0)))

    def kernel(*refs):
        for start, count, (out, row), rows in plans:
            total = functools.reduce(
                jnp.add, [ref[...].astype(F32) for ref in refs[start : start + count]]
            )
            out_ref = refs[len(operands) + out]
            out_ref[row : row + rows, :] = total.astype(out_ref.dtype)

    return pl.pallas_call(
        kernel,
        name="ring_add",
        grid=(1,),
        in_specs=specs,
        out_specs=[pl.BlockSpec(o.shape, lambda i: (0, 0)) for o in outs],
        out_shape=outs,
        compiler_params=pltpu.CompilerParams(vmem_limit_bytes=48 * MIB),
        cost_estimate=LIGHT,
    )(*operands)


def turned(parts, scale):
    rows, units = parts[0].shape

    def kernel(scale_ref, *refs):
        whole = jnp.concatenate([ref[...] for ref in refs[:-1]], axis=0) * scale_ref[0]
        refs[-1][...] = whole.T

    return pl.pallas_call(
        kernel,
        name="turned",
        grid=(1,),
        in_specs=[pl.BlockSpec(memory_space=pltpu.SMEM)]
        + [pl.BlockSpec(part.shape, lambda i: (0, 0)) for part in parts],
        out_specs=pl.BlockSpec((units, rows * len(parts)), lambda i: (0, 0)),
        out_shape=jax.ShapeDtypeStruct((units, rows * len(parts)), F32),
        compiler_params=pltpu.CompilerParams(vmem_limit_bytes=48 * MIB),
        cost_estimate=LIGHT,
    )(scale, *parts)


def interleaved(first, second, scale):
    rows, columns = first.shape
    step = min(32, rows)

    def kernel(scale_ref, first_ref, second_ref, out_ref):
        out_ref[:, 0, :] = first_ref[...] * scale_ref[0]
        out_ref[:, 1, :] = second_ref[...] * scale_ref[0]

    return pl.pallas_call(
        kernel,
        name="interleaved",
        grid=(rows // step,),
        in_specs=[pl.BlockSpec(memory_space=pltpu.SMEM)]
        + [pl.BlockSpec((step, columns), lambda i: (i, 0))] * 2,
        out_specs=pl.BlockSpec((step, 2, columns), lambda i: (i, 0, 0)),
        out_shape=jax.ShapeDtypeStruct((rows, 2, columns), F32),
        compiler_params=pltpu.CompilerParams(vmem_limit_bytes=48 * MIB),
        cost_estimate=LIGHT,
    )(scale, first, second)


def barrier(value, *others):
    return lax.optimization_barrier((value, *others))[0]


class Order:
    def __init__(self):
        self.last = None

    def __call__(self, step, operand, *others, wait=()):
        if self.last is not None:
            operand = barrier(operand, self.last, *wait)
        result = step(operand, *others)
        self.last = jax.tree.leaves(result)[0]
        return result


class Reducer:
    def __init__(self, order, rounds, partner, along):
        self.order, self.rounds, self.partner, self.along = order, rounds, partner, along
        self.flying, self.rings = [], []
        self.popped = None
        self.kept, self.done, self.late = {}, {}, []

    def send(self, name, sent, kept=None):
        if self.popped is not None:
            sent = barrier(sent, self.popped)
        if kept is not None:
            self.kept[name] = kept
        self.flying.append((name, self.partner(sent)))

    def ring(self, name, kept, other):
        self._enter(name, [kept], F32)
        self._enter(name + "/other", [other], BF)

    def _enter(self, name, arrays, final):
        shape = (arrays[0].shape[0] // self.rounds, arrays[0].shape[1])
        self.rings.append(
            dict(name=name, arrays=arrays, shape=shape, step=0, carry=[], final=final)
        )

    def turn(self, pop=True):
        if pop and self.flying:
            name, got = self.flying.pop(0)
            self.popped = got
            self._enter(name, [self.kept.pop(name), got], F32)
        rings, self.rings = self.rings, []
        groups, members = [], []
        for group in self._groups(rings):
            shape = group[0]["shape"]
            entries = []
            for ring in group:
                end = ring["step"] == self.rounds - 1
                pairs = [(array, ring["step"]) for array in ring["arrays"]] + ring["carry"]
                entries.append((pairs, ring["final"] if end else None))
            groups.append((shape, entries))
            members.append(group)
        if not groups:
            return

        def step(first):
            pairs = groups[0][1][0][0]
            pairs[0] = (first, pairs[0][1])
            return ring_add(groups)

        outs = list(self.order(step, groups[0][1][0][0][0][0]))
        for (shape, entries), group in zip(groups, members):
            message = None
            if any(final is None for _, final in entries):
                message = self.along(outs.pop(0))
            sent = 0
            for ring, (_, final) in zip(group, entries):
                if final is None:
                    ring["carry"] = [(message, sent)]
                    ring["step"] += 1
                    sent += 1
                    self.rings.append(ring)
                else:
                    self._finish(ring["name"], outs.pop(0))

    def _groups(self, rings):
        for shape in dict.fromkeys(ring["shape"] for ring in rings):
            members = [ring for ring in rings if ring["shape"] == shape]
            most = max(1, GROUP_BYTES // (2 * shape[0] * shape[1]))
            count = -(-len(members) // most)
            size = -(-len(members) // count)
            for start in range(0, len(members), size):
                yield members[start : start + size]

    def _finish(self, name, result):
        if name.endswith("/other"):
            self.late.append((name.split("/")[0], self.partner(result)))
        else:
            self.done[name] = result

    def close(self):
        late, self.late = self.late, []
        for name, got in late:
            self.done[name] = self.order(lambda a, n=name: self.done[n] + a.astype(F32), got)

    def busy(self):
        return bool(self.flying or self.rings)


def local(
    n_dp,
    tokens,
    segment_ids,
    cotangent,
    w_qkv,
    qkv_bias,
    w_out,
    w_gate_up,
    w_down,
    norm_gains,
    norm_biases,
):
    shard, width = tokens.shape
    group = segment_ids.shape[0]
    local_width = w_out.shape[0]
    units = w_down.shape[0]
    n_tensor = group // shard
    n_ring = n_dp // 2
    me = lax.axis_index("tensor")
    data_index = lax.axis_index("dp")
    to_core = [(t, t ^ 1) for t in range(n_tensor)]
    to_x = [(t, t ^ 2) for t in range(n_tensor)]
    to_y = [(d, d ^ 1) for d in range(n_dp)]
    up_z = [(d, (d + 2) % n_dp) for d in range(n_dp)]
    order = Order()

    def core(value):
        return lax.ppermute(value, "tensor", to_core)

    def across(value):
        return lax.ppermute(value, "tensor", to_x)

    def over_dp(value, step):
        return lax.ppermute(value, "dp", [(d, d ^ (1 << step)) for d in range(n_dp)])

    dp_steps = (n_dp - 1).bit_length()

    def in_pieces(values):
        blocks = values.reshape((n_tensor, shard) + values.shape[1:])
        return jnp.concatenate(
            [lax.dynamic_index_in_dim(blocks, me ^ k, 0, False) for k in range(n_tensor)], 0
        )

    def stack(*pieces):
        return jnp.concatenate(pieces, 0)

    def rows_of(half, rows, w, dims):
        return order(lambda r, *more: pair_product(half, (r, *more), w, dims), *rows)

    def hop(pair):
        return pair[0], [core(pair[1])]

    def send_far(pair):
        mine, tiles = hop(pair)
        return across(order(lambda t: add_tiles(mine, (t,)), *tiles))

    ring_index = data_index // 2
    rings = jnp.stack([(ring_index - 1 - s + 2 * n_ring) % n_ring for s in range(n_ring)])
    keep_blocks = (2 * rings + data_index % 2).astype(jnp.int32)
    send_blocks = (2 * rings + 1 - data_index % 2).astype(jnp.int32)

    depth = width // n_dp

    def grad_of(sets, pieces, *cots, splits=1):
        def step(first):
            arrays = [(first,) + cots[0][1:], *cots[1:]]
            return weight_grad(sets, pieces, arrays, splits, depth)

        return order(step, cots[0][0])

    reducer = Reducer(
        order,
        n_ring,
        lambda value: lax.ppermute(value, "dp", to_y),
        lambda value: lax.ppermute(value, "dp", up_z),
    )

    me_one = me[None].astype(jnp.int32)
    gains = [norm_gains[index : index + 1] for index in range(2)]
    shifts = [norm_biases[index : index + 1] for index in range(2)]
    live = (segment_ids >= 0).astype(F32)
    live_rows = lax.dynamic_slice_in_dim(live, me * shard, shard, 0)

    one_own = order(norm_rows, tokens, gains[0], shifts[0])
    one_far = across(one_own)
    one_near = core(one_own)
    out_cot = (cotangent.astype(F32) * live_rows[:, None]).astype(BF)
    in_near = core(out_cot)
    live_total = jnp.sum(live)[None]
    table = rope_tables(in_pieces(positions_of(segment_ids)))
    w_flat = w_gate_up.reshape(width, 2 * units)
    w_split = jnp.transpose(w_qkv, (1, 0, 2))
    bias_rows = qkv_bias[:, None, :]
    qkv = order(
        lambda a: project(0, a, one_near, w_split, bias_rows, table, None),
        one_own, wait=(w_flat, table),
    )
    one_far = barrier(one_far, qkv)
    one_last = core(one_far)
    in_far = across(barrier(out_cot, one_far))
    qkv = order(
        lambda a: project(1, a, one_last, w_split, bias_rows, table, qkv), one_far
    )
    attended, lse = order(lambda q: attend(me_one, segment_ids, q), qkv)
    attended = barrier(attended, in_far)
    branch_far = send_far(rows_of(1, (attended,), w_out, NN))
    near, tiles = hop(rows_of(0, (attended,), w_out, NN))
    in_far = barrier(in_far, attended)
    in_last = core(in_far)
    incoming = (out_cot, in_near, in_far, in_last)
    incoming_full = order(stack, *incoming)
    act_grad = order(
        lambda r: lax.dot_general(r, w_down, NT, preferred_element_type=F32), incoming_full
    )
    live_total = order(jnp.add, over_dp(live_total, 0), live_total)
    hidden, two_own = order(
        lambda t: add_norm_rows(t, near, branch_far, tiles, gains[1], shifts[1]), tokens
    )
    two_far = across(two_own)
    two_near = core(two_own)
    fed = order(lambda a: feed(0, a, two_near, w_flat, act_grad, None), two_own)
    for step in range(1, dp_steps):
        live_total = order(jnp.add, over_dp(live_total, step), live_total)
    live_total = live_total[0]
    two_far = barrier(two_far, order.last)
    two_last = core(two_far)
    activated, gate_cot, up_cot = order(
        lambda a: feed(1, a, two_last, w_flat, act_grad, fed), two_far
    )
    two = (two_own, two_near, two_far, two_last)
    one = (one_own, one_near, one_far, one_last)

    down_sent = grad_of([send_blocks], incoming, (activated, 0, units), splits=2)
    reducer.send("down1", down_sent[1])
    (gate_sent,) = grad_of([send_blocks], two, (gate_cot, 0, units))
    down_kept = grad_of([keep_blocks], incoming, (activated, 0, units), splits=2)
    reducer.kept["down1"] = down_kept[1]
    reducer.ring("down0", down_kept[0], down_sent[0])
    second_far_pair = rows_of(1, (gate_cot, up_cot), w_flat, NT)
    reducer.turn(pop=False)
    second_near_pair = rows_of(0, (gate_cot, up_cot), w_flat, NT)

    reducer.send("gate", gate_sent)
    reducer.turn()
    second_far = send_far(second_far_pair)
    second_near, second_tiles = hop(second_near_pair)
    (reducer.kept["gate"],) = grad_of([keep_blocks], two, (gate_cot, 0, units))
    up_grads = grad_of([send_blocks, keep_blocks], two, (up_cot, 0, units))
    reducer.send("up", *up_grads)
    reducer.turn(pop=False)
    hidden_grad, branch_own, sums_two = order(
        lambda h: norm_rows_back(
            h, second_near, second_far, second_tiles, out_cot, gains[1], (F32, BF)
        ),
        hidden,
    )
    branch_far = across(branch_own)
    branch_near = core(branch_own)
    down_pair = rows_of(1, (activated,), w_down, NN)
    down_near_pair = rows_of(0, (activated,), w_down, NN)

    reducer.turn()
    branch_last = core(barrier(branch_far, order.last))
    branch = (branch_own, branch_near, branch_far, branch_last)
    branch_full = order(stack, *branch)
    attended_grad = order(
        lambda r: lax.dot_general(r, w_out, NT, preferred_element_type=F32).astype(BF),
        branch_full,
    )
    raw_cot = order(
        lambda g: attend_back(me_one, segment_ids, qkv, attended, g, lse, table), attended_grad
    )
    reducer.turn(pop=False)
    query_key_grads = grad_of([send_blocks, keep_blocks], one, (raw_cot, 0, 2 * local_width))
    reducer.send("query_key", *query_key_grads)

    reducer.turn()
    out_grads = grad_of([send_blocks, keep_blocks], branch, (attended, 0, local_width))
    reducer.send("out", *out_grads)
    value_grads = grad_of([send_blocks, keep_blocks], one, (raw_cot, 2, local_width))
    first_far_pair = rows_of(1, (raw_cot,), w_split, NT)
    first_near_pair = rows_of(0, (raw_cot,), w_split, NT)
    bias_sum = order(lambda r: jnp.sum(r.astype(F32), axis=0).reshape(3, local_width), raw_cot)

    reducer.turn(pop=False)
    reducer.turn()
    reducer.send("value", *value_grads)
    first_far = send_far(first_far_pair)
    first_near, first_tiles = hop(first_near_pair)

    reducer.turn()
    input_grad, sums_one = order(
        lambda t: norm_rows_back(
            t, first_near, first_far, first_tiles, hidden_grad, gains[0], (F32,)
        ),
        tokens,
    )
    down_far = send_far(down_pair)
    down_near, down_tiles = hop(down_near_pair)
    rows_sum = jnp.concatenate([sums_one[:1], sums_two[:1], sums_one[1:], sums_two[1:]], 0)
    rows_near = core(rows_sum)

    reducer.turn()
    reducer.close()
    rows_sum = order(jnp.add, rows_near, rows_sum)
    rows_far = across(rows_sum)
    rows_sum = order(jnp.add, rows_far, rows_sum)
    small = jnp.concatenate([rows_sum.reshape(-1), bias_sum.reshape(-1)])
    scaled = {}
    scale = (1.0 / live_total)[None]

    def finish():
        done = reducer.done
        for name, parts in (("down", ("down0", "down1")), ("out", ("out",))):
            if name not in scaled and all(part in done for part in parts):
                scaled[name] = order(
                    lambda first, rest=parts[1:]: turned([first, *[done[r] for r in rest]], scale),
                    done[parts[0]],
                )
        if "gate_up" not in scaled and "gate" in done and "up" in done:
            scaled["gate_up"] = order(
                lambda g: interleaved(g, done["up"], scale), done["gate"]
            )
        for name in ("query_key", "value"):
            if name not in scaled and name in done:
                scaled[name] = done[name] * scale

    for step in range(dp_steps):
        small_far = over_dp(small, step)
        reducer.turn()
        small = order(jnp.add, small_far, small)
        finish()
        if step == 1:
            output = order(lambda h: add_rows(h, down_near, down_far, down_tiles), hidden)
    small = small * scale
    rows_sum = small[: 4 * width].reshape(4, width)
    bias_sum = small[4 * width :].reshape(3, local_width)
    while reducer.busy():
        reducer.turn()
        finish()
    return (
        output,
        input_grad,
        jnp.concatenate([scaled["query_key"], scaled["value"]], 1).reshape(-1, 3, local_width),
        bias_sum,
        scaled["out"],
        scaled["gate_up"],
        scaled["down"],
        rows_sum[:2],
        rows_sum[2:],
    )


def solution(mesh):
    in_specs = (
        P(("dp", "tensor"), None),
        P("dp"),
        P(("dp", "tensor"), None),
        P(None, None, "tensor"),
        P(None, "tensor"),
        P("tensor", None),
        P(None, None, "tensor"),
        P("tensor", None),
        P(),
        P(),
    )
    out_specs = (
        P(("dp", "tensor"), None),
        P(("dp", "tensor"), None),
        P("dp", None, "tensor"),
        P(None, "tensor"),
        P("tensor", "dp"),
        P("dp", None, "tensor"),
        P("tensor", "dp"),
        P(),
        P(),
    )
    return jax.shard_map(
        functools.partial(local, mesh.shape["dp"]),
        mesh=mesh,
        in_specs=in_specs,
        out_specs=out_specs,
        check_vma=False,
    )
```

```python
import functools

import jax
import jax.numpy as jnp
from jax import lax
from jax.experimental import pallas as pl
from jax.experimental.pallas import tpu as pltpu
from jax.sharding import PartitionSpec as P

HD = 64
ROT = 16
LANES = 128
epsilon = 1e-05
rope_base = 10000.0
BF = jnp.bfloat16
F32 = jnp.float32
MIB = 1 << 20
GROUP_BYTES = 1_200_000
LIGHT = pl.CostEstimate(flops=1, bytes_accessed=1, transcendentals=0)
NT = (((1,), (1,)), ((), ()))
TN = (((0,), (0,)), ((), ()))
NN = (((1,), (0,)), ((), ()))


def positions_of(segments):
    row_index = jnp.arange(segments.shape[0], dtype=jnp.int32)
    previous = jnp.concatenate([jnp.full((1,), -2, jnp.int32), segments[:-1]])
    starts = jnp.where(segments != previous, row_index, 0)
    return row_index - lax.cummax(starts, axis=0)


def rope_tables(positions):
    half = ROT // 2
    dim = jnp.arange(LANES) % HD
    exponent = (dim % half).astype(F32) * 2.0 / ROT
    frequency = jnp.where(dim < ROT, rope_base ** (-exponent), 0.0)
    angles = positions.astype(F32)[:, None] * frequency[None, :]
    cosine, sine = jnp.cos(angles), jnp.sin(angles)
    lower = jnp.where(dim < half, -sine, 0.0)
    upper = jnp.where((dim >= half) & (dim < ROT), sine, 0.0)
    return jnp.stack([cosine, lower, upper])


def turn(block, table_ref, rows, sign):
    half = ROT // 2
    back = pltpu.roll(block, LANES - half, 1)
    ahead = pltpu.roll(block, half, 1)
    return (
        block * table_ref[0, rows, :]
        + sign * (back * table_ref[1, rows, :] + ahead * table_ref[2, rows, :])
    )


def project_kernel(
    first_ref, second_ref, w_ref, bias_ref, table_ref, old_ref, out_ref, rows_ref
):
    shard = first_ref.shape[0]

    @pl.when(pl.program_id(0) == 0)
    def _():
        rows_ref[:shard, :] = first_ref[...]
        rows_ref[shard:, :] = second_ref[...]

    raw = jnp.dot(rows_ref[...], w_ref[0], preferred_element_type=F32) + bias_ref[0]

    @pl.when(pl.program_id(0) < 2)
    def _():
        for start in range(0, raw.shape[1], LANES):
            piece = turn(raw[:, start : start + LANES], table_ref, slice(None), 1.0)
            out_ref[0, :, start : start + LANES] = piece.astype(BF)

    @pl.when(pl.program_id(0) == 2)
    def _():
        out_ref[0] = raw.astype(BF)


def project(half, first, second, w, bias, table, old):
    shard, width = first.shape
    local_width = w.shape[2]
    whole = jax.ShapeDtypeStruct((3, 4 * shard, local_width), BF)
    kernel = project_kernel
    operands = [first, second, w, bias, table]
    specs = [
        pl.BlockSpec((shard, width), lambda c: (0, 0)),
        pl.BlockSpec((shard, width), lambda c: (0, 0)),
        pl.BlockSpec((1, width, local_width), lambda c: (c, 0, 0)),
        pl.BlockSpec((1, 1, local_width), lambda c: (c, 0, 0)),
        pl.BlockSpec((3, 2 * shard, LANES), lambda c: (0, half, 0)),
    ]
    aliases = {}
    if old is None:

        def kernel(a, b, c, d, e, out_ref, rows_ref):
            project_kernel(a, b, c, d, e, None, out_ref, rows_ref)

    else:
        operands.append(old)
        specs.append(pl.BlockSpec(memory_space=pl.ANY))
        aliases = {5: 0}
    return pl.pallas_call(
        kernel,
        name="project",
        grid=(3,),
        in_specs=specs,
        out_specs=pl.BlockSpec((1, 2 * shard, local_width), lambda c: (c, half, 0)),
        out_shape=whole,
        input_output_aliases=aliases,
        scratch_shapes=[pltpu.VMEM((2 * shard, width), BF)],
        compiler_params=pltpu.CompilerParams(vmem_limit_bytes=48 * MIB),
        cost_estimate=LIGHT,
    )(*operands)


def feed_kernel(
    first_ref, second_ref, w0_ref, w1_ref, w2_ref, w3_ref, act_grad_ref,
    act_ref, gate_ref, up_ref, rows_ref, w_ref,
):
    shard = first_ref.shape[0]

    @pl.when(pl.program_id(0) == 0)
    def _():
        rows_ref[:shard, :] = first_ref[...]
        rows_ref[shard:, :] = second_ref[...]

    for index, part_ref in enumerate((w0_ref, w1_ref, w2_ref, w3_ref)):
        w_ref[:, index * LANES : (index + 1) * LANES] = part_ref[...]
    products = [
        jnp.dot(
            rows_ref[...],
            w_ref[:, 2 * index * LANES : 2 * (index + 1) * LANES],
            preferred_element_type=F32,
        )
        for index in range(2)
    ]
    for index, product in enumerate(products):
        lanes = slice(index * LANES, (index + 1) * LANES)
        gate, up = product[:, :LANES], product[:, LANES:]
        s = jax.nn.sigmoid(gate)
        silu = gate * s
        act_grad = act_grad_ref[:, lanes].astype(F32)
        act_ref[:, lanes] = (silu * up).astype(BF)
        gate_ref[:, lanes] = (act_grad * up * (s + silu * (1.0 - s))).astype(BF)
        up_ref[:, lanes] = (act_grad * silu).astype(BF)


def feed(half, first, second, w, act_grad, old):
    shard, width = first.shape
    units = w.shape[1] // 2
    tiles = units // LANES

    def tile(base, index):
        return pl.BlockSpec(
            (width, LANES), lambda j: (0, base + jnp.minimum(2 * j + index, tiles - 1))
        )

    operands = [first, second, w, w, w, w, act_grad]
    specs = [
        pl.BlockSpec((shard, width), lambda j: (0, 0)),
        pl.BlockSpec((shard, width), lambda j: (0, 0)),
        tile(0, 0),
        tile(tiles, 0),
        tile(0, 1),
        tile(tiles, 1),
        pl.BlockSpec((2 * shard, 2 * LANES), lambda j: (half, j)),
    ]
    kernel = feed_kernel
    aliases = {}
    if old is not None:

        def kernel(*refs):
            feed_kernel(*refs[:7], *refs[10:])

        operands += list(old)
        specs += [pl.BlockSpec(memory_space=pl.ANY)] * 3
        aliases = {7: 0, 8: 1, 9: 2}
    return pl.pallas_call(
        kernel,
        name="feed",
        grid=(pl.cdiv(tiles, 2),),
        in_specs=specs,
        out_specs=[pl.BlockSpec((2 * shard, 2 * LANES), lambda j: (half, j))] * 3,
        out_shape=[jax.ShapeDtypeStruct((4 * shard, units), BF)] * 3,
        input_output_aliases=aliases,
        scratch_shapes=[pltpu.VMEM((2 * shard, width), BF), pltpu.VMEM((width, 4 * LANES), BF)],
        compiler_params=pltpu.CompilerParams(vmem_limit_bytes=60 * MIB),
        cost_estimate=LIGHT,
    )(*operands)


def pair_product(half, rows, w, dims):
    group = rows[0].shape[0]
    shard = group // 4
    depth = sum(r.shape[1] for r in rows)
    turned = dims is NT
    width = w.shape[-2] if turned else w.shape[-1]
    tile = min(512, width)
    if w.ndim == 3:
        w_spec = pl.BlockSpec((w.shape[0], tile, w.shape[2]), lambda j: (0, j, 0))
    elif turned:
        w_spec = pl.BlockSpec((tile, depth), lambda j: (j, 0))
    else:
        w_spec = pl.BlockSpec((depth, tile), lambda j: (0, j))

    def kernel(*refs):
        rows_refs, w_ref = refs[: len(rows)], refs[len(rows)]
        first_ref, second_ref = refs[len(rows) + 1 :]
        if w.ndim == 3:
            part = w.shape[2]
            product = sum(
                lax.dot_general(
                    rows_refs[0][:, c * part : (c + 1) * part],
                    w_ref[c],
                    dims,
                    preferred_element_type=F32,
                )
                for c in range(w.shape[0])
            )
        elif turned:
            product, start = 0.0, 0
            for rows_ref in rows_refs:
                end = start + rows_ref.shape[1]
                product = product + lax.dot_general(
                    rows_ref[...], w_ref[:, start:end], dims, preferred_element_type=F32
                )
                start = end
        else:
            product = lax.dot_general(
                rows_refs[0][...], w_ref[...], dims, preferred_element_type=F32
            )
        product = product.astype(BF)
        first_ref[...] = product[:shard]
        second_ref[...] = product[shard:]

    return pl.pallas_call(
        kernel,
        name="pair_product",
        grid=(width // tile,),
        in_specs=[pl.BlockSpec((2 * shard, r.shape[1]), lambda j: (half, 0)) for r in rows]
        + [w_spec],
        out_specs=[pl.BlockSpec((shard, tile), lambda j: (0, j))] * 2,
        out_shape=[jax.ShapeDtypeStruct((shard, width), BF)] * 2,
        compiler_params=pltpu.CompilerParams(vmem_limit_bytes=48 * MIB),
        cost_estimate=LIGHT,
    )(*rows, w)


def centre_rows(values):
    average = jnp.mean(values, axis=-1, keepdims=True)
    centered = values - average
    variance = jnp.mean(centered * centered, axis=-1, keepdims=True)
    spread = lax.rsqrt(variance + epsilon)
    return centered * spread, spread


ROW_STEP = 64


def row_call(kernel, shard, width, inputs, per_row, outs):
    step = min(ROW_STEP, shard)
    specs = [
        pl.BlockSpec((step, a.shape[1]), lambda i: (i, 0))
        if rowwise
        else pl.BlockSpec(a.shape, lambda i: (0, 0))
        for a, rowwise in zip(inputs, per_row)
    ]
    out_specs = [
        pl.BlockSpec((step, width), lambda i: (i, 0))
        if o.shape[0] == shard
        else pl.BlockSpec(o.shape, lambda i: (0, 0))
        for o in outs
    ]
    return pl.pallas_call(
        kernel,
        name="row_call",
        grid=(shard // step,),
        in_specs=specs,
        out_specs=out_specs,
        out_shape=outs,
        compiler_params=pltpu.CompilerParams(vmem_limit_bytes=48 * MIB),
        cost_estimate=LIGHT,
    )(*inputs)


def norm_rows(tokens, gain, shift):
    def kernel(tokens_ref, gain_ref, shift_ref, out_ref):
        hat, _ = centre_rows(tokens_ref[...].astype(F32))
        out_ref[...] = (hat * gain_ref[...] + shift_ref[...]).astype(BF)

    shard, width = tokens.shape
    return row_call(
        kernel, shard, width, (tokens, gain, shift), (1, 0, 0),
        [jax.ShapeDtypeStruct((shard, width), BF)],
    )[0]


def total_of(own_ref, far_ref, tile_refs):
    tiles = jnp.concatenate([ref[...].astype(F32) for ref in tile_refs], axis=1)
    return own_ref[...].astype(F32) + tiles + far_ref[...].astype(F32)


def add_tiles(own, tiles):
    def kernel(own_ref, *refs):
        *tile_refs, out_ref = refs
        tiles = jnp.concatenate([ref[...].astype(F32) for ref in tile_refs], axis=1)
        out_ref[...] = (own_ref[...].astype(F32) + tiles).astype(BF)

    return row_call(
        kernel, *own.shape, (own, *tiles), (1,) * (1 + len(tiles)),
        [jax.ShapeDtypeStruct(own.shape, BF)],
    )[0]


def add_rows(values, own, far, tiles):
    def kernel(values_ref, own_ref, far_ref, *refs):
        *tile_refs, out_ref = refs
        total = values_ref[...] + total_of(own_ref, far_ref, tile_refs)
        out_ref[...] = total.astype(BF)

    return row_call(
        kernel, *own.shape, (values, own, far, *tiles), (1,) * (3 + len(tiles)),
        [jax.ShapeDtypeStruct(own.shape, BF)],
    )[0]


def add_norm_rows(tokens, own, far, tiles, gain, shift):
    def kernel(tokens_ref, own_ref, far_ref, gain_ref, shift_ref, *refs):
        *tile_refs, hidden_ref, out_ref = refs
        hidden = tokens_ref[...].astype(F32) + total_of(own_ref, far_ref, tile_refs)
        hidden_ref[...] = hidden
        hat, _ = centre_rows(hidden)
        out_ref[...] = (hat * gain_ref[...] + shift_ref[...]).astype(BF)

    shard, width = tokens.shape
    return row_call(
        kernel, shard, width, (tokens, own, far, gain, shift, *tiles),
        (1, 1, 1, 0, 0) + (1,) * len(tiles),
        [jax.ShapeDtypeStruct((shard, width), F32), jax.ShapeDtypeStruct((shard, width), BF)],
    )


def norm_rows_back(values, own, far, tiles, base, gain, dtypes):
    def kernel(values_ref, own_ref, far_ref, base_ref, gain_ref, *refs):
        tile_refs, grad_refs, sums_ref = refs[: len(tiles)], refs[len(tiles) : -1], refs[-1]
        hat, spread = centre_rows(values_ref[...].astype(F32))
        grad = total_of(own_ref, far_ref, tile_refs)
        scaled = grad * gain_ref[...]
        mean_scaled = jnp.mean(scaled, axis=-1, keepdims=True)
        mean_hat = jnp.mean(scaled * hat, axis=-1, keepdims=True)
        result = base_ref[...].astype(F32) + spread * (scaled - mean_scaled - hat * mean_hat)
        for ref in grad_refs:
            ref[...] = result.astype(ref.dtype)
        sums = jnp.concatenate(
            [
                jnp.sum(grad * hat, axis=0, keepdims=True),
                jnp.sum(grad, axis=0, keepdims=True),
            ],
            0,
        )

        @pl.when(pl.program_id(0) == 0)
        def _():
            sums_ref[...] = sums

        @pl.when(pl.program_id(0) > 0)
        def _():
            sums_ref[...] += sums

    shard, width = values.shape
    return row_call(
        kernel, shard, width, (values, own, far, base, gain, *tiles),
        (1, 1, 1, 1, 0) + (1,) * len(tiles),
        [jax.ShapeDtypeStruct((shard, width), d) for d in dtypes]
        + [jax.ShapeDtypeStruct((2, width), F32)],
    )


def head_lanes(shape, head):
    lane = lax.broadcasted_iota(jnp.int32, shape, 1)
    return (lane < HD) if head == 0 else (lane >= HD)


def attend_kernel(
    count, me_ref, column_ref, row_ref, low_ref, out_ref, lse_ref, bias_ref, key_ref, value_ref
):
    me = me_ref[0]
    shard = column_ref.shape[0] // count

    def place(index):
        return pl.multiple_of((index ^ me) * shard, shard)

    @pl.when(pl.program_id(0) == 0)
    def _():
        for index in range(count):
            span = (index + 1) * shard
            rows = slice(index * shard, span)
            own = lax.broadcasted_iota(jnp.int32, (shard, span), 0) + index * shard
            other = lax.broadcasted_iota(jnp.int32, (shard, span), 1)
            allowed = (column_ref[rows, :] == row_ref[:, :span]) & (other <= own)
            bias_ref[rows, :span] = jnp.where(allowed, 0.0, -1e30)

    for index in range(count):
        rows = slice(index * shard, (index + 1) * shard)
        here = pl.ds(place(index), shard)
        key_ref[rows, :] = low_ref[1, here, :]
        value_ref[rows, :] = low_ref[2, here, :]
    lane = lax.broadcasted_iota(jnp.int32, (shard, LANES), 1)
    for index in range(count):
        span = (index + 1) * shard
        rows = slice(index * shard, span)
        query = low_ref[0, pl.ds(place(index), shard), :] * jnp.asarray(HD**-0.5, BF)
        both = jnp.concatenate(
            [jnp.where(head_lanes(query.shape, head), query, 0) for head in range(2)], axis=0
        )
        scores = lax.dot_general(both, key_ref[:span, :], NT, preferred_element_type=F32)
        scores = scores.reshape(2, shard, span) + bias_ref[rows, :span][None]
        largest = jnp.max(scores, axis=2, keepdims=True)
        lifted = jnp.exp(scores - largest)
        total = jnp.sum(lifted, axis=2, keepdims=True)
        acc = jnp.dot(
            lifted.astype(BF).reshape(2 * shard, span), value_ref[:span, :],
            preferred_element_type=F32,
        ).reshape(2, shard, LANES) / total
        out_ref[pl.ds(place(index), shard), :] = jnp.where(lane < HD, acc[0], acc[1]).astype(BF)
        sums = largest + jnp.log(total)
        wide = jnp.where(lane == 0, sums[0], jnp.where(lane == 1, sums[1], 0.0))
        lse_ref[0, :, rows] = wide.T[:8, :]


def attend(me, segments, qkv):
    _, group, local_width = qkv.shape
    count = 4
    pairs = local_width // LANES

    kernel = functools.partial(attend_kernel, count)
    return pl.pallas_call(
        kernel,
        name="attend",
        grid_spec=pltpu.PrefetchScalarGridSpec(
            num_scalar_prefetch=1,
            grid=(pairs,),
            in_specs=[
                pl.BlockSpec((group, 1), lambda p, me: (0, 0)),
                pl.BlockSpec((1, group), lambda p, me: (0, 0)),
                pl.BlockSpec((3, group, LANES), lambda p, me: (0, 0, p)),
            ],
            out_specs=[
                pl.BlockSpec((group, LANES), lambda p, me: (0, p)),
                pl.BlockSpec((1, 8, group), lambda p, me: (p, 0, 0)),
            ],
            scratch_shapes=[
                pltpu.VMEM((group, group), F32),
                pltpu.VMEM((group, LANES), BF),
                pltpu.VMEM((group, LANES), BF),
            ],
        ),
        out_shape=[
            jax.ShapeDtypeStruct((group, local_width), BF),
            jax.ShapeDtypeStruct((pairs, 8, group), F32),
        ],
        compiler_params=pltpu.CompilerParams(vmem_limit_bytes=48 * MIB),
        cost_estimate=LIGHT,
    )(me, segments[:, None], segments[None, :], qkv)


def attend_back_kernel(
    count, me_ref, column_ref, row_ref, qkv_ref, out_ref, grad_ref, lse_ref, table_ref,
    raw_ref, bias_ref, key_grad_ref, value_grad_ref, key_turned_ref, key_ref, value_ref,
):
    me = me_ref[0]
    pair = pl.program_id(0)
    group = column_ref.shape[0]
    shard = group // count
    local_width = raw_ref.shape[1] // 3
    scale = jnp.asarray(HD**-0.5, BF)

    def place(index):
        return pl.multiple_of((index ^ me) * shard, shard)

    def target(part):
        return pl.ds(pl.multiple_of(part * local_width + pair * LANES, LANES), LANES)

    @pl.when(pair == 0)
    def _():
        for index in range(count):
            rows = slice(index * shard, group)
            keys = lax.broadcasted_iota(jnp.int32, (shard, group - index * shard), 0)
            queries = lax.broadcasted_iota(jnp.int32, (shard, group - index * shard), 1)
            own = slice(index * shard, (index + 1) * shard)
            allowed = (column_ref[own, :] == row_ref[:, rows]) & (keys <= queries)
            bias_ref[own, rows] = jnp.where(allowed, 0.0, -1e30)

    for index in range(count):
        rows = slice(index * shard, (index + 1) * shard)
        here = pl.ds(place(index), shard)
        keys = qkv_ref[1, here, :]
        key_ref[rows, :] = keys
        value_ref[rows, :] = qkv_ref[2, here, :]
        key_turned_ref[:, rows] = keys.astype(F32).T.astype(BF)

    sub = lax.broadcasted_iota(jnp.int32, (8, LANES), 0)
    lane = lax.broadcasted_iota(jnp.int32, (8, LANES), 1)
    chooser = jnp.where((lane // HD) == sub, 1.0, 0.0)

    def by_head(value):
        return jnp.concatenate(
            [jnp.where(head_lanes(value.shape, head), value, 0) for head in range(2)], axis=0
        )

    for index in reversed(range(count)):
        span = (index + 1) * shard
        rows = slice(index * shard, span)
        here = pl.ds(place(index), shard)
        grad = grad_ref[here, :]
        product = grad.astype(F32) * out_ref[here, :].astype(F32)
        centres = lax.dot_general(
            chooser, product, NT, precision=lax.Precision.HIGHEST, preferred_element_type=F32
        )
        centre = jnp.concatenate([centres[0:1, :], centres[1:2, :]], axis=1)
        lse = jnp.concatenate([lse_ref[0, 0:1, rows], lse_ref[0, 1:2, rows]], axis=1)
        both = by_head(qkv_ref[0, here, :] * scale)
        both_grad = by_head(grad)
        bias = bias_ref[:span, rows]
        scores = lax.dot_general(key_ref[:span, :], both, NT, preferred_element_type=F32)
        probs = jnp.exp(scores + jnp.concatenate([bias, bias], axis=1) - lse)
        prob_grad = lax.dot_general(
            value_ref[:span, :], both_grad, NT, preferred_element_type=F32
        )
        cot = (probs * (prob_grad - centre)).astype(BF)
        value_add = jnp.dot(probs.astype(BF), both_grad, preferred_element_type=F32)
        key_add = jnp.dot(cot, both, preferred_element_type=F32)
        if index == count - 1:
            value_grad_ref[...] = value_add
            key_grad_ref[...] = key_add
        else:
            value_grad_ref[:span, :] += value_add
            key_grad_ref[:span, :] += key_add
        turned = [
            jnp.dot(
                key_turned_ref[head * HD : (head + 1) * HD, :span],
                cot[:, head * shard : (head + 1) * shard],
                preferred_element_type=F32,
            )
            for head in range(2)
        ]
        query_grad = jnp.concatenate(turned, axis=0).T * HD**-0.5
        raw_ref[here, target(0)] = turn(query_grad, table_ref, here, -1.0).astype(BF)
    for index in range(count):
        rows = slice(index * shard, (index + 1) * shard)
        here = pl.ds(place(index), shard)
        raw_ref[here, target(1)] = turn(key_grad_ref[rows, :], table_ref, here, -1.0).astype(BF)
        raw_ref[here, target(2)] = value_grad_ref[rows, :].astype(BF)


def attend_back(me, segments, qkv, attended, grad, lse, table):
    _, group, local_width = qkv.shape
    count = 4
    pairs = local_width // LANES
    return pl.pallas_call(
        functools.partial(attend_back_kernel, count),
        name="attend_back",
        grid_spec=pltpu.PrefetchScalarGridSpec(
            num_scalar_prefetch=1,
            grid=(pairs,),
            in_specs=[
                pl.BlockSpec((group, 1), lambda p, me: (0, 0)),
                pl.BlockSpec((1, group), lambda p, me: (0, 0)),
                pl.BlockSpec((3, group, LANES), lambda p, me: (0, 0, p)),
                pl.BlockSpec((group, LANES), lambda p, me: (0, p)),
                pl.BlockSpec((group, LANES), lambda p, me: (0, p)),
                pl.BlockSpec((1, 8, group), lambda p, me: (p, 0, 0)),
                pl.BlockSpec((3, group, LANES), lambda p, me: (0, 0, 0)),
            ],
            out_specs=pl.BlockSpec((group, 3 * local_width), lambda p, me: (0, 0)),
            scratch_shapes=[
                pltpu.VMEM((group, group), F32),
                pltpu.VMEM((group, LANES), F32),
                pltpu.VMEM((group, LANES), F32),
                pltpu.VMEM((LANES, group), BF),
                pltpu.VMEM((group, LANES), BF),
                pltpu.VMEM((group, LANES), BF),
            ],
        ),
        out_shape=jax.ShapeDtypeStruct((group, 3 * local_width), BF),
        compiler_params=pltpu.CompilerParams(vmem_limit_bytes=48 * MIB),
        cost_estimate=LIGHT,
    )(me, segments[:, None], segments[None, :], qkv, attended, grad, lse, table)


def weight_grad(sets, pieces, cots, splits, depth):
    many = sets[0].shape[0]
    shard = pieces[0].shape[0]
    tokens = cots[0][0].shape[0]
    widths = [units for _, _, units in cots]
    share = depth // splits
    grouped = len(cots) * splits
    if depth % LANES:
        rows = jnp.concatenate(pieces, 0)
        results = []
        for blocks in sets:
            columns = [
                lax.dynamic_slice_in_dim(rows, blocks[index] * depth, depth, 1)
                for index in range(many)
            ]
            columns = jnp.concatenate(columns, 1)
            for (array, part, _), units in zip(cots, widths):
                products = lax.dot_general(
                    columns,
                    array[:, part * units : (part + 1) * units],
                    TN,
                    preferred_element_type=F32,
                ).astype(BF)
                products = products.reshape(many, splits, share, units)
                results += [
                    products[:, index].reshape(many * share, units) for index in range(splits)
                ]
        return results

    def kernel(blocks_ref, *refs):
        cots_refs = refs[len(pieces) : len(pieces) + len(cots)]
        out_refs, rows_ref = refs[len(pieces) + len(cots) : -1], refs[-1]
        for index, piece_ref in enumerate(refs[: len(pieces)]):
            rows_ref[index * shard : (index + 1) * shard, :] = piece_ref[...]
        products = [
            lax.dot_general(
                rows_ref[...], cots_ref[...], TN, preferred_element_type=F32
            ).astype(BF)
            for cots_ref in cots_refs
        ]
        for turn_index in range(len(sets)):

            @pl.when(pl.program_id(0) // many == turn_index)
            def _():
                mine = iter(out_refs[turn_index * grouped : (turn_index + 1) * grouped])
                for product in products:
                    for index in range(splits):
                        next(mine)[...] = product[index * share : (index + 1) * share]

    def out_spec(turn_index, units):
        return pl.BlockSpec(
            (share, units),
            lambda i, blocks: (jnp.clip(i - turn_index * many, 0, many - 1), 0),
        )

    def cots_spec(part, units):
        return pl.BlockSpec((tokens, units), lambda i, blocks: (0, part))

    order = [(t, units) for t in range(len(sets)) for units in widths for _ in range(splits)]
    return pl.pallas_call(
        kernel,
        name="weight_grad",
        grid_spec=pltpu.PrefetchScalarGridSpec(
            num_scalar_prefetch=1,
            grid=(len(sets) * many,),
            in_specs=[pl.BlockSpec((shard, depth), lambda i, blocks: (0, blocks[i]))] * len(pieces)
            + [cots_spec(part, units) for (_, part, _), units in zip(cots, widths)],
            out_specs=[out_spec(t, units) for t, units in order],
            scratch_shapes=[pltpu.VMEM((tokens, depth), BF)],
        ),
        out_shape=[jax.ShapeDtypeStruct((many * share, units), BF) for _, units in order],
        compiler_params=pltpu.CompilerParams(vmem_limit_bytes=60 * MIB),
        cost_estimate=LIGHT,
    )(jnp.concatenate(sets), *pieces, *[array for array, _, _ in cots])


def ring_add(groups):
    operands, specs, outs, plans = [], [], [], []
    for shape, entries in groups:
        sends = sum(final is None for _, final in entries)
        if sends:
            outs.append(jax.ShapeDtypeStruct((sends * shape[0], shape[1]), BF))
        message = len(outs) - 1
        sent = 0
        for pairs, final in entries:
            place = (message, sent * shape[0])
            if final is None:
                sent += 1
            else:
                outs.append(jax.ShapeDtypeStruct(shape, final))
                place = (len(outs) - 1, 0)
            plans.append((len(operands), len(pairs), place, shape[0]))
            for array, block in pairs:
                operands.append(array)
                specs.append(pl.BlockSpec(shape, lambda i, block=block: (block, 0)))

    def kernel(*refs):
        for start, count, (out, row), rows in plans:
            total = functools.reduce(
                jnp.add, [ref[...].astype(F32) for ref in refs[start : start + count]]
            )
            out_ref = refs[len(operands) + out]
            out_ref[row : row + rows, :] = total.astype(out_ref.dtype)

    return pl.pallas_call(
        kernel,
        name="ring_add",
        grid=(1,),
        in_specs=specs,
        out_specs=[pl.BlockSpec(o.shape, lambda i: (0, 0)) for o in outs],
        out_shape=outs,
        compiler_params=pltpu.CompilerParams(vmem_limit_bytes=48 * MIB),
        cost_estimate=LIGHT,
    )(*operands)


def turned(parts, scale):
    rows, units = parts[0].shape

    def kernel(scale_ref, *refs):
        whole = jnp.concatenate([ref[...] for ref in refs[:-1]], axis=0) * scale_ref[0]
        refs[-1][...] = whole.T

    return pl.pallas_call(
        kernel,
        name="turned",
        grid=(1,),
        in_specs=[pl.BlockSpec(memory_space=pltpu.SMEM)]
        + [pl.BlockSpec(part.shape, lambda i: (0, 0)) for part in parts],
        out_specs=pl.BlockSpec((units, rows * len(parts)), lambda i: (0, 0)),
        out_shape=jax.ShapeDtypeStruct((units, rows * len(parts)), F32),
        compiler_params=pltpu.CompilerParams(vmem_limit_bytes=48 * MIB),
        cost_estimate=LIGHT,
    )(scale, *parts)


def interleaved(first, second, scale):
    rows, columns = first.shape
    step = min(32, rows)

    def kernel(scale_ref, first_ref, second_ref, out_ref):
        out_ref[:, 0, :] = first_ref[...] * scale_ref[0]
        out_ref[:, 1, :] = second_ref[...] * scale_ref[0]

    return pl.pallas_call(
        kernel,
        name="interleaved",
        grid=(rows // step,),
        in_specs=[pl.BlockSpec(memory_space=pltpu.SMEM)]
        + [pl.BlockSpec((step, columns), lambda i: (i, 0))] * 2,
        out_specs=pl.BlockSpec((step, 2, columns), lambda i: (i, 0, 0)),
        out_shape=jax.ShapeDtypeStruct((rows, 2, columns), F32),
        compiler_params=pltpu.CompilerParams(vmem_limit_bytes=48 * MIB),
        cost_estimate=LIGHT,
    )(scale, first, second)


def barrier(value, *others):
    return lax.optimization_barrier((value, *others))[0]


class Order:
    def __init__(self):
        self.last = None

    def __call__(self, step, operand, *others, wait=()):
        if self.last is not None:
            operand = barrier(operand, self.last, *wait)
        result = step(operand, *others)
        self.last = jax.tree.leaves(result)[0]
        return result


class Reducer:
    def __init__(self, order, rounds, partner, along):
        self.order, self.rounds, self.partner, self.along = order, rounds, partner, along
        self.flying, self.rings = [], []
        self.popped = None
        self.kept, self.done, self.late = {}, {}, []

    def send(self, name, sent, kept=None):
        if self.popped is not None:
            sent = barrier(sent, self.popped)
        if kept is not None:
            self.kept[name] = kept
        self.flying.append((name, self.partner(sent)))

    def ring(self, name, kept, other):
        self._enter(name, [kept], F32)
        self._enter(name + "/other", [other], BF)

    def _enter(self, name, arrays, final):
        shape = (arrays[0].shape[0] // self.rounds, arrays[0].shape[1])
        self.rings.append(
            dict(name=name, arrays=arrays, shape=shape, step=0, carry=[], final=final)
        )

    def turn(self, pop=True):
        if pop and self.flying:
            name, got = self.flying.pop(0)
            self.popped = got
            self._enter(name, [self.kept.pop(name), got], F32)
        rings, self.rings = self.rings, []
        groups, members = [], []
        for group in self._groups(rings):
            shape = group[0]["shape"]
            entries = []
            for ring in group:
                end = ring["step"] == self.rounds - 1
                pairs = [(array, ring["step"]) for array in ring["arrays"]] + ring["carry"]
                entries.append((pairs, ring["final"] if end else None))
            groups.append((shape, entries))
            members.append(group)
        if not groups:
            return

        def step(first):
            pairs = groups[0][1][0][0]
            pairs[0] = (first, pairs[0][1])
            return ring_add(groups)

        outs = list(self.order(step, groups[0][1][0][0][0][0]))
        for (shape, entries), group in zip(groups, members):
            message = None
            if any(final is None for _, final in entries):
                message = self.along(outs.pop(0))
            sent = 0
            for ring, (_, final) in zip(group, entries):
                if final is None:
                    ring["carry"] = [(message, sent)]
                    ring["step"] += 1
                    sent += 1
                    self.rings.append(ring)
                else:
                    self._finish(ring["name"], outs.pop(0))

    def _groups(self, rings):
        for shape in dict.fromkeys(ring["shape"] for ring in rings):
            members = [ring for ring in rings if ring["shape"] == shape]
            most = max(1, GROUP_BYTES // (2 * shape[0] * shape[1]))
            count = -(-len(members) // most)
            size = -(-len(members) // count)
            for start in range(0, len(members), size):
                yield members[start : start + size]

    def _finish(self, name, result):
        if name.endswith("/other"):
            self.late.append((name.split("/")[0], self.partner(result)))
        else:
            self.done[name] = result

    def close(self):
        late, self.late = self.late, []
        for name, got in late:
            self.done[name] = self.order(lambda a, n=name: self.done[n] + a.astype(F32), got)

    def busy(self):
        return bool(self.flying or self.rings)


def local(
    n_dp,
    tokens,
    segment_ids,
    cotangent,
    w_qkv,
    qkv_bias,
    w_out,
    w_gate_up,
    w_down,
    norm_gains,
    norm_biases,
):
    shard, width = tokens.shape
    group = segment_ids.shape[0]
    local_width = w_out.shape[0]
    units = w_down.shape[0]
    n_tensor = group // shard
    n_ring = n_dp // 2
    me = lax.axis_index("tensor")
    data_index = lax.axis_index("dp")
    to_core = [(t, t ^ 1) for t in range(n_tensor)]
    to_x = [(t, t ^ 2) for t in range(n_tensor)]
    to_y = [(d, d ^ 1) for d in range(n_dp)]
    up_z = [(d, (d + 2) % n_dp) for d in range(n_dp)]
    order = Order()

    def core(value):
        return lax.ppermute(value, "tensor", to_core)

    def across(value):
        return lax.ppermute(value, "tensor", to_x)

    def over_dp(value, step):
        return lax.ppermute(value, "dp", [(d, d ^ (1 << step)) for d in range(n_dp)])

    dp_steps = (n_dp - 1).bit_length()

    def in_pieces(values):
        blocks = values.reshape((n_tensor, shard) + values.shape[1:])
        return jnp.concatenate(
            [lax.dynamic_index_in_dim(blocks, me ^ k, 0, False) for k in range(n_tensor)], 0
        )

    def stack(*pieces):
        return jnp.concatenate(pieces, 0)

    def rows_of(half, rows, w, dims):
        return order(lambda r, *more: pair_product(half, (r, *more), w, dims), *rows)

    def hop(pair):
        return pair[0], [core(pair[1])]

    def send_far(pair):
        mine, tiles = hop(pair)
        return across(order(lambda t: add_tiles(mine, (t,)), *tiles))

    ring_index = data_index // 2
    rings = jnp.stack([(ring_index - 1 - s + 2 * n_ring) % n_ring for s in range(n_ring)])
    keep_blocks = (2 * rings + data_index % 2).astype(jnp.int32)
    send_blocks = (2 * rings + 1 - data_index % 2).astype(jnp.int32)

    depth = width // n_dp

    def grad_of(sets, pieces, *cots, splits=1):
        def step(first):
            arrays = [(first,) + cots[0][1:], *cots[1:]]
            return weight_grad(sets, pieces, arrays, splits, depth)

        return order(step, cots[0][0])

    reducer = Reducer(
        order,
        n_ring,
        lambda value: lax.ppermute(value, "dp", to_y),
        lambda value: lax.ppermute(value, "dp", up_z),
    )

    me_one = me[None].astype(jnp.int32)
    gains = [norm_gains[index : index + 1] for index in range(2)]
    shifts = [norm_biases[index : index + 1] for index in range(2)]
    live = (segment_ids >= 0).astype(F32)
    live_rows = lax.dynamic_slice_in_dim(live, me * shard, shard, 0)

    one_own = order(norm_rows, tokens, gains[0], shifts[0])
    one_far = across(one_own)
    one_near = core(one_own)
    out_cot = (cotangent.astype(F32) * live_rows[:, None]).astype(BF)
    in_near = core(out_cot)
    live_total = jnp.sum(live)[None]
    table = rope_tables(in_pieces(positions_of(segment_ids)))
    w_flat = w_gate_up.reshape(width, 2 * units)
    w_split = jnp.transpose(w_qkv, (1, 0, 2))
    bias_rows = qkv_bias[:, None, :]
    qkv = order(
        lambda a: project(0, a, one_near, w_split, bias_rows, table, None),
        one_own, wait=(w_flat, table),
    )
    one_far = barrier(one_far, qkv)
    one_last = core(one_far)
    in_far = across(barrier(out_cot, one_far))
    qkv = order(
        lambda a: project(1, a, one_last, w_split, bias_rows, table, qkv), one_far
    )
    attended, lse = order(lambda q: attend(me_one, segment_ids, q), qkv)
    attended = barrier(attended, in_far)
    branch_far = send_far(rows_of(1, (attended,), w_out, NN))
    near, tiles = hop(rows_of(0, (attended,), w_out, NN))
    in_far = barrier(in_far, attended)
    in_last = core(in_far)
    incoming = (out_cot, in_near, in_far, in_last)
    incoming_full = order(stack, *incoming)
    act_grad = order(
        lambda r: lax.dot_general(r, w_down, NT, preferred_element_type=F32), incoming_full
    )
    live_total = order(jnp.add, over_dp(live_total, 0), live_total)
    hidden, two_own = order(
        lambda t: add_norm_rows(t, near, branch_far, tiles, gains[1], shifts[1]), tokens
    )
    two_far = across(two_own)
    two_near = core(two_own)
    fed = order(lambda a: feed(0, a, two_near, w_flat, act_grad, None), two_own)
    for step in range(1, dp_steps):
        live_total = order(jnp.add, over_dp(live_total, step), live_total)
    live_total = live_total[0]
    two_far = barrier(two_far, order.last)
    two_last = core(two_far)
    activated, gate_cot, up_cot = order(
        lambda a: feed(1, a, two_last, w_flat, act_grad, fed), two_far
    )
    two = (two_own, two_near, two_far, two_last)
    one = (one_own, one_near, one_far, one_last)

    down_sent = grad_of([send_blocks], incoming, (activated, 0, units), splits=2)
    reducer.send("down1", down_sent[1])
    (gate_sent,) = grad_of([send_blocks], two, (gate_cot, 0, units))
    down_kept = grad_of([keep_blocks], incoming, (activated, 0, units), splits=2)
    reducer.kept["down1"] = down_kept[1]
    reducer.ring("down0", down_kept[0], down_sent[0])
    second_far_pair = rows_of(1, (gate_cot, up_cot), w_flat, NT)
    reducer.turn(pop=False)
    second_near_pair = rows_of(0, (gate_cot, up_cot), w_flat, NT)

    reducer.send("gate", gate_sent)
    reducer.turn()
    second_far = send_far(second_far_pair)
    second_near, second_tiles = hop(second_near_pair)
    (reducer.kept["gate"],) = grad_of([keep_blocks], two, (gate_cot, 0, units))
    up_grads = grad_of([send_blocks, keep_blocks], two, (up_cot, 0, units))
    reducer.send("up", *up_grads)
    reducer.turn(pop=False)
    hidden_grad, branch_own, sums_two = order(
        lambda h: norm_rows_back(
            h, second_near, second_far, second_tiles, out_cot, gains[1], (F32, BF)
        ),
        hidden,
    )
    branch_far = across(branch_own)
    branch_near = core(branch_own)
    down_pair = rows_of(1, (activated,), w_down, NN)
    down_near_pair = rows_of(0, (activated,), w_down, NN)

    reducer.turn()
    branch_last = core(barrier(branch_far, order.last))
    branch = (branch_own, branch_near, branch_far, branch_last)
    branch_full = order(stack, *branch)
    attended_grad = order(
        lambda r: lax.dot_general(r, w_out, NT, preferred_element_type=F32).astype(BF),
        branch_full,
    )
    raw_cot = order(
        lambda g: attend_back(me_one, segment_ids, qkv, attended, g, lse, table), attended_grad
    )
    reducer.turn(pop=False)
    query_key_grads = grad_of([send_blocks, keep_blocks], one, (raw_cot, 0, 2 * local_width))
    reducer.send("query_key", *query_key_grads)

    reducer.turn()
    out_grads = grad_of([send_blocks, keep_blocks], branch, (attended, 0, local_width))
    reducer.send("out", *out_grads)
    value_grads = grad_of([send_blocks, keep_blocks], one, (raw_cot, 2, local_width))
    first_far_pair = rows_of(1, (raw_cot,), w_split, NT)
    first_near_pair = rows_of(0, (raw_cot,), w_split, NT)
    bias_sum = order(lambda r: jnp.sum(r.astype(F32), axis=0).reshape(3, local_width), raw_cot)

    reducer.turn(pop=False)
    reducer.turn()
    reducer.send("value", *value_grads)
    first_far = send_far(first_far_pair)
    first_near, first_tiles = hop(first_near_pair)

    reducer.turn()
    input_grad, sums_one = order(
        lambda t: norm_rows_back(
            t, first_near, first_far, first_tiles, hidden_grad, gains[0], (F32,)
        ),
        tokens,
    )
    down_far = send_far(down_pair)
    down_near, down_tiles = hop(down_near_pair)
    rows_sum = jnp.concatenate([sums_one[:1], sums_two[:1], sums_one[1:], sums_two[1:]], 0)
    rows_near = core(rows_sum)

    reducer.turn()
    reducer.close()
    rows_sum = order(jnp.add, rows_near, rows_sum)
    rows_far = across(rows_sum)
    rows_sum = order(jnp.add, rows_far, rows_sum)
    small = jnp.concatenate([rows_sum.reshape(-1), bias_sum.reshape(-1)])
    scaled = {}
    scale = (1.0 / live_total)[None]

    def finish():
        done = reducer.done
        for name, parts in (("down", ("down0", "down1")), ("out", ("out",))):
            if name not in scaled and all(part in done for part in parts):
                scaled[name] = order(
                    lambda first, rest=parts[1:]: turned([first, *[done[r] for r in rest]], scale),
                    done[parts[0]],
                )
        if "gate_up" not in scaled and "gate" in done and "up" in done:
            scaled["gate_up"] = order(
                lambda g: interleaved(g, done["up"], scale), done["gate"]
            )
        for name in ("query_key", "value"):
            if name not in scaled and name in done:
                scaled[name] = done[name] * scale

    for step in range(dp_steps):
        small_far = over_dp(small, step)
        reducer.turn()
        small = order(jnp.add, small_far, small)
        finish()
        if step == 1:
            output = order(lambda h: add_rows(h, down_near, down_far, down_tiles), hidden)
    small = small * scale
    rows_sum = small[: 4 * width].reshape(4, width)
    bias_sum = small[4 * width :].reshape(3, local_width)
    while reducer.busy():
        reducer.turn()
        finish()
    return (
        output,
        input_grad,
        jnp.concatenate([scaled["query_key"], scaled["value"]], 1).reshape(-1, 3, local_width),
        bias_sum,
        scaled["out"],
        scaled["gate_up"],
        scaled["down"],
        rows_sum[:2],
        rows_sum[2:],
    )


def solution(mesh):
    in_specs = (
        P(("dp", "tensor"), None),
        P("dp"),
        P(("dp", "tensor"), None),
        P(None, None, "tensor"),
        P(None, "tensor"),
        P("tensor", None),
        P(None, None, "tensor"),
        P("tensor", None),
        P(),
        P(),
    )
    out_specs = (
        P(("dp", "tensor"), None),
        P(("dp", "tensor"), None),
        P("dp", None, "tensor"),
        P(None, "tensor"),
        P("tensor", "dp"),
        P("dp", None, "tensor"),
        P("tensor", "dp"),
        P(),
        P(),
    )
    return jax.shard_map(
        functools.partial(local, mesh.shape["dp"]),
        mesh=mesh,
        in_specs=in_specs,
        out_specs=out_specs,
        check_vma=False,
    )
```

```python
import functools

import jax
import jax.numpy as jnp
from jax import lax
from jax.experimental import pallas as pl
from jax.experimental.pallas import tpu as pltpu
from jax.sharding import PartitionSpec as P

HD = 64
ROT = 16
LANES = 128
epsilon = 1e-05
rope_base = 10000.0
BF = jnp.bfloat16
F32 = jnp.float32
MIB = 1 << 20
GROUP_BYTES = 1_200_000
LIGHT = pl.CostEstimate(flops=1, bytes_accessed=1, transcendentals=0)
NT = (((1,), (1,)), ((), ()))
TN = (((0,), (0,)), ((), ()))
NN = (((1,), (0,)), ((), ()))


def positions_of(segments):
    row_index = jnp.arange(segments.shape[0], dtype=jnp.int32)
    previous = jnp.concatenate([jnp.full((1,), -2, jnp.int32), segments[:-1]])
    starts = jnp.where(segments != previous, row_index, 0)
    return row_index - lax.cummax(starts, axis=0)


def rope_tables(positions):
    half = ROT // 2
    dim = jnp.arange(LANES) % HD
    exponent = (dim % half).astype(F32) * 2.0 / ROT
    frequency = jnp.where(dim < ROT, rope_base ** (-exponent), 0.0)
    angles = positions.astype(F32)[:, None] * frequency[None, :]
    cosine, sine = jnp.cos(angles), jnp.sin(angles)
    lower = jnp.where(dim < half, -sine, 0.0)
    upper = jnp.where((dim >= half) & (dim < ROT), sine, 0.0)
    return jnp.stack([cosine, lower, upper])


def turn(block, table_ref, rows, sign):
    half = ROT // 2
    back = pltpu.roll(block, LANES - half, 1)
    ahead = pltpu.roll(block, half, 1)
    return (
        block * table_ref[0, rows, :]
        + sign * (back * table_ref[1, rows, :] + ahead * table_ref[2, rows, :])
    )


def project_kernel(
    first_ref, second_ref, w_ref, bias_ref, table_ref, old_ref, out_ref, rows_ref
):
    shard = first_ref.shape[0]

    @pl.when(pl.program_id(0) == 0)
    def _():
        rows_ref[:shard, :] = first_ref[...]
        rows_ref[shard:, :] = second_ref[...]

    raw = jnp.dot(rows_ref[...], w_ref[0], preferred_element_type=F32) + bias_ref[0]

    @pl.when(pl.program_id(0) < 2)
    def _():
        for start in range(0, raw.shape[1], LANES):
            piece = turn(raw[:, start : start + LANES], table_ref, slice(None), 1.0)
            out_ref[0, :, start : start + LANES] = piece.astype(BF)

    @pl.when(pl.program_id(0) == 2)
    def _():
        out_ref[0] = raw.astype(BF)


def project(half, first, second, w, bias, table, old):
    shard, width = first.shape
    local_width = w.shape[2]
    whole = jax.ShapeDtypeStruct((3, 4 * shard, local_width), BF)
    kernel = project_kernel
    operands = [first, second, w, bias, table]
    specs = [
        pl.BlockSpec((shard, width), lambda c: (0, 0)),
        pl.BlockSpec((shard, width), lambda c: (0, 0)),
        pl.BlockSpec((1, width, local_width), lambda c: (c, 0, 0)),
        pl.BlockSpec((1, 1, local_width), lambda c: (c, 0, 0)),
        pl.BlockSpec((3, 2 * shard, LANES), lambda c: (0, half, 0)),
    ]
    aliases = {}
    if old is None:

        def kernel(a, b, c, d, e, out_ref, rows_ref):
            project_kernel(a, b, c, d, e, None, out_ref, rows_ref)

    else:
        operands.append(old)
        specs.append(pl.BlockSpec(memory_space=pl.ANY))
        aliases = {5: 0}
    return pl.pallas_call(
        kernel,
        name="project",
        grid=(3,),
        in_specs=specs,
        out_specs=pl.BlockSpec((1, 2 * shard, local_width), lambda c: (c, half, 0)),
        out_shape=whole,
        input_output_aliases=aliases,
        scratch_shapes=[pltpu.VMEM((2 * shard, width), BF)],
        compiler_params=pltpu.CompilerParams(vmem_limit_bytes=48 * MIB),
        cost_estimate=LIGHT,
    )(*operands)


def feed_kernel(
    first_ref, second_ref, gate_w_ref, up_w_ref, act_grad_ref,
    act_ref, gate_ref, up_ref, rows_ref, w_ref,
):
    shard = first_ref.shape[0]

    @pl.when(pl.program_id(0) == 0)
    def _():
        rows_ref[:shard, :] = first_ref[...]
        rows_ref[shard:, :] = second_ref[...]

    w_ref[:, :LANES] = gate_w_ref[...]
    w_ref[:, LANES:] = up_w_ref[...]
    product = jnp.dot(rows_ref[...], w_ref[...], preferred_element_type=F32)
    gate, up = product[:, :LANES], product[:, LANES:]
    s = jax.nn.sigmoid(gate)
    silu = gate * s
    act_grad = act_grad_ref[...].astype(F32)
    act_ref[...] = (silu * up).astype(BF)
    gate_ref[...] = (act_grad * up * (s + silu * (1.0 - s))).astype(BF)
    up_ref[...] = (act_grad * silu).astype(BF)


def feed(half, first, second, w, act_grad, old):
    shard, width = first.shape
    units = w.shape[1] // 2
    tiles = units // LANES

    operands = [first, second, w, w, act_grad]
    specs = [
        pl.BlockSpec((shard, width), lambda j: (0, 0)),
        pl.BlockSpec((shard, width), lambda j: (0, 0)),
        pl.BlockSpec((width, LANES), lambda j: (0, j)),
        pl.BlockSpec((width, LANES), lambda j: (0, tiles + j)),
        pl.BlockSpec((2 * shard, LANES), lambda j: (half, j)),
    ]
    kernel = feed_kernel
    aliases = {}
    if old is not None:

        def kernel(*refs):
            feed_kernel(*refs[:5], *refs[8:])

        operands += list(old)
        specs += [pl.BlockSpec(memory_space=pl.ANY)] * 3
        aliases = {5: 0, 6: 1, 7: 2}
    return pl.pallas_call(
        kernel,
        name="feed",
        grid=(tiles,),
        in_specs=specs,
        out_specs=[pl.BlockSpec((2 * shard, LANES), lambda j: (half, j))] * 3,
        out_shape=[jax.ShapeDtypeStruct((4 * shard, units), BF)] * 3,
        input_output_aliases=aliases,
        scratch_shapes=[pltpu.VMEM((2 * shard, width), BF), pltpu.VMEM((width, 2 * LANES), BF)],
        compiler_params=pltpu.CompilerParams(vmem_limit_bytes=60 * MIB),
        cost_estimate=LIGHT,
    )(*operands)


def pair_product(half, rows, w, dims):
    group = rows[0].shape[0]
    shard = group // 4
    depth = sum(r.shape[1] for r in rows)
    turned = dims is NT
    width = w.shape[-2] if turned else w.shape[-1]
    tile = min(512, width)
    if w.ndim == 3:
        w_spec = pl.BlockSpec((w.shape[0], tile, w.shape[2]), lambda j: (0, j, 0))
    elif turned:
        w_spec = pl.BlockSpec((tile, depth), lambda j: (j, 0))
    else:
        w_spec = pl.BlockSpec((depth, tile), lambda j: (0, j))

    def kernel(*refs):
        rows_refs, w_ref = refs[: len(rows)], refs[len(rows)]
        first_ref, second_ref = refs[len(rows) + 1 :]
        if w.ndim == 3:
            part = w.shape[2]
            product = sum(
                lax.dot_general(
                    rows_refs[0][:, c * part : (c + 1) * part],
                    w_ref[c],
                    dims,
                    preferred_element_type=F32,
                )
                for c in range(w.shape[0])
            )
        elif turned:
            product, start = 0.0, 0
            for rows_ref in rows_refs:
                end = start + rows_ref.shape[1]
                product = product + lax.dot_general(
                    rows_ref[...], w_ref[:, start:end], dims, preferred_element_type=F32
                )
                start = end
        else:
            product = lax.dot_general(
                rows_refs[0][...], w_ref[...], dims, preferred_element_type=F32
            )
        product = product.astype(BF)
        first_ref[...] = product[:shard]
        second_ref[...] = product[shard:]

    return pl.pallas_call(
        kernel,
        name="pair_product",
        grid=(width // tile,),
        in_specs=[pl.BlockSpec((2 * shard, r.shape[1]), lambda j: (half, 0)) for r in rows]
        + [w_spec],
        out_specs=[pl.BlockSpec((shard, tile), lambda j: (0, j))] * 2,
        out_shape=[jax.ShapeDtypeStruct((shard, width), BF)] * 2,
        compiler_params=pltpu.CompilerParams(vmem_limit_bytes=48 * MIB),
        cost_estimate=LIGHT,
    )(*rows, w)


def centre_rows(values):
    average = jnp.mean(values, axis=-1, keepdims=True)
    centered = values - average
    variance = jnp.mean(centered * centered, axis=-1, keepdims=True)
    spread = lax.rsqrt(variance + epsilon)
    return centered * spread, spread


ROW_STEP = 128


def row_call(kernel, shard, width, inputs, per_row, outs):
    step = min(ROW_STEP, shard)
    specs = [
        pl.BlockSpec((step, a.shape[1]), lambda i: (i, 0))
        if rowwise
        else pl.BlockSpec(a.shape, lambda i: (0, 0))
        for a, rowwise in zip(inputs, per_row)
    ]
    out_specs = [
        pl.BlockSpec((step, width), lambda i: (i, 0))
        if o.shape[0] == shard
        else pl.BlockSpec(o.shape, lambda i: (0, 0))
        for o in outs
    ]
    return pl.pallas_call(
        kernel,
        name="row_call",
        grid=(shard // step,),
        in_specs=specs,
        out_specs=out_specs,
        out_shape=outs,
        compiler_params=pltpu.CompilerParams(vmem_limit_bytes=48 * MIB),
        cost_estimate=LIGHT,
    )(*inputs)


def norm_rows(tokens, gain, shift):
    def kernel(tokens_ref, gain_ref, shift_ref, out_ref):
        hat, _ = centre_rows(tokens_ref[...].astype(F32))
        out_ref[...] = (hat * gain_ref[...] + shift_ref[...]).astype(BF)

    shard, width = tokens.shape
    return row_call(
        kernel, shard, width, (tokens, gain, shift), (1, 0, 0),
        [jax.ShapeDtypeStruct((shard, width), BF)],
    )[0]


def total_of(own_ref, far_ref, tile_refs):
    tiles = jnp.concatenate([ref[...].astype(F32) for ref in tile_refs], axis=1)
    return own_ref[...].astype(F32) + tiles + far_ref[...].astype(F32)


def add_tiles(own, tiles):
    def kernel(own_ref, *refs):
        *tile_refs, out_ref = refs
        tiles = jnp.concatenate([ref[...].astype(F32) for ref in tile_refs], axis=1)
        out_ref[...] = (own_ref[...].astype(F32) + tiles).astype(BF)

    return row_call(
        kernel, *own.shape, (own, *tiles), (1,) * (1 + len(tiles)),
        [jax.ShapeDtypeStruct(own.shape, BF)],
    )[0]


def add_rows(values, own, far, tiles):
    def kernel(values_ref, own_ref, far_ref, *refs):
        *tile_refs, out_ref = refs
        total = values_ref[...] + total_of(own_ref, far_ref, tile_refs)
        out_ref[...] = total.astype(BF)

    return row_call(
        kernel, *own.shape, (values, own, far, *tiles), (1,) * (3 + len(tiles)),
        [jax.ShapeDtypeStruct(own.shape, BF)],
    )[0]


def add_norm_rows(tokens, own, far, tiles, gain, shift):
    def kernel(tokens_ref, own_ref, far_ref, gain_ref, shift_ref, *refs):
        *tile_refs, hidden_ref, out_ref = refs
        hidden = tokens_ref[...].astype(F32) + total_of(own_ref, far_ref, tile_refs)
        hidden_ref[...] = hidden
        hat, _ = centre_rows(hidden)
        out_ref[...] = (hat * gain_ref[...] + shift_ref[...]).astype(BF)

    shard, width = tokens.shape
    return row_call(
        kernel, shard, width, (tokens, own, far, gain, shift, *tiles),
        (1, 1, 1, 0, 0) + (1,) * len(tiles),
        [jax.ShapeDtypeStruct((shard, width), F32), jax.ShapeDtypeStruct((shard, width), BF)],
    )


def norm_rows_back(values, own, far, tiles, base, gain, dtypes):
    def kernel(values_ref, own_ref, far_ref, base_ref, gain_ref, *refs):
        tile_refs, grad_refs, sums_ref = refs[: len(tiles)], refs[len(tiles) : -1], refs[-1]
        hat, spread = centre_rows(values_ref[...].astype(F32))
        grad = total_of(own_ref, far_ref, tile_refs)
        scaled = grad * gain_ref[...]
        mean_scaled = jnp.mean(scaled, axis=-1, keepdims=True)
        mean_hat = jnp.mean(scaled * hat, axis=-1, keepdims=True)
        result = base_ref[...].astype(F32) + spread * (scaled - mean_scaled - hat * mean_hat)
        for ref in grad_refs:
            ref[...] = result.astype(ref.dtype)
        sums = jnp.concatenate(
            [
                jnp.sum(grad * hat, axis=0, keepdims=True),
                jnp.sum(grad, axis=0, keepdims=True),
            ],
            0,
        )

        @pl.when(pl.program_id(0) == 0)
        def _():
            sums_ref[...] = sums

        @pl.when(pl.program_id(0) > 0)
        def _():
            sums_ref[...] += sums

    shard, width = values.shape
    return row_call(
        kernel, shard, width, (values, own, far, base, gain, *tiles),
        (1, 1, 1, 1, 0) + (1,) * len(tiles),
        [jax.ShapeDtypeStruct((shard, width), d) for d in dtypes]
        + [jax.ShapeDtypeStruct((2, width), F32)],
    )


def head_lanes(shape, head):
    lane = lax.broadcasted_iota(jnp.int32, shape, 1)
    return (lane < HD) if head == 0 else (lane >= HD)


def attend_kernel(
    count, me_ref, column_ref, row_ref, low_ref, out_ref, lse_ref, bias_ref, key_ref, value_ref
):
    me = me_ref[0]
    shard = column_ref.shape[0] // count

    def place(index):
        return pl.multiple_of((index ^ me) * shard, shard)

    @pl.when(pl.program_id(0) == 0)
    def _():
        for index in range(count):
            span = (index + 1) * shard
            rows = slice(index * shard, span)
            own = lax.broadcasted_iota(jnp.int32, (shard, span), 0) + index * shard
            other = lax.broadcasted_iota(jnp.int32, (shard, span), 1)
            allowed = (column_ref[rows, :] == row_ref[:, :span]) & (other <= own)
            bias_ref[rows, :span] = jnp.where(allowed, 0.0, -1e30)

    for index in range(count):
        rows = slice(index * shard, (index + 1) * shard)
        here = pl.ds(place(index), shard)
        key_ref[rows, :] = low_ref[1, here, :]
        value_ref[rows, :] = low_ref[2, here, :]
    lane = lax.broadcasted_iota(jnp.int32, (shard, LANES), 1)
    for index in range(count):
        span = (index + 1) * shard
        rows = slice(index * shard, span)
        query = low_ref[0, pl.ds(place(index), shard), :] * jnp.asarray(HD**-0.5, BF)
        both = jnp.concatenate(
            [jnp.where(head_lanes(query.shape, head), query, 0) for head in range(2)], axis=0
        )
        scores = lax.dot_general(both, key_ref[:span, :], NT, preferred_element_type=F32)
        scores = scores.reshape(2, shard, span) + bias_ref[rows, :span][None]
        largest = jnp.max(scores, axis=2, keepdims=True)
        lifted = jnp.exp(scores - largest)
        total = jnp.sum(lifted, axis=2, keepdims=True)
        acc = jnp.dot(
            lifted.astype(BF).reshape(2 * shard, span), value_ref[:span, :],
            preferred_element_type=F32,
        ).reshape(2, shard, LANES) / total
        out_ref[pl.ds(place(index), shard), :] = jnp.where(lane < HD, acc[0], acc[1]).astype(BF)
        sums = largest + jnp.log(total)
        wide = jnp.where(lane == 0, sums[0], jnp.where(lane == 1, sums[1], 0.0))
        lse_ref[0, :, rows] = wide.T[:8, :]


def attend(me, segments, qkv):
    _, group, local_width = qkv.shape
    count = 4
    pairs = local_width // LANES

    kernel = functools.partial(attend_kernel, count)
    return pl.pallas_call(
        kernel,
        name="attend",
        grid_spec=pltpu.PrefetchScalarGridSpec(
            num_scalar_prefetch=1,
            grid=(pairs,),
            in_specs=[
                pl.BlockSpec((group, 1), lambda p, me: (0, 0)),
                pl.BlockSpec((1, group), lambda p, me: (0, 0)),
                pl.BlockSpec((3, group, LANES), lambda p, me: (0, 0, p)),
            ],
            out_specs=[
                pl.BlockSpec((group, LANES), lambda p, me: (0, p)),
                pl.BlockSpec((1, 8, group), lambda p, me: (p, 0, 0)),
            ],
            scratch_shapes=[
                pltpu.VMEM((group, group), F32),
                pltpu.VMEM((group, LANES), BF),
                pltpu.VMEM((group, LANES), BF),
            ],
        ),
        out_shape=[
            jax.ShapeDtypeStruct((group, local_width), BF),
            jax.ShapeDtypeStruct((pairs, 8, group), F32),
        ],
        compiler_params=pltpu.CompilerParams(vmem_limit_bytes=48 * MIB),
        cost_estimate=LIGHT,
    )(me, segments[:, None], segments[None, :], qkv)


def attend_back_kernel(
    count, me_ref, column_ref, row_ref, qkv_ref, out_ref, grad_ref, lse_ref, table_ref,
    raw_ref, bias_ref, key_grad_ref, value_grad_ref, key_turned_ref, key_ref, value_ref,
):
    me = me_ref[0]
    pair = pl.program_id(0)
    group = column_ref.shape[0]
    shard = group // count
    local_width = raw_ref.shape[1] // 3
    scale = jnp.asarray(HD**-0.5, BF)

    def place(index):
        return pl.multiple_of((index ^ me) * shard, shard)

    def target(part):
        return pl.ds(pl.multiple_of(part * local_width + pair * LANES, LANES), LANES)

    @pl.when(pair == 0)
    def _():
        for index in range(count):
            rows = slice(index * shard, group)
            keys = lax.broadcasted_iota(jnp.int32, (shard, group - index * shard), 0)
            queries = lax.broadcasted_iota(jnp.int32, (shard, group - index * shard), 1)
            own = slice(index * shard, (index + 1) * shard)
            allowed = (column_ref[own, :] == row_ref[:, rows]) & (keys <= queries)
            bias_ref[own, rows] = jnp.where(allowed, 0.0, -1e30)

    for index in range(count):
        rows = slice(index * shard, (index + 1) * shard)
        here = pl.ds(place(index), shard)
        keys = qkv_ref[1, here, :]
        key_ref[rows, :] = keys
        value_ref[rows, :] = qkv_ref[2, here, :]
        key_turned_ref[:, rows] = keys.astype(F32).T.astype(BF)

    sub = lax.broadcasted_iota(jnp.int32, (8, LANES), 0)
    lane = lax.broadcasted_iota(jnp.int32, (8, LANES), 1)
    chooser = jnp.where((lane // HD) == sub, 1.0, 0.0)

    def by_head(value):
        return jnp.concatenate(
            [jnp.where(head_lanes(value.shape, head), value, 0) for head in range(2)], axis=0
        )

    for index in reversed(range(count)):
        span = (index + 1) * shard
        rows = slice(index * shard, span)
        here = pl.ds(place(index), shard)
        grad = grad_ref[here, :]
        product = grad.astype(F32) * out_ref[here, :].astype(F32)
        centres = lax.dot_general(
            chooser, product, NT, precision=lax.Precision.HIGHEST, preferred_element_type=F32
        )
        centre = jnp.concatenate([centres[0:1, :], centres[1:2, :]], axis=1)
        lse = jnp.concatenate([lse_ref[0, 0:1, rows], lse_ref[0, 1:2, rows]], axis=1)
        both = by_head(qkv_ref[0, here, :] * scale)
        both_grad = by_head(grad)
        bias = bias_ref[:span, rows]
        scores = lax.dot_general(key_ref[:span, :], both, NT, preferred_element_type=F32)
        probs = jnp.exp(scores + jnp.concatenate([bias, bias], axis=1) - lse)
        prob_grad = lax.dot_general(
            value_ref[:span, :], both_grad, NT, preferred_element_type=F32
        )
        cot = (probs * (prob_grad - centre)).astype(BF)
        value_add = jnp.dot(probs.astype(BF), both_grad, preferred_element_type=F32)
        key_add = jnp.dot(cot, both, preferred_element_type=F32)
        if index == count - 1:
            value_grad_ref[...] = value_add
            key_grad_ref[...] = key_add
        else:
            value_grad_ref[:span, :] += value_add
            key_grad_ref[:span, :] += key_add
        turned = [
            jnp.dot(
                key_turned_ref[head * HD : (head + 1) * HD, :span],
                cot[:, head * shard : (head + 1) * shard],
                preferred_element_type=F32,
            )
            for head in range(2)
        ]
        query_grad = jnp.concatenate(turned, axis=0).T * HD**-0.5
        raw_ref[here, target(0)] = turn(query_grad, table_ref, here, -1.0).astype(BF)
    for index in range(count):
        rows = slice(index * shard, (index + 1) * shard)
        here = pl.ds(place(index), shard)
        raw_ref[here, target(1)] = turn(key_grad_ref[rows, :], table_ref, here, -1.0).astype(BF)
        raw_ref[here, target(2)] = value_grad_ref[rows, :].astype(BF)


def attend_back(me, segments, qkv, attended, grad, lse, table):
    _, group, local_width = qkv.shape
    count = 4
    pairs = local_width // LANES
    return pl.pallas_call(
        functools.partial(attend_back_kernel, count),
        name="attend_back",
        grid_spec=pltpu.PrefetchScalarGridSpec(
            num_scalar_prefetch=1,
            grid=(pairs,),
            in_specs=[
                pl.BlockSpec((group, 1), lambda p, me: (0, 0)),
                pl.BlockSpec((1, group), lambda p, me: (0, 0)),
                pl.BlockSpec((3, group, LANES), lambda p, me: (0, 0, p)),
                pl.BlockSpec((group, LANES), lambda p, me: (0, p)),
                pl.BlockSpec((group, LANES), lambda p, me: (0, p)),
                pl.BlockSpec((1, 8, group), lambda p, me: (p, 0, 0)),
                pl.BlockSpec((3, group, LANES), lambda p, me: (0, 0, 0)),
            ],
            out_specs=pl.BlockSpec((group, 3 * local_width), lambda p, me: (0, 0)),
            scratch_shapes=[
                pltpu.VMEM((group, group), F32),
                pltpu.VMEM((group, LANES), F32),
                pltpu.VMEM((group, LANES), F32),
                pltpu.VMEM((LANES, group), BF),
                pltpu.VMEM((group, LANES), BF),
                pltpu.VMEM((group, LANES), BF),
            ],
        ),
        out_shape=jax.ShapeDtypeStruct((group, 3 * local_width), BF),
        compiler_params=pltpu.CompilerParams(vmem_limit_bytes=48 * MIB),
        cost_estimate=LIGHT,
    )(me, segments[:, None], segments[None, :], qkv, attended, grad, lse, table)


def weight_grad(sets, pieces, cots, splits, depth):
    many = sets[0].shape[0]
    shard = pieces[0].shape[0]
    tokens = cots[0][0].shape[0]
    widths = [units for _, _, units in cots]
    share = depth // splits
    grouped = len(cots) * splits
    if depth % LANES:
        rows = jnp.concatenate(pieces, 0)
        results = []
        for blocks in sets:
            columns = [
                lax.dynamic_slice_in_dim(rows, blocks[index] * depth, depth, 1)
                for index in range(many)
            ]
            columns = jnp.concatenate(columns, 1)
            for (array, part, _), units in zip(cots, widths):
                products = lax.dot_general(
                    columns,
                    array[:, part * units : (part + 1) * units],
                    TN,
                    preferred_element_type=F32,
                ).astype(BF)
                products = products.reshape(many, splits, share, units)
                results += [
                    products[:, index].reshape(many * share, units) for index in range(splits)
                ]
        return results

    def kernel(blocks_ref, *refs):
        cots_refs = refs[len(pieces) : len(pieces) + len(cots)]
        out_refs, rows_ref = refs[len(pieces) + len(cots) : -1], refs[-1]
        for index, piece_ref in enumerate(refs[: len(pieces)]):
            rows_ref[index * shard : (index + 1) * shard, :] = piece_ref[...]
        products = [
            lax.dot_general(
                rows_ref[...], cots_ref[...], TN, preferred_element_type=F32
            ).astype(BF)
            for cots_ref in cots_refs
        ]
        for turn_index in range(len(sets)):

            @pl.when(pl.program_id(0) // many == turn_index)
            def _():
                mine = iter(out_refs[turn_index * grouped : (turn_index + 1) * grouped])
                for product in products:
                    for index in range(splits):
                        next(mine)[...] = product[index * share : (index + 1) * share]

    def out_spec(turn_index, units):
        return pl.BlockSpec(
            (share, units),
            lambda i, blocks: (jnp.clip(i - turn_index * many, 0, many - 1), 0),
        )

    def cots_spec(part, units):
        return pl.BlockSpec((tokens, units), lambda i, blocks: (0, part))

    order = [(t, units) for t in range(len(sets)) for units in widths for _ in range(splits)]
    return pl.pallas_call(
        kernel,
        name="weight_grad",
        grid_spec=pltpu.PrefetchScalarGridSpec(
            num_scalar_prefetch=1,
            grid=(len(sets) * many,),
            in_specs=[pl.BlockSpec((shard, depth), lambda i, blocks: (0, blocks[i]))] * len(pieces)
            + [cots_spec(part, units) for (_, part, _), units in zip(cots, widths)],
            out_specs=[out_spec(t, units) for t, units in order],
            scratch_shapes=[pltpu.VMEM((tokens, depth), BF)],
        ),
        out_shape=[jax.ShapeDtypeStruct((many * share, units), BF) for _, units in order],
        compiler_params=pltpu.CompilerParams(vmem_limit_bytes=60 * MIB),
        cost_estimate=LIGHT,
    )(jnp.concatenate(sets), *pieces, *[array for array, _, _ in cots])


def ring_add(groups):
    operands, specs, outs, plans = [], [], [], []
    for shape, entries in groups:
        sends = sum(final is None for _, final in entries)
        if sends:
            outs.append(jax.ShapeDtypeStruct((sends * shape[0], shape[1]), BF))
        message = len(outs) - 1
        sent = 0
        for pairs, final in entries:
            place = (message, sent * shape[0])
            if final is None:
                sent += 1
            else:
                outs.append(jax.ShapeDtypeStruct(shape, final))
                place = (len(outs) - 1, 0)
            plans.append((len(operands), len(pairs), place, shape[0]))
            for array, block in pairs:
                operands.append(array)
                specs.append(pl.BlockSpec(shape, lambda i, block=block: (block, 0)))

    def kernel(*refs):
        for start, count, (out, row), rows in plans:
            total = functools.reduce(
                jnp.add, [ref[...].astype(F32) for ref in refs[start : start + count]]
            )
            out_ref = refs[len(operands) + out]
            out_ref[row : row + rows, :] = total.astype(out_ref.dtype)

    return pl.pallas_call(
        kernel,
        name="ring_add",
        grid=(1,),
        in_specs=specs,
        out_specs=[pl.BlockSpec(o.shape, lambda i: (0, 0)) for o in outs],
        out_shape=outs,
        compiler_params=pltpu.CompilerParams(vmem_limit_bytes=48 * MIB),
        cost_estimate=LIGHT,
    )(*operands)


def turned(parts, scale):
    rows, units = parts[0].shape

    def kernel(scale_ref, *refs):
        whole = jnp.concatenate([ref[...] for ref in refs[:-1]], axis=0) * scale_ref[0]
        refs[-1][...] = whole.T

    return pl.pallas_call(
        kernel,
        name="turned",
        grid=(1,),
        in_specs=[pl.BlockSpec(memory_space=pltpu.SMEM)]
        + [pl.BlockSpec(part.shape, lambda i: (0, 0)) for part in parts],
        out_specs=pl.BlockSpec((units, rows * len(parts)), lambda i: (0, 0)),
        out_shape=jax.ShapeDtypeStruct((units, rows * len(parts)), F32),
        compiler_params=pltpu.CompilerParams(vmem_limit_bytes=48 * MIB),
        cost_estimate=LIGHT,
    )(scale, *parts)


def interleaved(first, second, scale):
    rows, columns = first.shape
    step = min(32, rows)

    def kernel(scale_ref, first_ref, second_ref, out_ref):
        out_ref[:, 0, :] = first_ref[...] * scale_ref[0]
        out_ref[:, 1, :] = second_ref[...] * scale_ref[0]

    return pl.pallas_call(
        kernel,
        name="interleaved",
        grid=(rows // step,),
        in_specs=[pl.BlockSpec(memory_space=pltpu.SMEM)]
        + [pl.BlockSpec((step, columns), lambda i: (i, 0))] * 2,
        out_specs=pl.BlockSpec((step, 2, columns), lambda i: (i, 0, 0)),
        out_shape=jax.ShapeDtypeStruct((rows, 2, columns), F32),
        compiler_params=pltpu.CompilerParams(vmem_limit_bytes=48 * MIB),
        cost_estimate=LIGHT,
    )(scale, first, second)


def barrier(value, *others):
    return lax.optimization_barrier((value, *others))[0]


class Order:
    def __init__(self):
        self.last = None

    def __call__(self, step, operand, *others, wait=()):
        if self.last is not None:
            operand = barrier(operand, self.last, *wait)
        result = step(operand, *others)
        self.last = jax.tree.leaves(result)[0]
        return result


class Reducer:
    def __init__(self, order, rounds, partner, along):
        self.order, self.rounds, self.partner, self.along = order, rounds, partner, along
        self.flying, self.rings = [], []
        self.popped = None
        self.kept, self.done, self.late = {}, {}, []

    def send(self, name, sent, kept=None):
        if self.popped is not None:
            sent = barrier(sent, self.popped)
        if kept is not None:
            self.kept[name] = kept
        self.flying.append((name, self.partner(sent)))

    def ring(self, name, kept, other):
        self._enter(name, [kept], F32)
        self._enter(name + "/other", [other], BF)

    def _enter(self, name, arrays, final):
        shape = (arrays[0].shape[0] // self.rounds, arrays[0].shape[1])
        self.rings.append(
            dict(name=name, arrays=arrays, shape=shape, step=0, carry=[], final=final)
        )

    def turn(self, pop=True):
        if pop and self.flying:
            name, got = self.flying.pop(0)
            self.popped = got
            self._enter(name, [self.kept.pop(name), got], F32)
        rings, self.rings = self.rings, []
        groups, members = [], []
        for group in self._groups(rings):
            shape = group[0]["shape"]
            entries = []
            for ring in group:
                end = ring["step"] == self.rounds - 1
                pairs = [(array, ring["step"]) for array in ring["arrays"]] + ring["carry"]
                entries.append((pairs, ring["final"] if end else None))
            groups.append((shape, entries))
            members.append(group)
        if not groups:
            return

        def step(first):
            pairs = groups[0][1][0][0]
            pairs[0] = (first, pairs[0][1])
            return ring_add(groups)

        outs = list(self.order(step, groups[0][1][0][0][0][0]))
        for (shape, entries), group in zip(groups, members):
            message = None
            if any(final is None for _, final in entries):
                message = self.along(outs.pop(0))
            sent = 0
            for ring, (_, final) in zip(group, entries):
                if final is None:
                    ring["carry"] = [(message, sent)]
                    ring["step"] += 1
                    sent += 1
                    self.rings.append(ring)
                else:
                    self._finish(ring["name"], outs.pop(0))

    def _groups(self, rings):
        for shape in dict.fromkeys(ring["shape"] for ring in rings):
            members = [ring for ring in rings if ring["shape"] == shape]
            most = max(1, GROUP_BYTES // (2 * shape[0] * shape[1]))
            count = -(-len(members) // most)
            size = -(-len(members) // count)
            for start in range(0, len(members), size):
                yield members[start : start + size]

    def _finish(self, name, result):
        if name.endswith("/other"):
            self.late.append((name.split("/")[0], self.partner(result)))
        else:
            self.done[name] = result

    def close(self):
        late, self.late = self.late, []
        for name, got in late:
            self.done[name] = self.order(lambda a, n=name: self.done[n] + a.astype(F32), got)

    def busy(self):
        return bool(self.flying or self.rings)


def local(
    n_dp,
    tokens,
    segment_ids,
    cotangent,
    w_qkv,
    qkv_bias,
    w_out,
    w_gate_up,
    w_down,
    norm_gains,
    norm_biases,
):
    shard, width = tokens.shape
    group = segment_ids.shape[0]
    local_width = w_out.shape[0]
    units = w_down.shape[0]
    n_tensor = group // shard
    n_ring = n_dp // 2
    me = lax.axis_index("tensor")
    data_index = lax.axis_index("dp")
    to_core = [(t, t ^ 1) for t in range(n_tensor)]
    to_x = [(t, t ^ 2) for t in range(n_tensor)]
    to_y = [(d, d ^ 1) for d in range(n_dp)]
    up_z = [(d, (d + 2) % n_dp) for d in range(n_dp)]
    order = Order()

    def core(value):
        return lax.ppermute(value, "tensor", to_core)

    def across(value):
        return lax.ppermute(value, "tensor", to_x)

    def over_dp(value, step):
        return lax.ppermute(value, "dp", [(d, d ^ (1 << step)) for d in range(n_dp)])

    dp_steps = (n_dp - 1).bit_length()

    def in_pieces(values):
        blocks = values.reshape((n_tensor, shard) + values.shape[1:])
        return jnp.concatenate(
            [lax.dynamic_index_in_dim(blocks, me ^ k, 0, False) for k in range(n_tensor)], 0
        )

    def stack(*pieces):
        return jnp.concatenate(pieces, 0)

    def rows_of(half, rows, w, dims):
        return order(lambda r, *more: pair_product(half, (r, *more), w, dims), *rows)

    def hop(pair):
        return pair[0], [core(pair[1])]

    def send_far(pair):
        mine, tiles = hop(pair)
        return across(order(lambda t: add_tiles(mine, (t,)), *tiles))

    ring_index = data_index // 2
    rings = jnp.stack([(ring_index - 1 - s + 2 * n_ring) % n_ring for s in range(n_ring)])
    keep_blocks = (2 * rings + data_index % 2).astype(jnp.int32)
    send_blocks = (2 * rings + 1 - data_index % 2).astype(jnp.int32)

    depth = width // n_dp

    def grad_of(sets, pieces, *cots, splits=1):
        def step(first):
            arrays = [(first,) + cots[0][1:], *cots[1:]]
            return weight_grad(sets, pieces, arrays, splits, depth)

        return order(step, cots[0][0])

    reducer = Reducer(
        order,
        n_ring,
        lambda value: lax.ppermute(value, "dp", to_y),
        lambda value: lax.ppermute(value, "dp", up_z),
    )

    me_one = me[None].astype(jnp.int32)
    gains = [norm_gains[index : index + 1] for index in range(2)]
    shifts = [norm_biases[index : index + 1] for index in range(2)]
    live = (segment_ids >= 0).astype(F32)
    live_rows = lax.dynamic_slice_in_dim(live, me * shard, shard, 0)

    one_own = order(norm_rows, tokens, gains[0], shifts[0])
    one_far = across(one_own)
    one_near = core(one_own)
    out_cot = (cotangent.astype(F32) * live_rows[:, None]).astype(BF)
    in_near = core(out_cot)
    live_total = jnp.sum(live)[None]
    table = rope_tables(in_pieces(positions_of(segment_ids)))
    w_flat = w_gate_up.reshape(width, 2 * units)
    w_split = jnp.transpose(w_qkv, (1, 0, 2))
    bias_rows = qkv_bias[:, None, :]
    qkv = order(
        lambda a: project(0, a, one_near, w_split, bias_rows, table, None),
        one_own, wait=(w_flat, table),
    )
    one_far = barrier(one_far, qkv)
    one_last = core(one_far)
    in_far = across(barrier(out_cot, one_far))
    qkv = order(
        lambda a: project(1, a, one_last, w_split, bias_rows, table, qkv), one_far
    )
    attended, lse = order(lambda q: attend(me_one, segment_ids, q), qkv)
    attended = barrier(attended, in_far)
    branch_far = send_far(rows_of(1, (attended,), w_out, NN))
    near, tiles = hop(rows_of(0, (attended,), w_out, NN))
    in_far = barrier(in_far, attended)
    in_last = core(in_far)
    incoming = (out_cot, in_near, in_far, in_last)
    incoming_full = order(stack, *incoming)
    act_grad = order(
        lambda r: lax.dot_general(r, w_down, NT, preferred_element_type=F32), incoming_full
    )
    live_total = order(jnp.add, over_dp(live_total, 0), live_total)
    hidden, two_own = order(
        lambda t: add_norm_rows(t, near, branch_far, tiles, gains[1], shifts[1]), tokens
    )
    two_far = across(two_own)
    two_near = core(two_own)
    fed = order(lambda a: feed(0, a, two_near, w_flat, act_grad, None), two_own)
    for step in range(1, dp_steps):
        live_total = order(jnp.add, over_dp(live_total, step), live_total)
    live_total = live_total[0]
    two_far = barrier(two_far, order.last)
    two_last = core(two_far)
    activated, gate_cot, up_cot = order(
        lambda a: feed(1, a, two_last, w_flat, act_grad, fed), two_far
    )
    two = (two_own, two_near, two_far, two_last)
    one = (one_own, one_near, one_far, one_last)

    down_sent = grad_of([send_blocks], incoming, (activated, 0, units), splits=2)
    reducer.send("down1", down_sent[1])
    (gate_sent,) = grad_of([send_blocks], two, (gate_cot, 0, units))
    down_kept = grad_of([keep_blocks], incoming, (activated, 0, units), splits=2)
    reducer.kept["down1"] = down_kept[1]
    reducer.ring("down0", down_kept[0], down_sent[0])
    second_far_pair = rows_of(1, (gate_cot, up_cot), w_flat, NT)
    reducer.turn(pop=False)
    second_near_pair = rows_of(0, (gate_cot, up_cot), w_flat, NT)

    reducer.send("gate", gate_sent)
    reducer.turn()
    second_far = send_far(second_far_pair)
    second_near, second_tiles = hop(second_near_pair)
    (reducer.kept["gate"],) = grad_of([keep_blocks], two, (gate_cot, 0, units))
    up_grads = grad_of([send_blocks, keep_blocks], two, (up_cot, 0, units))
    reducer.send("up", *up_grads)
    reducer.turn(pop=False)
    hidden_grad, branch_own, sums_two = order(
        lambda h: norm_rows_back(
            h, second_near, second_far, second_tiles, out_cot, gains[1], (F32, BF)
        ),
        hidden,
    )
    branch_far = across(branch_own)
    branch_near = core(branch_own)
    down_pair = rows_of(1, (activated,), w_down, NN)
    down_near_pair = rows_of(0, (activated,), w_down, NN)

    reducer.turn()
    branch_last = core(barrier(branch_far, order.last))
    branch = (branch_own, branch_near, branch_far, branch_last)
    branch_full = order(stack, *branch)
    attended_grad = order(
        lambda r: lax.dot_general(r, w_out, NT, preferred_element_type=F32).astype(BF),
        branch_full,
    )
    raw_cot = order(
        lambda g: attend_back(me_one, segment_ids, qkv, attended, g, lse, table), attended_grad
    )
    reducer.turn(pop=False)
    query_key_grads = grad_of([send_blocks, keep_blocks], one, (raw_cot, 0, 2 * local_width))
    reducer.send("query_key", *query_key_grads)

    reducer.turn()
    out_grads = grad_of([send_blocks, keep_blocks], branch, (attended, 0, local_width))
    reducer.send("out", *out_grads)
    value_grads = grad_of([send_blocks, keep_blocks], one, (raw_cot, 2, local_width))
    first_far_pair = rows_of(1, (raw_cot,), w_split, NT)
    first_near_pair = rows_of(0, (raw_cot,), w_split, NT)
    bias_sum = order(lambda r: jnp.sum(r.astype(F32), axis=0).reshape(3, local_width), raw_cot)

    reducer.turn(pop=False)
    reducer.turn()
    reducer.send("value", *value_grads)
    first_far = send_far(first_far_pair)
    first_near, first_tiles = hop(first_near_pair)

    reducer.turn()
    input_grad, sums_one = order(
        lambda t: norm_rows_back(
            t, first_near, first_far, first_tiles, hidden_grad, gains[0], (F32,)
        ),
        tokens,
    )
    down_far = send_far(down_pair)
    down_near, down_tiles = hop(down_near_pair)
    rows_sum = jnp.concatenate([sums_one[:1], sums_two[:1], sums_one[1:], sums_two[1:]], 0)
    rows_near = core(rows_sum)

    reducer.turn()
    reducer.close()
    rows_sum = order(jnp.add, rows_near, rows_sum)
    rows_far = across(rows_sum)
    rows_sum = order(jnp.add, rows_far, rows_sum)
    small = jnp.concatenate([rows_sum.reshape(-1), bias_sum.reshape(-1)])
    scaled = {}
    scale = (1.0 / live_total)[None]

    def finish():
        done = reducer.done
        for name, parts in (("down", ("down0", "down1")), ("out", ("out",))):
            if name not in scaled and all(part in done for part in parts):
                scaled[name] = order(
                    lambda first, rest=parts[1:]: turned([first, *[done[r] for r in rest]], scale),
                    done[parts[0]],
                )
        if "gate_up" not in scaled and "gate" in done and "up" in done:
            scaled["gate_up"] = order(
                lambda g: interleaved(g, done["up"], scale), done["gate"]
            )
        for name in ("query_key", "value"):
            if name not in scaled and name in done:
                scaled[name] = done[name] * scale

    for step in range(dp_steps):
        small_far = over_dp(small, step)
        reducer.turn()
        small = order(jnp.add, small_far, small)
        finish()
        if step == 1:
            output = order(lambda h: add_rows(h, down_near, down_far, down_tiles), hidden)
    small = small * scale
    rows_sum = small[: 4 * width].reshape(4, width)
    bias_sum = small[4 * width :].reshape(3, local_width)
    while reducer.busy():
        reducer.turn()
        finish()
    return (
        output,
        input_grad,
        jnp.concatenate([scaled["query_key"], scaled["value"]], 1).reshape(-1, 3, local_width),
        bias_sum,
        scaled["out"],
        scaled["gate_up"],
        scaled["down"],
        rows_sum[:2],
        rows_sum[2:],
    )


def solution(mesh):
    in_specs = (
        P(("dp", "tensor"), None),
        P("dp"),
        P(("dp", "tensor"), None),
        P(None, None, "tensor"),
        P(None, "tensor"),
        P("tensor", None),
        P(None, None, "tensor"),
        P("tensor", None),
        P(),
        P(),
    )
    out_specs = (
        P(("dp", "tensor"), None),
        P(("dp", "tensor"), None),
        P("dp", None, "tensor"),
        P(None, "tensor"),
        P("tensor", "dp"),
        P("dp", None, "tensor"),
        P("tensor", "dp"),
        P(),
        P(),
    )
    return jax.shard_map(
        functools.partial(local, mesh.shape["dp"]),
        mesh=mesh,
        in_specs=in_specs,
        out_specs=out_specs,
        check_vma=False,
    )
```
